32 devices in a mesh: groups: 2 (over x), row: 8 (over z, y), col: 2 (over core).
Axes of the slice: x: 2, y: 2, z: 4, core: 2. Of those that a mesh axis runs over, the one named last changes fastest.
Arguments:
- a_vals: bfloat16 [64, 20, 64, 64], P(('groups', 'row'), 'col'), parts along dimension 0, may hold values from -0.75 to 0.75
- b_vals: bfloat16 [64, 20, 64, 64], P(('groups', 'row'), 'col'), parts along dimension 0, may hold values from -2 to 2
- cols: int32 [64, 20], P(('groups', 'row'), 'col'), parts along dimension 0, may hold values from 0 to 31, as said below
Outputs:
- c_vals: bfloat16 [64, 20, 64, 64], P(('groups', 'row'), 'col'), parts along dimension 0
The draws below stay inside these ranges and needn't reach their ends.
There are 2 independent parts, one for each index of `groups`. The reference program is written for one: setup_inputs(seed, part) draws one part's arguments, and reference() takes and returns one part's arrays. A program takes and returns all parts, laid end to end along the dimension named above; each array names one. Nothing has to cross between parts.
Inputs may be any that keep to these rules, and one draw needn't show every extreme that they name: `cols`: within a block row all 20 columns differ; slots 0 to 9 hold columns below 16, the other slots columns from 16 on. For each group of 4 consecutive block rows (starting at a multiple of 4) and each half, exactly one group of 4 consecutive block columns (starting at a multiple of 4) in that half is named by every row of the group in every one of its columns, so that 4 * 4 slots of the group fall into it; no group of 4 block columns can receive more.
All inputs are finite; a program needn't handle non-finite values.
Results may differ from the reference program's by a relative error of at most 0.001.
Values may be sent and summed in bfloat16 or wider, within the bound.
No kernel may reach another device: no remote copies, remote signals or barrier semaphores. Data moves between devices by JAX's collectives and lax.ppermute only.
A program may use at most 128 MiB of HBM per device.

```python
import jax
import jax.numpy as jnp
from jax import lax

BS = 64
RB = 4
K = 20
NB = 32


def draw_cols(key, part):
    key = jax.random.fold_in(key, 11)
    first, second = jax.random.split(key)
    half_split = NB // 2
    panels = half_split // RB
    hot = jax.random.randint(first, (NB // RB, 2), 0, panels)
    random_jitter = jax.random.randint(second, (NB, 2, half_split), 0, 16384)
    column_block = jnp.arange(half_split, dtype=jnp.int32)
    block_panel = column_block // RB
    dense_rows = hot[jnp.arange(NB, dtype=jnp.int32) // RB]
    extra_weight = jnp.where(block_panel[None, None, :] == dense_rows[:, :, None], 1 << 24, 0)
    ranking_score = extra_weight + random_jitter * half_split + column_block[None, None, :]
    _, chosen = lax.top_k(ranking_score, K // 2)
    chosen = chosen.astype(jnp.int32) + (jnp.arange(2, dtype=jnp.int32) * half_split)[None, :, None]
    return chosen.reshape(NB, K)


def shard_levels(rng, extent, cuts, least, high):
    gain, own = 1.0, jax.random.fold_in(rng, 6)
    for dim, parts in cuts:
        draws = jnp.exp(jax.random.uniform(jax.random.fold_in(own, dim), (parts,), jnp.float32, least / len(cuts), high / len(cuts)))
        gain = gain * jnp.repeat(draws, extent[dim] // parts).reshape([-1 if axis == dim else 1 for axis in range(len(extent))])
    return gain


def gaussian(stream_key, extent, spread, reach, shards=(), kind=jnp.bfloat16):
    drawn = spread * jax.random.normal(stream_key, extent, jnp.float32)
    if shards:
        drawn = drawn * shard_levels(stream_key, extent, shards, -0.22, 0.18)
    return jnp.clip(drawn, -reach, reach).astype(kind)


def setup_inputs(seed: int = 0, part: int = 0) -> dict:
    splits = jax.random.split(jax.random.key(seed), 4)
    part_keys = jax.random.split(jax.random.fold_in(splits[3], part), 4)
    a_vals = gaussian(part_keys[0], (NB, K, BS, BS), BS ** -0.5, 0.75, ((0, 8), (1, 2)))
    b_vals = gaussian(part_keys[1], (NB, K, BS, BS), 0.3, 2.0, ((0, 8), (1, 2)))
    cols = draw_cols(jax.random.fold_in(jax.random.fold_in(splits[3], part), 71), part)
    return {"a_vals": a_vals, "b_vals": b_vals, "cols": cols}


def reference(a_vals, b_vals, cols):
    def one_row(args):
        a_row, c_row = args
        inner = b_vals[c_row].astype(jnp.float32)
        inner_cols = cols[c_row]
        prod = jnp.einsum('mab,mnbc->mnac', a_row.astype(jnp.float32), inner)
        match = (inner_cols[:, :, None] == c_row[None, None, :]).astype(jnp.float32)
        return jnp.einsum('mnk,mnac->kac', match, prod)

    out = lax.map(one_row, (a_vals, cols))
    return out.astype(jnp.bfloat16)
```

```python
import functools

import jax
import jax.numpy as jnp
from jax import lax
from jax.experimental import pallas as pl
from jax.experimental.pallas import tpu as pltpu
from jax.sharding import PartitionSpec as P

VMEM = pltpu.VMEM
LIMIT = 48 * 1024 * 1024


def pack_kernel(b_ref, o_ref):
    pairs, slots = o_ref.shape[:2]
    for p in range(pairs):
        for n in range(slots):
            o_ref[p, n] = jnp.concatenate([b_ref[2 * p, n], b_ref[2 * p + 1, n]], axis=-1)


def pack(b_vals):
    rows, slots, bs, _ = b_vals.shape
    return pl.pallas_call(
        pack_kernel,
        out_shape=jax.ShapeDtypeStruct((rows // 2, slots, bs, 2 * bs), b_vals.dtype),
        in_specs=[pl.BlockSpec(memory_space=VMEM)],
        out_specs=pl.BlockSpec(memory_space=VMEM),
        compiler_params=pltpu.CompilerParams(vmem_limit_bytes=LIMIT),
    )(b_vals)


def dense_kernel(where_ref, own_ref, other_ref, o_ref, blocks):
    rows, slots = own_ref.shape[:2]
    blocks[:, :slots] = own_ref[...]
    blocks[:, slots : 2 * slots] = other_ref[...]
    blocks[:, 2 * slots] = jnp.zeros_like(blocks[:, 2 * slots])
    bs = own_ref.shape[-1]
    for i in range(rows):
        def body(q, carry):
            left = blocks[i, where_ref[i, 2 * q]]
            right = blocks[i, where_ref[i, 2 * q + 1]]
            o_ref[q, i * bs : (i + 1) * bs, :] = jnp.concatenate([left, right], axis=-1)
            return carry

        lax.fori_loop(0, o_ref.shape[0], body, 0)


def dense_rows(where, own, other):
    rows, slots, bs, _ = own.shape
    return pl.pallas_call(
        dense_kernel,
        out_shape=jax.ShapeDtypeStruct((where.shape[1] // 2, rows * bs, 2 * bs), own.dtype),
        grid_spec=pltpu.PrefetchScalarGridSpec(
            num_scalar_prefetch=1,
            grid=(),
            in_specs=[pl.BlockSpec(memory_space=VMEM)] * 2,
            out_specs=pl.BlockSpec(memory_space=VMEM),
            scratch_shapes=[VMEM((rows, 2 * slots + 1, bs, bs), own.dtype)],
        ),
        compiler_params=pltpu.CompilerParams(vmem_limit_bytes=LIMIT),
    )(where, own, other)


def product_kernel(where_ref, place_ref, a_ref, g_ref, o_ref, blocks, total, sems):
    sources, pairs, slots, bs, _ = g_ref.shape
    groups = total.shape[0]
    copies = [
        pltpu.make_async_copy(g_ref.at[s], blocks.at[s, :, pl.ds(0, slots)], sems.at[s])
        for s in range(sources)
    ]
    for copy in copies:
        copy.start()
    blocks[:, :, slots] = jnp.zeros_like(blocks[:, :, slots])
    low = lax.broadcasted_iota(jnp.int32, (bs, 2 * bs), 1) < bs

    def turn(x):
        return jnp.concatenate([x[:, bs:], x[:, :bs]], axis=-1)

    for s, copy in enumerate(copies):
        copy.wait()
        a = jnp.concatenate([a_ref[s * pairs + p] for p in range(pairs)], axis=-1)
        for g in range(groups):
            panel = []
            for p in range(pairs):
                for h in range(2):
                    j = (s * pairs + p) * 2 + h
                    tiles = []
                    for q in (2 * g, 2 * g + 1):
                        left = blocks[s, p, where_ref[j, 2 * q]]
                        right = blocks[s, p, where_ref[j, 2 * q + 1]]
                        if h == 0:
                            right = turn(right)
                        else:
                            left = turn(left)
                        tiles.append(jnp.where(low, left, right))
                    panel.append(jnp.concatenate(tiles, axis=-1))
            part = jnp.dot(a, jnp.concatenate(panel, axis=0), preferred_element_type=jnp.float32)
            for t in range(2):
                piece = part[:, t * 2 * bs : (t + 1) * 2 * bs]
                if s == 0:
                    total[g, t] = piece
                else:
                    total[g, t] += piece
    for i in range(o_ref.shape[0]):
        for k in range(slots):
            l = place_ref[i, k]
            tile = total[l // 4, (l // 2) % 2, i * bs : (i + 1) * bs, :]
            tile = jnp.where(l % 2 == 0, tile, pltpu.roll(tile, bs, 1))
            o_ref[i, k] = tile[:, :bs].astype(o_ref.dtype)


def product(where, place, a, gathered):
    sources, pairs, slots, bs, _ = gathered.shape
    rows = a.shape[1] // bs
    groups = where.shape[1] // 4
    return pl.pallas_call(
        product_kernel,
        out_shape=jax.ShapeDtypeStruct((rows, slots, bs, bs), gathered.dtype),
        grid_spec=pltpu.PrefetchScalarGridSpec(
            num_scalar_prefetch=2,
            grid=(),
            in_specs=[pl.BlockSpec(memory_space=VMEM), pl.BlockSpec(memory_space=pl.ANY)],
            out_specs=pl.BlockSpec(memory_space=VMEM),
            scratch_shapes=[
                VMEM((sources, pairs, slots + 1, bs, 2 * bs), gathered.dtype),
                VMEM((groups, 2, rows * bs, 2 * bs), jnp.float32),
                pltpu.SemaphoreType.DMA((sources,)),
            ],
        ),
        compiler_params=pltpu.CompilerParams(vmem_limit_bytes=LIMIT),
    )(where, place, a, gathered)


def slot_of(cols, first, count):
    slots = cols.shape[1]
    hit = cols[:, :, None] == first + jnp.arange(count, dtype=jnp.int32)[None, None, :]
    slot = jnp.arange(slots, dtype=jnp.int32)[None, :, None]
    return slots - jnp.sum(jnp.where(hit, slots - slot, 0), axis=1)


def local(sources, a_vals, b_vals, cols):
    rows, slots, bs, _ = a_vals.shape
    half = sources * rows // 2
    me = lax.axis_index("col")
    gathered = lax.all_gather(pack(b_vals), "row", axis=0)
    all_cols = lax.all_gather(cols, ("row", "col"), axis=0).reshape(sources, 2, rows, slots)
    swap = [(0, 1), (1, 0)]
    a_other = lax.ppermute(a_vals, "col", swap)
    my_half = lax.dynamic_index_in_dim(all_cols, me, 1, keepdims=False).reshape(sources * rows, slots)
    chip = lax.dynamic_index_in_dim(all_cols, lax.axis_index("row"), 0, keepdims=False)
    other = lax.dynamic_index_in_dim(chip, 1 - me, 0, keepdims=False)
    a_where = slot_of(jnp.concatenate([cols, other], axis=1), 0, 2 * half)
    a = dense_rows(a_where, a_vals, a_other)
    b_where = slot_of(my_half, me * half, half)
    return product(b_where, cols - me * half, a, gathered)


def solution(mesh):
    return jax.shard_map(
        functools.partial(local, mesh.shape["row"]),
        mesh=mesh,
        in_specs=(
            P(("groups", "row"), "col", None, None),
            P(("groups", "row"), "col", None, None),
            P(("groups", "row"), "col"),
        ),
        out_specs=P(("groups", "row"), "col", None, None),
        check_vma=False,
    )
```

```python
import functools

import jax
import jax.numpy as jnp
import numpy as np
from jax import lax
from jax.experimental import pallas as pl
from jax.experimental.pallas import tpu as pltpu
from jax.sharding import PartitionSpec as P

VMEM = pltpu.VMEM
SMEM = pltpu.SMEM
LIMIT = 48 * 1024 * 1024
FOOT = 16


def params():
    return pltpu.CompilerParams(vmem_limit_bytes=LIMIT)


def cost(flops, size):
    return pl.CostEstimate(flops=flops, bytes_accessed=size, transcendentals=0)


def pack_kernel(half, cols_ref, b_ref, *o_refs):
    _, slots, bs, _ = b_ref.shape
    row = lax.broadcasted_iota(jnp.int32, (FOOT, 2 * bs), 0)
    lane = lax.broadcasted_iota(jnp.int32, (FOOT, 2 * bs), 1)
    for p, o_ref in enumerate(o_refs):
        for n in range(slots):
            o_ref[n * bs : (n + 1) * bs, :] = jnp.concatenate([b_ref[2 * p, n], b_ref[2 * p + 1, n]], axis=-1)
        foot = jnp.full((FOOT, 2 * bs), slots, jnp.int32)
        for h in range(2):
            for n in range(slots):
                here = (row == h) & (lane == lax.rem(cols_ref[2 * p + h, n], half))
                foot = jnp.where(here, n, foot)
        o_ref[slots * bs :, :] = foot.astype(jnp.float32).astype(o_ref.dtype)


def pack(half, cols, b_vals):
    rows, slots, bs, _ = b_vals.shape
    shape = jax.ShapeDtypeStruct((slots * bs + FOOT, 2 * bs), b_vals.dtype)
    return pl.pallas_call(
        functools.partial(pack_kernel, half),
        out_shape=[shape] * (rows // 2),
        grid_spec=pltpu.PrefetchScalarGridSpec(
            num_scalar_prefetch=1,
            grid=(),
            in_specs=[pl.BlockSpec(memory_space=VMEM)],
            out_specs=[pl.BlockSpec(memory_space=VMEM)] * (rows // 2),
        ),
        compiler_params=params(),
        cost_estimate=cost(0, 2 * b_vals.size * 2),
    )(cols, b_vals)


def dense_kernel(cols_ref, others_ref, own_ref, other_ref, o_ref, blocks, where):
    rows, slots, bs, _ = own_ref.shape
    count = o_ref.shape[0]
    blocks[:, :slots] = own_ref[...]
    blocks[:, slots : 2 * slots] = other_ref[...]
    blocks[:, 2 * slots] = jnp.zeros_like(blocks[:, 2 * slots])
    for i in range(rows):
        def clear(j, carry):
            where[i, j] = 2 * slots
            return carry

        lax.fori_loop(0, 2 * count, clear, 0, unroll=8)
        for m in range(slots):
            where[i, cols_ref[i, m]] = m
            where[i, others_ref[i, m]] = slots + m

    def body(q, carry):
        for i in range(rows):
            left = blocks[i, where[i, 2 * q]]
            right = blocks[i, where[i, 2 * q + 1]]
            o_ref[q, i * bs : (i + 1) * bs, :] = jnp.concatenate([left, right], axis=-1)
        return carry

    lax.fori_loop(0, count, body, 0, unroll=4)


def dense_rows(count, cols, others, own, other):
    rows, slots, bs, _ = own.shape
    return pl.pallas_call(
        dense_kernel,
        out_shape=jax.ShapeDtypeStruct((count // 2, rows * bs, 2 * bs), own.dtype),
        grid_spec=pltpu.PrefetchScalarGridSpec(
            num_scalar_prefetch=2,
            grid=(),
            in_specs=[pl.BlockSpec(memory_space=VMEM)] * 2,
            out_specs=pl.BlockSpec(memory_space=VMEM),
            scratch_shapes=[VMEM((rows, 2 * slots + 1, bs, bs), own.dtype), SMEM((rows, count), jnp.int32)],
        ),
        compiler_params=params(),
        cost_estimate=cost(0, 4 * own.size * 2),
    )(cols, others, own, other)


def add_products(done, ids_ref, a_ref, parts, total, first, feet, where, sem):
    groups, bs = total.shape[0], total.shape[3] // 2
    slots = (parts[0][0].shape[0] - FOOT) // bs
    pairs = len(parts[0])
    for s, source in enumerate(parts):
        for p, part in enumerate(source):
            feet[s * pairs + p] = part[slots * bs :, :].astype(jnp.float32).astype(jnp.int32)
    copy = pltpu.make_async_copy(feet, where, sem)
    copy.start()
    copy.wait()
    low = lax.broadcasted_iota(jnp.int32, (bs, 2 * bs), 1) < bs

    def block(part, slot):
        at = pl.multiple_of(jnp.minimum(slot, slots - 1) * bs, bs)
        return jnp.where(slot < slots, part[pl.ds(at, bs), :], jnp.zeros((bs, 2 * bs), part.dtype))

    def turn(x):
        return jnp.concatenate([x[:, bs:], x[:, :bs]], axis=-1)

    for s, source in enumerate(parts):
        a = jnp.concatenate([a_ref[ids_ref[done + s] * pairs + p] for p in range(pairs)], axis=-1)

        def body(g, carry, s=s, source=source, a=a):
            panel = []
            for p, part in enumerate(source):
                for h in range(2):
                    tiles = []
                    for q in (2 * g, 2 * g + 1):
                        left = block(part, where[s * pairs + p, h, 2 * q])
                        right = block(part, where[s * pairs + p, h, 2 * q + 1])
                        if h == 0:
                            right = turn(right)
                        else:
                            left = turn(left)
                        tiles.append(jnp.where(low, left, right))
                    panel.append(jnp.concatenate(tiles, axis=-1))
            sums = jnp.dot(a, jnp.concatenate(panel, axis=0), preferred_element_type=jnp.float32)
            for t in range(2):
                piece = sums[:, t * 2 * bs : (t + 1) * 2 * bs]
                if s == 0 and first:
                    total[g, t] = piece
                else:
                    total[g, t] += piece
            return carry

        lax.fori_loop(0, groups, body, 0, unroll=min(groups, 4))


def first_kernel(done, pairs, ids_ref, a_ref, *refs):
    *parts, total, feet, where, sem = refs
    parts = [parts[k : k + pairs] for k in range(0, len(parts), pairs)]
    add_products(done, ids_ref, a_ref, parts, total, True, feet, where, sem)


def middle_kernel(done, pairs, ids_ref, a_ref, before, *refs):
    *parts, total, feet, where, sem = refs
    parts = [parts[k : k + pairs] for k in range(0, len(parts), pairs)]
    add_products(done, ids_ref, a_ref, parts, total, False, feet, where, sem)


def last_kernel(done, pairs, ids_ref, place_ref, a_ref, total, *refs):
    *parts, o_ref, feet, where, sem = refs
    parts = [parts[k : k + pairs] for k in range(0, len(parts), pairs)]
    add_products(done, ids_ref, a_ref, parts, total, False, feet, where, sem)
    rows, slots, bs, _ = o_ref.shape
    half = total.shape[0] * 4
    for i in range(rows):
        for k in range(slots):
            l = lax.rem(place_ref[i, k], half)
            tile = total[l // 4, (l // 2) % 2, i * bs : (i + 1) * bs, :]
            tile = jnp.where(l % 2 == 0, tile, pltpu.roll(tile, bs, 1))
            o_ref[i, k] = tile[:, :bs].astype(o_ref.dtype)


def product(kernel, done, ids, a, total, parts, out, place=None):
    pairs = len(parts[0])
    flat = [part for source in parts for part in source]
    scalars = [ids] if place is None else [ids, place]
    arrays = [a] if total is None else [a, total]
    aliases = {} if total is None or place is not None else {len(scalars) + 1: 0}
    lanes = flat[0].shape[1]
    return pl.pallas_call(
        functools.partial(kernel, done, pairs),
        out_shape=out,
        grid_spec=pltpu.PrefetchScalarGridSpec(
            num_scalar_prefetch=len(scalars),
            grid=(),
            in_specs=[pl.BlockSpec(memory_space=VMEM)] * (len(arrays) + len(flat)),
            out_specs=pl.BlockSpec(memory_space=VMEM),
            scratch_shapes=[
                VMEM((len(flat), FOOT, lanes), jnp.int32),
                SMEM((len(flat), FOOT, lanes), jnp.int32),
                pltpu.SemaphoreType.DMA,
            ],
        ),
        input_output_aliases=aliases,
        compiler_params=params(),
        cost_estimate=cost(2 * a.shape[1] * 256 * 1024 * len(parts), 2 * len(flat) * flat[0].size),
    )(*scalars, *arrays, *flat)


def local(order, a_vals, b_vals, cols):
    sources = len(order)
    rows, slots, bs, _ = a_vals.shape
    half = sources * rows // 2
    pairs = rows // 2
    spots = {r: k for k, r in enumerate(order)}
    hops = {1: sources // 2, -1: (sources - 1) // 2}
    trips = [(way, step) for step in range(1, hops[1] + 1) for way in (1, -1) if step <= hops[way]]
    def ring(way):
        return [
            (order[r] * 2 + c, order[(r + (way if c == 0 else -way)) % sources] * 2 + c)
            for r in range(sources)
            for c in range(2)
        ]

    names = np.asarray(
        [
            [[r] + [order[(spots[r] - (w if c == 0 else -w) * t) % sources] for w, t in trips] for c in range(2)]
            for r in range(sources)
        ],
        np.int32,
    )
    ids = jnp.asarray(names)[lax.axis_index("row"), lax.axis_index("col")]

    own = pack(half, cols, b_vals)
    swap = [(0, 1), (1, 0)]
    others = lax.ppermute(cols, "col", swap)
    a_other = lax.ppermute(a_vals, "col", swap)
    rounds = [[own]]
    held = {1: list(own), -1: list(own)}
    for step in range(1, hops[1] + 1):
        ways = [way for way in (1, -1) if step <= hops[way]]
        for p in range(pairs):
            for way in ways:
                held[way][p] = lax.ppermute(held[way][p], ("row", "col"), ring(way))
        rounds.append([list(held[way]) for way in ways])
    a = dense_rows(2 * half, cols, others, a_vals, a_other)
    total_shape = jax.ShapeDtypeStruct((half // 4, 2, rows * bs, 2 * bs), jnp.float32)
    total, done = None, 0
    for step, parts in enumerate(rounds):
        if step == 0:
            total = product(first_kernel, done, ids, a, None, parts, total_shape)
        elif step < len(rounds) - 1:
            total = product(middle_kernel, done, ids, a, total, parts, total_shape)
        else:
            out = jax.ShapeDtypeStruct(a_vals.shape, a_vals.dtype)
            return product(last_kernel, done, ids, a, total, parts, out, cols)
        done += len(parts)


def ring_order(mesh):
    count = mesh.shape["row"]
    coords = [getattr(d, "coords", None) for d in mesh.devices[0, :, 0]]
    loop = [*range(0, count, 2), *range(count - 1 - count % 2, 0, -2)]
    if None not in coords:
        steps = [
            sum(abs(x - y) for x, y in zip(coords[loop[k - 1]], coords[loop[k]]))
            for k in range(count)
        ]
        if max(steps) <= 1:
            return loop
    return list(range(count))


def solution(mesh):
    return jax.shard_map(
        functools.partial(local, ring_order(mesh)),
        mesh=mesh,
        in_specs=(
            P(("groups", "row"), "col", None, None),
            P(("groups", "row"), "col", None, None),
            P(("groups", "row"), "col"),
        ),
        out_specs=P(("groups", "row"), "col", None, None),
        check_vma=False,
    )
```

```python
import functools
import math

import jax
import jax.numpy as jnp
import numpy as np
from jax import lax
from jax.experimental import pallas as pl
from jax.experimental.pallas import tpu as pltpu
from jax.sharding import PartitionSpec as P

VMEM = pltpu.VMEM
SMEM = pltpu.SMEM
LIMIT = 48 * 1024 * 1024
WHOLE = 63 * 1024 * 1024
BUSY = 50
FOOT = 16


def params(limit=LIMIT):
    return pltpu.CompilerParams(vmem_limit_bytes=limit)


def cost(flops, size):
    return pl.CostEstimate(flops=flops, bytes_accessed=size, transcendentals=0)


def pack_kernel(half, cols_hbm, b_hbm, *refs):
    *o_refs, cols_ref, b_ref, sem, sems = refs
    rows, slots, bs, _ = b_ref.shape
    copies = [pltpu.make_async_copy(b_hbm.at[r], b_ref.at[r], sems.at[r]) for r in range(rows)]
    fetch = pltpu.make_async_copy(cols_hbm, cols_ref, sem)
    fetch.start()
    for copy in copies:
        copy.start()
    row = lax.broadcasted_iota(jnp.int32, (FOOT, 2 * bs), 0)
    lane = lax.broadcasted_iota(jnp.int32, (FOOT, 2 * bs), 1)
    fetch.wait()
    for p, o_ref in enumerate(o_refs):
        foot = jnp.full((FOOT, 2 * bs), slots, jnp.int32)
        for h in range(2):
            for n in range(slots):
                here = (row == h) & (lane == lax.rem(cols_ref[2 * p + h, n], half))
                foot = jnp.where(here, n, foot)
        o_ref[slots * bs :, :] = foot.astype(jnp.float32).astype(o_ref.dtype)
        copies[2 * p].wait()
        copies[2 * p + 1].wait()
        for n in range(slots):
            o_ref[n * bs : (n + 1) * bs, :] = jnp.concatenate([b_ref[2 * p, n], b_ref[2 * p + 1, n]], axis=-1)


def pack(half, cols, b_vals):
    rows, slots, bs, _ = b_vals.shape
    shape = jax.ShapeDtypeStruct((slots * bs + FOOT, 2 * bs), b_vals.dtype)
    return pl.pallas_call(
        functools.partial(pack_kernel, half),
        out_shape=[shape] * (rows // 2),
        in_specs=[pl.BlockSpec(memory_space=pl.ANY)] * 2,
        out_specs=[pl.BlockSpec(memory_space=VMEM)] * (rows // 2),
        scratch_shapes=[
            SMEM(cols.shape, cols.dtype),
            VMEM(b_vals.shape, b_vals.dtype),
            pltpu.SemaphoreType.DMA,
            pltpu.SemaphoreType.DMA((rows,)),
        ],
        compiler_params=params(WHOLE),
        cost_estimate=cost(0, 2 * b_vals.size * 2),
    )(cols, b_vals)


def dense_kernel(ids_ref, cols_ref, others_ref, own_ref, other_ref, o_ref, blocks, where):
    rows, slots, bs, _ = own_ref.shape
    sources, pairs = o_ref.shape[:2]
    blocks[:, :slots] = own_ref[...]
    blocks[:, slots : 2 * slots] = other_ref[...]
    blocks[:, 2 * slots] = jnp.zeros_like(blocks[:, 2 * slots])
    for i in range(rows):
        def clear(j, carry):
            where[i, j] = 2 * slots
            return carry

        lax.fori_loop(0, 2 * sources * pairs, clear, 0, unroll=8)
        for m in range(slots):
            where[i, cols_ref[i, m]] = m
            where[i, others_ref[i, m]] = slots + m

    def body(s, carry):
        for p in range(pairs):
            j = (ids_ref[s] * pairs + p) * 2
            for i in range(rows):
                left = blocks[i, where[i, j]]
                right = blocks[i, where[i, j + 1]]
                o_ref[s, p, i * bs : (i + 1) * bs, :] = jnp.concatenate([left, right], axis=-1)
        return carry

    lax.fori_loop(0, sources, body, 0, unroll=2)


def dense_rows(ids, cols, others, own, other):
    rows, slots, bs, _ = own.shape
    sources = ids.shape[0]
    return pl.pallas_call(
        dense_kernel,
        out_shape=jax.ShapeDtypeStruct((sources, rows // 2, rows * bs, 2 * bs), own.dtype),
        grid_spec=pltpu.PrefetchScalarGridSpec(
            num_scalar_prefetch=3,
            grid=(),
            in_specs=[pl.BlockSpec(memory_space=VMEM)] * 2,
            out_specs=pl.BlockSpec(memory_space=VMEM),
            scratch_shapes=[
                VMEM((rows, 2 * slots + 1, bs, bs), own.dtype),
                SMEM((rows, sources * rows), jnp.int32),
            ],
        ),
        compiler_params=params(),
        cost_estimate=cost(0, BUSY * 8 * own.size),
    )(ids, cols, others, own, other)


def fetch_feet(parts, feet, where, sem):
    for k, part in enumerate(parts):
        feet[k] = part[part.shape[0] - FOOT :, :].astype(jnp.float32).astype(jnp.int32)
    copy = pltpu.make_async_copy(feet, where, sem)
    copy.start()
    return copy


def add_products(done, a_ref, parts, total, first, where):
    groups, bs = total.shape[0], total.shape[3] // 2
    slots = (parts[0].shape[0] - FOOT) // bs
    pairs = a_ref.shape[1]
    low = lax.broadcasted_iota(jnp.int32, (bs, 2 * bs), 1) < bs

    def block(part, slot):
        at = pl.multiple_of(jnp.minimum(slot, slots - 1) * bs, bs)
        return jnp.where(slot < slots, part[pl.ds(at, bs), :], jnp.zeros((bs, 2 * bs), part.dtype))

    def turn(x):
        return jnp.concatenate([x[:, bs:], x[:, :bs]], axis=-1)

    for s in range(len(parts) // pairs):
        source = parts[s * pairs : (s + 1) * pairs]
        a = jnp.concatenate([a_ref[done + s, p] for p in range(pairs)], axis=-1)

        def body(g, carry, s=s, source=source, a=a):
            panel = []
            for p, part in enumerate(source):
                for h in range(2):
                    tiles = []
                    for q in (2 * g, 2 * g + 1):
                        left = block(part, where[s * pairs + p, h, 2 * q])
                        right = block(part, where[s * pairs + p, h, 2 * q + 1])
                        if h == 0:
                            right = turn(right)
                        else:
                            left = turn(left)
                        tiles.append(jnp.where(low, left, right))
                    panel.append(jnp.concatenate(tiles, axis=-1))
            sums = jnp.dot(a, jnp.concatenate(panel, axis=0), preferred_element_type=jnp.float32)
            for t in range(2):
                piece = sums[:, t * 2 * bs : (t + 1) * 2 * bs]
                if s == 0 and first:
                    total[g, t] = piece
                else:
                    total[g, t] += piece
            return carry

        lax.fori_loop(0, groups, body, 0, unroll=min(groups, 4))


def first_kernel(done, a_ref, *refs):
    *parts, total, feet, where, sem = refs
    fetch_feet(parts, feet, where, sem).wait()
    add_products(done, a_ref, parts, total, True, where)


def middle_kernel(done, a_ref, before, *refs):
    *parts, total, feet, where, sem = refs
    fetch_feet(parts, feet, where, sem).wait()
    add_products(done, a_ref, parts, total, False, where)


def last_kernel(done, a_ref, total, cols_hbm, *refs):
    *parts, o_hbm, feet, where, sem, cols_ref, o_ref, cols_sem, sems = refs
    fetch = pltpu.make_async_copy(cols_hbm, cols_ref, cols_sem)
    fetch.start()
    fetch_feet(parts, feet, where, sem).wait()
    add_products(done, a_ref, parts, total, False, where)
    fetch.wait()
    rows, slots, bs, _ = o_ref.shape
    half = total.shape[0] * 4
    copies = [pltpu.make_async_copy(o_ref.at[i], o_hbm.at[i], sems.at[i]) for i in range(rows)]
    for i in range(rows):
        for k in range(slots):
            l = lax.rem(cols_ref[i, k], half)
            tile = total[l // 4, (l // 2) % 2, i * bs : (i + 1) * bs, :]
            tile = jnp.where(l % 2 == 0, tile, pltpu.roll(tile, bs, 1))
            o_ref[i, k] = tile[:, :bs].astype(o_ref.dtype)
        copies[i].start()
    for copy in copies:
        copy.wait()


def product(kernel, done, a, total, parts, out, cols=None):
    parts = [part for source in parts for part in source]
    hbm, vmem = pl.BlockSpec(memory_space=pl.ANY), pl.BlockSpec(memory_space=VMEM)
    lanes = parts[0].shape[1]
    scratch = [
        VMEM((len(parts), FOOT, lanes), jnp.int32),
        SMEM((len(parts), FOOT, lanes), jnp.int32),
        pltpu.SemaphoreType.DMA,
    ]
    arrays, specs = [a], [vmem]
    if total is not None:
        arrays, specs = arrays + [total], specs + [vmem]
    if cols is not None:
        arrays, specs = arrays + [cols], specs + [hbm]
        scratch += [
            SMEM(cols.shape, cols.dtype),
            VMEM(out.shape, out.dtype),
            pltpu.SemaphoreType.DMA,
            pltpu.SemaphoreType.DMA(out.shape[:1]),
        ]
    return pl.pallas_call(
        functools.partial(kernel, done),
        out_shape=out,
        in_specs=specs + [vmem] * len(parts),
        out_specs=vmem if cols is None else hbm,
        scratch_shapes=scratch,
        input_output_aliases={1: 0} if total is not None and cols is None else {},
        compiler_params=params(),
        cost_estimate=cost(BUSY * len(parts) * a.shape[2] * math.prod(out.shape) // 2, 0),
    )(*arrays, *parts)


def local(order, a_vals, b_vals, cols):
    sources = len(order)
    rows, slots, bs, _ = a_vals.shape
    half = sources * rows // 2
    pairs = rows // 2
    spots = {r: k for k, r in enumerate(order)}
    hops = {1: sources // 2, -1: (sources - 1) // 2}
    trips = [(way, step) for step in range(1, hops[1] + 1) for way in (1, -1) if step <= hops[way]]
    def ring(way):
        return [
            (order[r] * 2 + c, order[(r + (way if c == 0 else -way)) % sources] * 2 + c)
            for r in range(sources)
            for c in range(2)
        ]

    names = np.asarray(
        [
            [[r] + [order[(spots[r] - (w if c == 0 else -w) * t) % sources] for w, t in trips] for c in range(2)]
            for r in range(sources)
        ],
        np.int32,
    )
    ids = jnp.asarray(names)[lax.axis_index("row"), lax.axis_index("col")]

    own = pack(half, cols, b_vals)
    swap = [(0, 1), (1, 0)]
    *own, a_later, cols_later = lax.optimization_barrier((*own, a_vals, cols))
    others = lax.ppermute(cols_later, "col", swap)
    a_other = lax.ppermute(a_later, "col", swap)
    rounds = [[own]]
    held = {1: list(own), -1: list(own)}
    for step in range(1, hops[1] + 1):
        ways = [way for way in (1, -1) if step <= hops[way]]
        for p in range(pairs):
            for way in ways:
                held[way][p] = lax.ppermute(held[way][p], ("row", "col"), ring(way))
        rounds.append([list(held[way]) for way in ways])
    a = dense_rows(ids, cols, others, a_vals, a_other)
    total_shape = jax.ShapeDtypeStruct((half // 4, 2, rows * bs, 2 * bs), jnp.float32)
    total, done = None, 0
    for step, parts in enumerate(rounds):
        if step == 0:
            total = product(first_kernel, done, a, None, parts, total_shape)
        elif step < len(rounds) - 1:
            total = product(middle_kernel, done, a, total, parts, total_shape)
        else:
            out = jax.ShapeDtypeStruct(a_vals.shape, a_vals.dtype)
            return product(last_kernel, done, a, total, parts, out, cols)
        done += len(parts)


def ring_order(mesh):
    count = mesh.shape["row"]
    coords = [getattr(d, "coords", None) for d in mesh.devices[0, :, 0]]
    loop = [*range(0, count, 2), *range(count - 1 - count % 2, 0, -2)]
    if None not in coords:
        steps = [
            sum(abs(x - y) for x, y in zip(coords[loop[k - 1]], coords[loop[k]]))
            for k in range(count)
        ]
        if max(steps) <= 1:
            return loop
    return list(range(count))


def solution(mesh):
    return jax.shard_map(
        functools.partial(local, ring_order(mesh)),
        mesh=mesh,
        in_specs=(
            P(("groups", "row"), "col", None, None),
            P(("groups", "row"), "col", None, None),
            P(("groups", "row"), "col"),
        ),
        out_specs=P(("groups", "row"), "col", None, None),
        check_vma=False,
    )
```

```python
import functools
import math

import jax
import jax.numpy as jnp
import numpy as np
from jax import lax
from jax.experimental import pallas as pl
from jax.experimental.pallas import tpu as pltpu
from jax.sharding import PartitionSpec as P

VMEM = pltpu.VMEM
SMEM = pltpu.SMEM
LIMIT = 48 * 1024 * 1024
WHOLE = 63 * 1024 * 1024
BUSY = 100
FOOT = 16


def params(limit=LIMIT):
    return pltpu.CompilerParams(vmem_limit_bytes=limit)


def cost(flops, size):
    return pl.CostEstimate(flops=flops, bytes_accessed=size, transcendentals=0)


def pack_kernel(half, cols_hbm, b_hbm, *refs):
    *o_refs, cols_ref, b_ref, sem, sems = refs
    rows, slots, bs, _ = b_ref.shape
    copies = [pltpu.make_async_copy(b_hbm.at[r], b_ref.at[r], sems.at[r]) for r in range(rows)]
    fetch = pltpu.make_async_copy(cols_hbm, cols_ref, sem)
    fetch.start()
    for copy in copies:
        copy.start()
    row = lax.broadcasted_iota(jnp.int32, (FOOT, 2 * bs), 0)
    lane = lax.broadcasted_iota(jnp.int32, (FOOT, 2 * bs), 1)
    fetch.wait()
    for p, o_ref in enumerate(o_refs):
        foot = jnp.full((FOOT, 2 * bs), slots, jnp.int32)
        for h in range(2):
            for n in range(slots):
                here = (row == h) & (lane == lax.rem(cols_ref[2 * p + h, n], half))
                foot = jnp.where(here, n, foot)
        o_ref[slots * bs :, :] = foot.astype(jnp.float32).astype(o_ref.dtype)
        copies[2 * p].wait()
        copies[2 * p + 1].wait()
        for n in range(slots):
            o_ref[n * bs : (n + 1) * bs, :] = jnp.concatenate([b_ref[2 * p, n], b_ref[2 * p + 1, n]], axis=-1)


def pack(half, cols, b_vals):
    rows, slots, bs, _ = b_vals.shape
    shape = jax.ShapeDtypeStruct((slots * bs + FOOT, 2 * bs), b_vals.dtype)
    return pl.pallas_call(
        functools.partial(pack_kernel, half),
        out_shape=[shape] * (rows // 2),
        in_specs=[pl.BlockSpec(memory_space=pl.ANY)] * 2,
        out_specs=[pl.BlockSpec(memory_space=VMEM)] * (rows // 2),
        scratch_shapes=[
            SMEM(cols.shape, cols.dtype),
            VMEM(b_vals.shape, b_vals.dtype),
            pltpu.SemaphoreType.DMA,
            pltpu.SemaphoreType.DMA((rows,)),
        ],
        compiler_params=params(WHOLE),
        cost_estimate=cost(0, 2 * b_vals.size * 2),
    )(cols, b_vals)


def dense_kernel(ids_ref, cols_ref, others_ref, own_ref, other_ref, o_ref, blocks, where):
    rows, slots, bs, _ = own_ref.shape
    sources, pairs = o_ref.shape[:2]
    blocks[:, :slots] = own_ref[...]
    blocks[:, slots : 2 * slots] = other_ref[...]
    blocks[:, 2 * slots] = jnp.zeros_like(blocks[:, 2 * slots])
    for i in range(rows):
        def clear(j, carry):
            where[i, j] = 2 * slots
            return carry

        lax.fori_loop(0, 2 * sources * pairs, clear, 0, unroll=8)
        for m in range(slots):
            where[i, cols_ref[i, m]] = m
            where[i, others_ref[i, m]] = slots + m

    def body(s, carry):
        for p in range(pairs):
            j = (ids_ref[s] * pairs + p) * 2
            for i in range(rows):
                left = blocks[i, where[i, j]]
                right = blocks[i, where[i, j + 1]]
                o_ref[s, p, i * bs : (i + 1) * bs, :] = jnp.concatenate([left, right], axis=-1)
        return carry

    lax.fori_loop(0, sources, body, 0, unroll=2)


def dense_rows(ids, cols, others, own, other):
    rows, slots, bs, _ = own.shape
    sources = ids.shape[0]
    return pl.pallas_call(
        dense_kernel,
        out_shape=jax.ShapeDtypeStruct((sources, rows // 2, rows * bs, 2 * bs), own.dtype),
        grid_spec=pltpu.PrefetchScalarGridSpec(
            num_scalar_prefetch=3,
            grid=(),
            in_specs=[pl.BlockSpec(memory_space=VMEM)] * 2,
            out_specs=pl.BlockSpec(memory_space=VMEM),
            scratch_shapes=[
                VMEM((rows, 2 * slots + 1, bs, bs), own.dtype),
                SMEM((rows, sources * rows), jnp.int32),
            ],
        ),
        compiler_params=params(),
        cost_estimate=cost(0, BUSY * 8 * own.size),
    )(ids, cols, others, own, other)


def fetch_feet(parts, feet, where, sem):
    for k, part in enumerate(parts):
        feet[k] = part[part.shape[0] - FOOT :, :].astype(jnp.float32).astype(jnp.int32)
    copy = pltpu.make_async_copy(feet, where, sem)
    copy.start()
    return copy


def add_products(done, a_ref, parts, total, first, where):
    groups, bs = total.shape[0], total.shape[3] // 2
    slots = (parts[0].shape[0] - FOOT) // bs
    pairs = a_ref.shape[1]
    low = lax.broadcasted_iota(jnp.int32, (bs, 2 * bs), 1) < bs

    def block(part, slot):
        at = pl.multiple_of(jnp.minimum(slot, slots - 1) * bs, bs)
        return jnp.where(slot < slots, part[pl.ds(at, bs), :], jnp.zeros((bs, 2 * bs), part.dtype))

    def turn(x):
        return jnp.concatenate([x[:, bs:], x[:, :bs]], axis=-1)

    for s in range(len(parts) // pairs):
        source = parts[s * pairs : (s + 1) * pairs]
        a = jnp.concatenate([a_ref[done + s, p] for p in range(pairs)], axis=-1)

        def body(g, carry, s=s, source=source, a=a):
            panel = []
            for p, part in enumerate(source):
                for h in range(2):
                    tiles = []
                    for q in (2 * g, 2 * g + 1):
                        left = block(part, where[s * pairs + p, h, 2 * q])
                        right = block(part, where[s * pairs + p, h, 2 * q + 1])
                        if h == 0:
                            right = turn(right)
                        else:
                            left = turn(left)
                        tiles.append(jnp.where(low, left, right))
                    panel.append(jnp.concatenate(tiles, axis=-1))
            sums = jnp.dot(a, jnp.concatenate(panel, axis=0), preferred_element_type=jnp.float32)
            for t in range(2):
                piece = sums[:, t * 2 * bs : (t + 1) * 2 * bs]
                if s == 0 and first:
                    total[g, t] = piece
                else:
                    total[g, t] += piece
            return carry

        lax.fori_loop(0, groups, body, 0, unroll=min(groups, 4))


def first_kernel(done, a_ref, *refs):
    *parts, total, feet, where, sem = refs
    fetch_feet(parts, feet, where, sem).wait()
    add_products(done, a_ref, parts, total, True, where)


def middle_kernel(done, a_ref, before, *refs):
    *parts, total, feet, where, sem = refs
    fetch_feet(parts, feet, where, sem).wait()
    add_products(done, a_ref, parts, total, False, where)


def last_kernel(done, a_ref, total, cols_hbm, *refs):
    *parts, o_hbm, feet, where, sem, cols_ref, o_ref, cols_sem, sems = refs
    fetch = pltpu.make_async_copy(cols_hbm, cols_ref, cols_sem)
    fetch.start()
    fetch_feet(parts, feet, where, sem).wait()
    add_products(done, a_ref, parts, total, False, where)
    fetch.wait()
    rows, slots, bs, _ = o_ref.shape
    half = total.shape[0] * 4
    copies = [pltpu.make_async_copy(o_ref.at[i], o_hbm.at[i], sems.at[i]) for i in range(rows)]
    for i in range(rows):
        for k in range(slots):
            l = lax.rem(cols_ref[i, k], half)
            tile = total[l // 4, (l // 2) % 2, i * bs : (i + 1) * bs, :]
            tile = jnp.where(l % 2 == 0, tile, pltpu.roll(tile, bs, 1))
            o_ref[i, k] = tile[:, :bs].astype(o_ref.dtype)
        copies[i].start()
    for copy in copies:
        copy.wait()


def product(kernel, done, a, total, parts, out, cols=None):
    parts = [part for source in parts for part in source]
    hbm, vmem = pl.BlockSpec(memory_space=pl.ANY), pl.BlockSpec(memory_space=VMEM)
    lanes = parts[0].shape[1]
    scratch = [
        VMEM((len(parts), FOOT, lanes), jnp.int32),
        SMEM((len(parts), FOOT, lanes), jnp.int32),
        pltpu.SemaphoreType.DMA,
    ]
    arrays, specs = [a], [vmem]
    if total is not None:
        arrays, specs = arrays + [total], specs + [vmem]
    if cols is not None:
        arrays, specs = arrays + [cols], specs + [hbm]
        scratch += [
            SMEM(cols.shape, cols.dtype),
            VMEM(out.shape, out.dtype),
            pltpu.SemaphoreType.DMA,
            pltpu.SemaphoreType.DMA(out.shape[:1]),
        ]
    return pl.pallas_call(
        functools.partial(kernel, done),
        out_shape=out,
        in_specs=specs + [vmem] * len(parts),
        out_specs=vmem if cols is None else hbm,
        scratch_shapes=scratch,
        input_output_aliases={1: 0} if total is not None and cols is None else {},
        compiler_params=params(),
        cost_estimate=cost(BUSY * len(parts) * a.shape[2] * math.prod(out.shape) // 2, 0),
    )(*arrays, *parts)


def local(order, a_vals, b_vals, cols):
    sources = len(order)
    rows, slots, bs, _ = a_vals.shape
    half = sources * rows // 2
    pairs = rows // 2
    spots = {r: k for k, r in enumerate(order)}
    hops = {1: sources // 2, -1: (sources - 1) // 2}
    trips = [(way, step) for step in range(1, hops[1] + 1) for way in (1, -1) if step <= hops[way]]
    def ring(way):
        return [
            (order[r] * 2 + c, order[(r + (way if c == 0 else -way)) % sources] * 2 + c)
            for r in range(sources)
            for c in range(2)
        ]

    names = np.asarray(
        [
            [[r] + [order[(spots[r] - (w if c == 0 else -w) * t) % sources] for w, t in trips] for c in range(2)]
            for r in range(sources)
        ],
        np.int32,
    )
    ids = jnp.asarray(names)[lax.axis_index("row"), lax.axis_index("col")]

    own = pack(half, cols, b_vals)
    swap = [(0, 1), (1, 0)]
    a_other, others = (lax.ppermute(x, "col", swap) for x in (a_vals, cols))
    a = dense_rows(ids, cols, others, a_vals, a_other)
    held = {way: list(own) for way in hops}
    rounds = [[own]]
    for step in range(1, hops[1] + 1):
        ways = [way for way in hops if step <= hops[way]]
        for p in range(pairs):
            for way in ways:
                part = held[way][p]
                if step == 2:
                    part, _ = lax.optimization_barrier((part, a))
                held[way][p] = lax.ppermute(part, ("row", "col"), ring(way))
        rounds.append([list(held[way]) for way in ways])
    rounds[:2] = [rounds[0] + rounds[1]]
    total_shape = jax.ShapeDtypeStruct((half // 4, 2, rows * bs, 2 * bs), jnp.float32)
    total = product(first_kernel, 0, a, None, rounds[0], total_shape)
    used = len(rounds[0])
    for parts in rounds[1:-1]:
        total = product(middle_kernel, used, a, total, parts, total_shape)
        used += len(parts)
    out = jax.ShapeDtypeStruct(a_vals.shape, a_vals.dtype)
    return product(last_kernel, used, a, total, rounds[-1], out, cols)


def ring_order(mesh):
    count = mesh.shape["row"]
    coords = [getattr(d, "coords", None) for d in mesh.devices[0, :, 0]]
    loop = [*range(0, count, 2), *range(count - 1 - count % 2, 0, -2)]
    if None not in coords:
        steps = [
            sum(abs(x - y) for x, y in zip(coords[loop[k - 1]], coords[loop[k]]))
            for k in range(count)
        ]
        if max(steps) <= 1:
            return loop
    return list(range(count))


def solution(mesh):
    return jax.shard_map(
        functools.partial(local, ring_order(mesh)),
        mesh=mesh,
        in_specs=(
            P(("groups", "row"), "col", None, None),
            P(("groups", "row"), "col", None, None),
            P(("groups", "row"), "col"),
        ),
        out_specs=P(("groups", "row"), "col", None, None),
        check_vma=False,
    )
```

```python
import functools
import math

import jax
import jax.numpy as jnp
import numpy as np
from jax import lax
from jax.experimental import pallas as pl
from jax.experimental.pallas import tpu as pltpu
from jax.sharding import PartitionSpec as P

VMEM = pltpu.VMEM
SMEM = pltpu.SMEM
LIMIT = 48 * 1024 * 1024
WHOLE = 63 * 1024 * 1024
BUSY = 5
FOOT = 16


def params(limit=LIMIT):
    return pltpu.CompilerParams(vmem_limit_bytes=limit)


def cost(flops, size):
    return pl.CostEstimate(flops=flops, bytes_accessed=size, transcendentals=0)


def pack_kernel(half, cols_hbm, b_hbm, o_ref, cols_ref, b_ref, sem, sems):
    rows, slots, bs, _ = b_ref.shape
    copies = [pltpu.make_async_copy(b_hbm.at[r], b_ref.at[r], sems.at[r]) for r in range(rows)]
    fetch = pltpu.make_async_copy(cols_hbm, cols_ref, sem)
    fetch.start()
    for copy in copies:
        copy.start()
    row = lax.broadcasted_iota(jnp.int32, (FOOT, 2 * bs), 0)
    lane = lax.broadcasted_iota(jnp.int32, (FOOT, 2 * bs), 1)
    fetch.wait()
    foot = jnp.full((FOOT, 2 * bs), slots, jnp.int32)
    for r in range(rows):
        for n in range(slots):
            here = (row == r) & (lane == lax.rem(cols_ref[r, n], half))
            foot = jnp.where(here, n, foot)
    o_ref[rows // 2 * slots * bs :, :] = foot.astype(jnp.float32).astype(o_ref.dtype)
    for p in range(rows // 2):
        copies[2 * p].wait()
        copies[2 * p + 1].wait()
        for n in range(slots):
            at = (p * slots + n) * bs
            o_ref[at : at + bs, :] = jnp.concatenate([b_ref[2 * p, n], b_ref[2 * p + 1, n]], axis=-1)


def pack(half, cols, b_vals):
    rows, slots, bs, _ = b_vals.shape
    return pl.pallas_call(
        functools.partial(pack_kernel, half),
        out_shape=jax.ShapeDtypeStruct((rows // 2 * slots * bs + FOOT, 2 * bs), b_vals.dtype),
        in_specs=[pl.BlockSpec(memory_space=pl.ANY)] * 2,
        out_specs=pl.BlockSpec(memory_space=VMEM),
        scratch_shapes=[
            SMEM(cols.shape, cols.dtype),
            VMEM(b_vals.shape, b_vals.dtype),
            pltpu.SemaphoreType.DMA,
            pltpu.SemaphoreType.DMA((rows,)),
        ],
        compiler_params=params(WHOLE),
        cost_estimate=cost(0, 2 * b_vals.size * 2),
    )(cols, b_vals)


def dense_kernel(cols_ref, others_ref, own_ref, other_ref, o_ref, blocks, where):
    rows, slots, bs, _ = own_ref.shape
    sources, pairs = o_ref.shape[:2]
    blocks[:, :slots] = own_ref[...]
    blocks[:, slots : 2 * slots] = other_ref[...]
    blocks[:, 2 * slots] = jnp.zeros_like(blocks[:, 2 * slots])
    for i in range(rows):
        def clear(j, carry):
            where[i, j] = 2 * slots
            return carry

        lax.fori_loop(0, 2 * sources * pairs, clear, 0, unroll=8)
        for m in range(slots):
            where[i, cols_ref[i, m]] = m
            where[i, others_ref[i, m]] = slots + m

    def body(s, carry):
        for p in range(pairs):
            j = (s * pairs + p) * 2
            for i in range(rows):
                left = blocks[i, where[i, j]]
                right = blocks[i, where[i, j + 1]]
                o_ref[s, p, i * bs : (i + 1) * bs, :] = jnp.concatenate([left, right], axis=-1)
        return carry

    lax.fori_loop(0, sources, body, 0, unroll=2)


def dense_rows(sources, cols, others, own, other):
    rows, slots, bs, _ = own.shape
    return pl.pallas_call(
        dense_kernel,
        out_shape=jax.ShapeDtypeStruct((sources, rows // 2, rows * bs, 2 * bs), own.dtype),
        grid_spec=pltpu.PrefetchScalarGridSpec(
            num_scalar_prefetch=2,
            grid=(),
            in_specs=[pl.BlockSpec(memory_space=VMEM)] * 2,
            out_specs=pl.BlockSpec(memory_space=VMEM),
            scratch_shapes=[
                VMEM((rows, 2 * slots + 1, bs, bs), own.dtype),
                SMEM((rows, sources * rows), jnp.int32),
            ],
        ),
        compiler_params=params(),
        cost_estimate=cost(0, BUSY * 8 * own.size),
    )(cols, others, own, other)


def look_up(table, k):
    value = jnp.int32(table[0])
    for n, entry in enumerate(table[1:], 1):
        value = jnp.where(k == n, entry, value)
    return value


def arrived_from(order, way, steps):
    spots = [order.index(r) for r in range(len(order))]
    ahead = jnp.where(lax.axis_index("col") == 0, way, -way) * steps
    return look_up(order, lax.rem(look_up(spots, lax.axis_index("row")) - ahead + len(order), len(order)))


def add_products(a, part, total, first, feet, where, sem):
    groups, bs = total.shape[0], total.shape[3] // 2
    pairs = a.shape[0]
    slots = (part.shape[0] - FOOT) // bs // pairs
    feet[...] = part[pairs * slots * bs :, :].astype(jnp.float32).astype(jnp.int32)
    copy = pltpu.make_async_copy(feet, where, sem)
    copy.start()
    copy.wait()
    low = lax.broadcasted_iota(jnp.int32, (bs, 2 * bs), 1) < bs
    panels = jnp.concatenate([a[p] for p in range(pairs)], axis=-1)

    def block(p, slot):
        at = pl.multiple_of((p * slots + jnp.minimum(slot, slots - 1)) * bs, bs)
        return jnp.where(slot < slots, part[pl.ds(at, bs), :], jnp.zeros((bs, 2 * bs), part.dtype))

    def turn(x):
        return jnp.concatenate([x[:, bs:], x[:, :bs]], axis=-1)

    def body(g, carry):
        panel = []
        for p in range(pairs):
            for h in range(2):
                tiles = []
                for q in (2 * g, 2 * g + 1):
                    left = block(p, where[2 * p + h, 2 * q])
                    right = block(p, where[2 * p + h, 2 * q + 1])
                    if h == 0:
                        right = turn(right)
                    else:
                        left = turn(left)
                    tiles.append(jnp.where(low, left, right))
                panel.append(jnp.concatenate(tiles, axis=-1))
        sums = jnp.dot(panels, jnp.concatenate(panel, axis=0), preferred_element_type=jnp.float32)
        for t in range(2):
            piece = sums[:, t * 2 * bs : (t + 1) * 2 * bs]
            if first:
                total[g, t] = piece
            else:
                total[g, t] += piece
        return carry

    lax.fori_loop(0, groups, body, 0, unroll=min(groups, 4))


def first_kernel(source, a_ref, part, total, *scratch):
    add_products(a_ref.at[source()], part, total, True, *scratch)


def middle_kernel(source, a_ref, before, part, total, *scratch):
    add_products(a_ref.at[source()], part, total, False, *scratch)


def last_kernel(source, a_ref, total, cols_hbm, part, o_hbm, feet, where, sem, cols_ref, o_ref, cols_sem, sems):
    fetch = pltpu.make_async_copy(cols_hbm, cols_ref, cols_sem)
    fetch.start()
    add_products(a_ref.at[source()], part, total, False, feet, where, sem)
    fetch.wait()
    rows, slots, bs, _ = o_ref.shape
    half = total.shape[0] * 4
    copies = [pltpu.make_async_copy(o_ref.at[i], o_hbm.at[i], sems.at[i]) for i in range(rows)]
    for i in range(rows):
        for k in range(slots):
            l = lax.rem(cols_ref[i, k], half)
            tile = total[l // 4, (l // 2) % 2, i * bs : (i + 1) * bs, :]
            tile = jnp.where(l % 2 == 0, tile, pltpu.roll(tile, bs, 1))
            o_ref[i, k] = tile[:, :bs].astype(o_ref.dtype)
        copies[i].start()
    for copy in copies:
        copy.wait()


def product(kernel, source, a, total, part, out, cols=None):
    hbm, vmem = pl.BlockSpec(memory_space=pl.ANY), pl.BlockSpec(memory_space=VMEM)
    scratch = [
        VMEM((FOOT, part.shape[1]), jnp.int32),
        SMEM((FOOT, part.shape[1]), jnp.int32),
        pltpu.SemaphoreType.DMA,
    ]
    arrays, specs = [a], [vmem]
    if total is not None:
        arrays, specs = arrays + [total], specs + [vmem]
    if cols is not None:
        arrays, specs = arrays + [cols], specs + [hbm]
        scratch += [
            SMEM(cols.shape, cols.dtype),
            VMEM(out.shape, out.dtype),
            pltpu.SemaphoreType.DMA,
            pltpu.SemaphoreType.DMA(out.shape[:1]),
        ]
    return pl.pallas_call(
        functools.partial(kernel, source),
        out_shape=out,
        in_specs=specs + [vmem],
        out_specs=vmem if cols is None else hbm,
        scratch_shapes=scratch,
        input_output_aliases={1: 0} if total is not None and cols is None else {},
        compiler_params=params(),
        cost_estimate=cost(BUSY * 2 * a.shape[2] * math.prod(out.shape), 0),
    )(*arrays, part)


def local(order, a_vals, b_vals, cols):
    sources = len(order)
    rows, slots, bs, _ = a_vals.shape
    half = sources * rows // 2
    hops = {1: sources // 2, -1: (sources - 1) // 2}

    def ring(way):
        return [
            (order[r] * 2 + c, order[(r + (way if c == 0 else -way)) % sources] * 2 + c)
            for r in range(sources)
            for c in range(2)
        ]

    own = pack(half, cols, b_vals)
    _, *mine = lax.optimization_barrier((own, a_vals, cols))
    swap = [(0, 1), (1, 0)]
    a_other, others = (lax.ppermute(x, "col", swap) for x in mine)
    a = dense_rows(sources, cols, others, a_vals, a_other)
    total_shape = jax.ShapeDtypeStruct((half // 4, 2, rows * bs, 2 * bs), jnp.float32)
    waiting = [(0, 1, own)]
    total = None

    def add():
        step, way, part = waiting.pop(0)
        kernel = first_kernel if total is None else middle_kernel
        return product(kernel, functools.partial(arrived_from, order, way, step), a, total, part, total_shape)

    held = {1: own, -1: own}
    for step in range(1, hops[1] + 1):
        for way in hops:
            if step > hops[way]:
                continue
            part = held[way]
            if step > 1:
                waiting.append((step - 1, way, part))
                if total is None:
                    part, a = lax.optimization_barrier((part, a))
                else:
                    part, total = lax.optimization_barrier((part, total))
            held[way] = lax.ppermute(part, ("row", "col"), ring(way))
            if step > 1:
                total = add()
    waiting += [(step - 1, -1, held[-1])] if hops[-1] < hops[1] else []
    waiting += [(hops[-1], -1, held[-1])] if hops[-1] == hops[1] else []
    while waiting:
        total = add()
    out = jax.ShapeDtypeStruct(a_vals.shape, a_vals.dtype)
    source = functools.partial(arrived_from, order, 1, hops[1])
    return product(last_kernel, source, a, total, held[1], out, cols)


def ring_order(mesh):
    count = mesh.shape["row"]
    coords = [getattr(d, "coords", None) for d in mesh.devices[0, :, 0]]
    loop = [*range(0, count, 2), *range(count - 1 - count % 2, 0, -2)]
    if None not in coords:
        steps = [
            sum(abs(x - y) for x, y in zip(coords[loop[k - 1]], coords[loop[k]]))
            for k in range(count)
        ]
        if max(steps) <= 1:
            return loop
    return list(range(count))


def solution(mesh):
    return jax.shard_map(
        functools.partial(local, ring_order(mesh)),
        mesh=mesh,
        in_specs=(
            P(("groups", "row"), "col", None, None),
            P(("groups", "row"), "col", None, None),
            P(("groups", "row"), "col"),
        ),
        out_specs=P(("groups", "row"), "col", None, None),
        check_vma=False,
    )
```

```python
import functools
import math

import jax
import jax.numpy as jnp
import numpy as np
from jax import lax
from jax.experimental import pallas as pl
from jax.experimental.pallas import tpu as pltpu
from jax.sharding import PartitionSpec as P

VMEM = pltpu.VMEM
SMEM = pltpu.SMEM
LIMIT = 48 * 1024 * 1024
WHOLE = 63 * 1024 * 1024
TIE = 3
FOOT = 16


def params(limit=LIMIT):
    return pltpu.CompilerParams(vmem_limit_bytes=limit)


def cost(flops, size):
    return pl.CostEstimate(flops=flops, bytes_accessed=size, transcendentals=0)


def pack_kernel(half, cols_hbm, b_hbm, *refs):
    *o_refs, cols_ref, b_ref, sem, sems = refs
    rows, slots, bs, _ = b_ref.shape
    copies = [pltpu.make_async_copy(b_hbm.at[r], b_ref.at[r], sems.at[r]) for r in range(rows)]
    fetch = pltpu.make_async_copy(cols_hbm, cols_ref, sem)
    fetch.start()
    for copy in copies:
        copy.start()
    row = lax.broadcasted_iota(jnp.int32, (FOOT, 2 * bs), 0)
    lane = lax.broadcasted_iota(jnp.int32, (FOOT, 2 * bs), 1)
    fetch.wait()
    for p, o_ref in enumerate(o_refs):
        foot = jnp.full((FOOT, 2 * bs), slots, jnp.int32)
        for h in range(2):
            for n in range(slots):
                here = (row == h) & (lane == lax.rem(cols_ref[2 * p + h, n], half))
                foot = jnp.where(here, n, foot)
        o_ref[slots * bs :, :] = foot.astype(jnp.float32).astype(o_ref.dtype)
        copies[2 * p].wait()
        copies[2 * p + 1].wait()
        for n in range(slots):
            o_ref[n * bs : (n + 1) * bs, :] = jnp.concatenate([b_ref[2 * p, n], b_ref[2 * p + 1, n]], axis=-1)


def pack(half, cols, b_vals):
    rows, slots, bs, _ = b_vals.shape
    shapes = [(slots * bs + FOOT, 2 * bs)] * (rows // 2)
    return pl.pallas_call(
        functools.partial(pack_kernel, half),
        out_shape=[jax.ShapeDtypeStruct(shape, b_vals.dtype) for shape in shapes],
        in_specs=[pl.BlockSpec(memory_space=pl.ANY)] * 2,
        out_specs=[pl.BlockSpec(memory_space=VMEM)] * len(shapes),
        scratch_shapes=[
            SMEM(cols.shape, cols.dtype),
            VMEM(b_vals.shape, b_vals.dtype),
            pltpu.SemaphoreType.DMA,
            pltpu.SemaphoreType.DMA((rows,)),
        ],
        compiler_params=params(WHOLE),
        cost_estimate=cost(0, 2 * b_vals.size * 2),
    )(cols, b_vals)


def dense_kernel(cols_ref, others_ref, own_ref, other_ref, o_ref, blocks, where):
    rows, slots, bs, _ = own_ref.shape
    sources, pairs = o_ref.shape[:2]
    blocks[:, :slots] = own_ref[...]
    blocks[:, slots : 2 * slots] = other_ref[...]
    blocks[:, 2 * slots] = jnp.zeros_like(blocks[:, 2 * slots])
    for i in range(rows):
        def clear(j, carry):
            where[i, j] = 2 * slots
            return carry

        lax.fori_loop(0, 2 * sources * pairs, clear, 0, unroll=8)
        for m in range(slots):
            where[i, cols_ref[i, m]] = m
            where[i, others_ref[i, m]] = slots + m

    def body(s, carry):
        for p in range(pairs):
            j = (s * pairs + p) * 2
            for i in range(rows):
                left = blocks[i, where[i, j]]
                right = blocks[i, where[i, j + 1]]
                o_ref[s, p, i * bs : (i + 1) * bs, :] = jnp.concatenate([left, right], axis=-1)
        return carry

    lax.fori_loop(0, sources, body, 0, unroll=2)


def dense_rows(sources, cols, others, own, other):
    rows, slots, bs, _ = own.shape
    return pl.pallas_call(
        dense_kernel,
        out_shape=jax.ShapeDtypeStruct((sources, rows // 2, rows * bs, 2 * bs), own.dtype),
        grid_spec=pltpu.PrefetchScalarGridSpec(
            num_scalar_prefetch=2,
            grid=(),
            in_specs=[pl.BlockSpec(memory_space=VMEM)] * 2,
            out_specs=pl.BlockSpec(memory_space=VMEM),
            scratch_shapes=[
                VMEM((rows, 2 * slots + 1, bs, bs), own.dtype),
                SMEM((rows, sources * rows), jnp.int32),
            ],
        ),
        compiler_params=params(),
        cost_estimate=cost(0, 8 * own.size),
    )(cols, others, own, other)


def look_up(table, k):
    value = jnp.int32(table[0])
    for n, entry in enumerate(table[1:], 1):
        value = jnp.where(k == n, entry, value)
    return value


def arrived_from(order, way, steps):
    spots = [order.index(r) for r in range(len(order))]
    ahead = jnp.where(lax.axis_index("col") == 0, way, -way) * steps
    return look_up(order, lax.rem(look_up(spots, lax.axis_index("row")) - ahead + len(order), len(order)))


def add_products(panels, parts, total, first, feet, where, sem):
    groups, bs = total.shape[0], total.shape[3] // 2
    slots = (parts[0].shape[0] - FOOT) // bs
    for k, part in enumerate(parts):
        feet[k] = part[slots * bs :, :].astype(jnp.float32).astype(jnp.int32)
    copy = pltpu.make_async_copy(feet, where, sem)
    copy.start()
    copy.wait()
    low = lax.broadcasted_iota(jnp.int32, (bs, 2 * bs), 1) < bs
    left_side = jnp.concatenate([panel[...] for panel in panels], axis=-1)

    def block(part, slot):
        at = pl.multiple_of(jnp.minimum(slot, slots - 1) * bs, bs)
        return jnp.where(slot < slots, part[pl.ds(at, bs), :], jnp.zeros((bs, 2 * bs), part.dtype))

    def turn(x):
        return jnp.concatenate([x[:, bs:], x[:, :bs]], axis=-1)

    def body(g, carry):
        rows = []
        for k, part in enumerate(parts):
            for h in range(2):
                tiles = []
                for q in (2 * g, 2 * g + 1):
                    left = block(part, where[k, h, 2 * q])
                    right = block(part, where[k, h, 2 * q + 1])
                    if h == 0:
                        right = turn(right)
                    else:
                        left = turn(left)
                    tiles.append(jnp.where(low, left, right))
                rows.append(jnp.concatenate(tiles, axis=-1))
        sums = jnp.dot(left_side, jnp.concatenate(rows, axis=0), preferred_element_type=jnp.float32)
        for t in range(2):
            piece = sums[:, t * 2 * bs : (t + 1) * 2 * bs]
            if first:
                total[g, t] = piece
            else:
                total[g, t] += piece
        return carry

    lax.fori_loop(0, groups, body, 0, unroll=min(groups, 4))


def split(a_ref, sources, parts):
    return [a_ref.at[place, p] for place in [source() for source in sources] for p in range(a_ref.shape[1])], parts


def first_kernel(sources, a_ref, *refs):
    *parts, total, feet, where, sem = refs
    add_products(*split(a_ref, sources, parts), total, True, feet, where, sem)


def middle_kernel(sources, a_ref, before, *refs):
    *parts, total, feet, where, sem = refs
    add_products(*split(a_ref, sources, parts), total, False, feet, where, sem)


def last_kernel(sources, a_ref, total, cols_hbm, *refs):
    *parts, o_hbm, feet, where, sem, cols_ref, o_ref, cols_sem, sems = refs
    fetch = pltpu.make_async_copy(cols_hbm, cols_ref, cols_sem)
    fetch.start()
    add_products(*split(a_ref, sources, parts), total, False, feet, where, sem)
    fetch.wait()
    rows, slots, bs, _ = o_ref.shape
    half = total.shape[0] * 4
    copies = [pltpu.make_async_copy(o_ref.at[i], o_hbm.at[i], sems.at[i]) for i in range(rows)]
    for i in range(rows):
        for k in range(slots):
            l = lax.rem(cols_ref[i, k], half)
            tile = total[l // 4, (l // 2) % 2, i * bs : (i + 1) * bs, :]
            tile = jnp.where(l % 2 == 0, tile, pltpu.roll(tile, bs, 1))
            o_ref[i, k] = tile[:, :bs].astype(o_ref.dtype)
        copies[i].start()
    for copy in copies:
        copy.wait()


def product(order, arrived, a, total, out, cols=None):
    hbm, vmem = pl.BlockSpec(memory_space=pl.ANY), pl.BlockSpec(memory_space=VMEM)
    kernel = first_kernel if total is None else middle_kernel if cols is None else last_kernel
    sources = [functools.partial(arrived_from, order, way, steps) for way, steps, _ in arrived]
    parts = [ref for _, _, refs in arrived for ref in refs]
    feet = (len(arrived) * a.shape[1], FOOT, parts[0].shape[1])
    scratch = [VMEM(feet, jnp.int32), SMEM(feet, jnp.int32), pltpu.SemaphoreType.DMA]
    arrays, specs = [a], [vmem]
    if total is not None:
        arrays, specs = arrays + [total], specs + [vmem]
    if cols is not None:
        arrays, specs = arrays + [cols], specs + [hbm]
        scratch += [
            SMEM(cols.shape, cols.dtype),
            VMEM(out.shape, out.dtype),
            pltpu.SemaphoreType.DMA,
            pltpu.SemaphoreType.DMA(out.shape[:1]),
        ]
    return pl.pallas_call(
        functools.partial(kernel, sources),
        out_shape=out,
        in_specs=specs + [vmem] * len(parts),
        out_specs=vmem if cols is None else hbm,
        scratch_shapes=scratch,
        input_output_aliases={1: 0} if total is not None and cols is None else {},
        compiler_params=params(),
        cost_estimate=cost(2 * len(arrived) * a.shape[2] * math.prod(out.shape), 0),
    )(*arrays, *parts)


def local(order, a_vals, b_vals, cols):
    sources = len(order)
    rows, slots, bs, _ = a_vals.shape
    half = sources * rows // 2
    hops = {1: sources // 2, -1: (sources - 1) // 2}

    def ring(way):
        return [
            (order[r] * 2 + c, order[(r + (way if c == 0 else -way)) % sources] * 2 + c)
            for r in range(sources)
            for c in range(2)
        ]

    parts = pack(half, cols, b_vals)
    _, *mine = lax.optimization_barrier((parts[0], a_vals, cols))
    swap = [(0, 1), (1, 0)]
    a_other, others = (lax.ppermute(x, "col", swap) for x in mine)
    a = dense_rows(sources, cols, others, a_vals, a_other)
    total_shape = jax.ShapeDtypeStruct((half // 4, 2, rows * bs, 2 * bs), jnp.float32)
    total = None
    held = {way: parts for way in hops}
    arrived = [(1, 0, parts)]
    for step in range(1, hops[1] + 1):
        ways = [way for way in hops if step <= hops[way]]
        for way in ways:
            sent = list(held[way])
            if step == TIE:
                sent = [lax.optimization_barrier((part, a))[0] for part in sent]
            elif total is not None and way == 1:
                sent[0], total = lax.optimization_barrier((sent[0], total))
            held[way] = [lax.ppermute(part, ("row", "col"), ring(way)) for part in sent]
        if step == 1:
            arrived += [(way, 1, held[way]) for way in ways]
        elif step >= TIE:
            total = product(order, arrived, a, total, total_shape)
            arrived = before
        before = [(way, step, held[way]) for way in ways]
    total = product(order, arrived[:1], a, total, total_shape)
    out = jax.ShapeDtypeStruct(a_vals.shape, a_vals.dtype)
    return product(order, arrived[1:] + before, a, total, out, cols)


def ring_order(mesh):
    count = mesh.shape["row"]
    coords = [getattr(d, "coords", None) for d in mesh.devices[0, :, 0]]
    loop = [*range(0, count, 2), *range(count - 1 - count % 2, 0, -2)]
    if None not in coords:
        steps = [
            sum(abs(x - y) for x, y in zip(coords[loop[k - 1]], coords[loop[k]]))
            for k in range(count)
        ]
        if max(steps) <= 1:
            return loop
    return list(range(count))


def solution(mesh):
    return jax.shard_map(
        functools.partial(local, ring_order(mesh)),
        mesh=mesh,
        in_specs=(
            P(("groups", "row"), "col", None, None),
            P(("groups", "row"), "col", None, None),
            P(("groups", "row"), "col"),
        ),
        out_specs=P(("groups", "row"), "col", None, None),
        check_vma=False,
    )
```

```python
import functools
import math

import jax
import jax.numpy as jnp
import numpy as np
from jax import lax
from jax.experimental import pallas as pl
from jax.experimental.pallas import tpu as pltpu
from jax.sharding import PartitionSpec as P

VMEM = pltpu.VMEM
SMEM = pltpu.SMEM
LIMIT = 48 * 1024 * 1024
WHOLE = 63 * 1024 * 1024
FOOT = 16


def params(limit=LIMIT):
    return pltpu.CompilerParams(vmem_limit_bytes=limit)


def cost(flops, size):
    return pl.CostEstimate(flops=flops, bytes_accessed=size, transcendentals=0)


def pack_kernel(half, cols_hbm, b_hbm, *refs):
    *o_refs, cols_ref, b_ref, sem, sems = refs
    rows, slots, bs, _ = b_ref.shape
    copies = [pltpu.make_async_copy(b_hbm.at[r], b_ref.at[r], sems.at[r]) for r in range(rows)]
    fetch = pltpu.make_async_copy(cols_hbm, cols_ref, sem)
    fetch.start()
    for copy in copies:
        copy.start()
    row = lax.broadcasted_iota(jnp.int32, (FOOT, 2 * bs), 0)
    lane = lax.broadcasted_iota(jnp.int32, (FOOT, 2 * bs), 1)
    fetch.wait()
    for p, o_ref in enumerate(o_refs):
        foot = jnp.full((FOOT, 2 * bs), slots, jnp.int32)
        for h in range(2):
            for n in range(slots):
                here = (row == h) & (lane == lax.rem(cols_ref[2 * p + h, n], half))
                foot = jnp.where(here, n, foot)
        o_ref[slots * bs :, :] = foot.astype(jnp.float32).astype(o_ref.dtype)
        copies[2 * p].wait()
        copies[2 * p + 1].wait()
        for n in range(slots):
            o_ref[n * bs : (n + 1) * bs, :] = jnp.concatenate([b_ref[2 * p, n], b_ref[2 * p + 1, n]], axis=-1)


def pack(half, cols, b_vals):
    rows, slots, bs, _ = b_vals.shape
    shapes = [(slots * bs + FOOT, 2 * bs)] * (rows // 2)
    return pl.pallas_call(
        functools.partial(pack_kernel, half),
        out_shape=[jax.ShapeDtypeStruct(shape, b_vals.dtype) for shape in shapes],
        in_specs=[pl.BlockSpec(memory_space=pl.ANY)] * 2,
        out_specs=[pl.BlockSpec(memory_space=VMEM)] * len(shapes),
        scratch_shapes=[
            SMEM(cols.shape, cols.dtype),
            VMEM(b_vals.shape, b_vals.dtype),
            pltpu.SemaphoreType.DMA,
            pltpu.SemaphoreType.DMA((rows,)),
        ],
        compiler_params=params(WHOLE),
        cost_estimate=cost(0, 2 * b_vals.size * 2),
    )(cols, b_vals)


def dense_kernel(cols_ref, others_ref, own_ref, other_ref, o_ref, blocks, where):
    rows, slots, bs, _ = own_ref.shape
    sources, pairs = o_ref.shape[:2]
    blocks[:, :slots] = own_ref[...]
    blocks[:, slots : 2 * slots] = other_ref[...]
    blocks[:, 2 * slots] = jnp.zeros_like(blocks[:, 2 * slots])
    for i in range(rows):
        def clear(j, carry):
            where[i, j] = 2 * slots
            return carry

        lax.fori_loop(0, 2 * sources * pairs, clear, 0, unroll=8)
        for m in range(slots):
            where[i, cols_ref[i, m]] = m
            where[i, others_ref[i, m]] = slots + m

    def body(s, carry):
        for p in range(pairs):
            j = (s * pairs + p) * 2
            for i in range(rows):
                left = blocks[i, where[i, j]]
                right = blocks[i, where[i, j + 1]]
                o_ref[s, p, i * bs : (i + 1) * bs, :] = jnp.concatenate([left, right], axis=-1)
        return carry

    lax.fori_loop(0, sources, body, 0, unroll=2)


def dense_rows(sources, cols, others, own, other):
    rows, slots, bs, _ = own.shape
    return pl.pallas_call(
        dense_kernel,
        out_shape=jax.ShapeDtypeStruct((sources, rows // 2, rows * bs, 2 * bs), own.dtype),
        grid_spec=pltpu.PrefetchScalarGridSpec(
            num_scalar_prefetch=2,
            grid=(),
            in_specs=[pl.BlockSpec(memory_space=VMEM)] * 2,
            out_specs=pl.BlockSpec(memory_space=VMEM),
            scratch_shapes=[
                VMEM((rows, 2 * slots + 1, bs, bs), own.dtype),
                SMEM((rows, sources * rows), jnp.int32),
            ],
        ),
        compiler_params=params(),
        cost_estimate=cost(0, 8 * own.size),
    )(cols, others, own, other)


def look_up(table, k):
    value = jnp.int32(table[0])
    for n, entry in enumerate(table[1:], 1):
        value = jnp.where(k == n, entry, value)
    return value


def arrived_from(order, way, steps):
    spots = [order.index(r) for r in range(len(order))]
    ahead = jnp.where(lax.axis_index("col") == 0, way, -way) * steps
    return look_up(order, lax.rem(look_up(spots, lax.axis_index("row")) - ahead + len(order), len(order)))


def add_products(panels, parts, total, first, feet, where, sem):
    groups, bs = total.shape[0], total.shape[3] // 2
    slots = (parts[0].shape[0] - FOOT) // bs
    for k, part in enumerate(parts):
        feet[k] = part[slots * bs :, :].astype(jnp.float32).astype(jnp.int32)
    copy = pltpu.make_async_copy(feet, where, sem)
    copy.start()
    copy.wait()
    low = lax.broadcasted_iota(jnp.int32, (bs, 2 * bs), 1) < bs
    left_side = jnp.concatenate([panel[...] for panel in panels], axis=-1)

    def block(part, slot):
        at = pl.multiple_of(jnp.minimum(slot, slots - 1) * bs, bs)
        return jnp.where(slot < slots, part[pl.ds(at, bs), :], jnp.zeros((bs, 2 * bs), part.dtype))

    def body(g, carry):
        rows = []
        for k, part in enumerate(parts):
            for h in range(2):
                tiles = []
                for q in (2 * g, 2 * g + 1):
                    left = block(part, where[k, h, 2 * q])
                    right = block(part, where[k, h, 2 * q + 1])
                    if h == 0:
                        right = pltpu.roll(right, bs, 1)
                    else:
                        left = pltpu.roll(left, bs, 1)
                    tiles.append(jnp.where(low, left, right))
                rows.append(jnp.concatenate(tiles, axis=-1))
        sums = jnp.dot(left_side, jnp.concatenate(rows, axis=0), preferred_element_type=jnp.float32)
        for t in range(2):
            piece = sums[:, t * 2 * bs : (t + 1) * 2 * bs]
            if first:
                total[g, t] = piece
            else:
                total[g, t] += piece
        return carry

    lax.fori_loop(0, groups, body, 0, unroll=min(groups, 4))


def split(a_ref, sources, parts):
    return [a_ref.at[place, p] for place in [source() for source in sources] for p in range(a_ref.shape[1])], parts


def first_kernel(sources, a_ref, *refs):
    *parts, total, feet, where, sem = refs
    add_products(*split(a_ref, sources, parts), total, True, feet, where, sem)


def middle_kernel(sources, a_ref, before, *refs):
    *parts, total, feet, where, sem = refs
    add_products(*split(a_ref, sources, parts), total, False, feet, where, sem)


def last_kernel(sources, a_ref, total, cols_hbm, *refs):
    *parts, o_hbm, feet, where, sem, cols_ref, o_ref, cols_sem, sems = refs
    fetch = pltpu.make_async_copy(cols_hbm, cols_ref, cols_sem)
    fetch.start()
    add_products(*split(a_ref, sources, parts), total, False, feet, where, sem)
    fetch.wait()
    rows, slots, bs, _ = o_ref.shape
    half = total.shape[0] * 4
    copies = [pltpu.make_async_copy(o_ref.at[i], o_hbm.at[i], sems.at[i]) for i in range(rows)]
    for i in range(rows):
        for k in range(slots):
            l = lax.rem(cols_ref[i, k], half)
            tile = total[l // 4, (l // 2) % 2, i * bs : (i + 1) * bs, :].astype(o_ref.dtype)
            tile = jnp.where(l % 2 == 0, tile, pltpu.roll(tile, bs, 1))
            o_ref[i, k] = tile[:, :bs]
        copies[i].start()
    for copy in copies:
        copy.wait()


def product(order, arrived, a, total, out, cols=None):
    hbm, vmem = pl.BlockSpec(memory_space=pl.ANY), pl.BlockSpec(memory_space=VMEM)
    kernel = first_kernel if total is None else middle_kernel if cols is None else last_kernel
    sources = [functools.partial(arrived_from, order, way, steps) for way, steps, _ in arrived]
    parts = [ref for _, _, refs in arrived for ref in refs]
    feet = (len(arrived) * a.shape[1], FOOT, parts[0].shape[1])
    scratch = [VMEM(feet, jnp.int32), SMEM(feet, jnp.int32), pltpu.SemaphoreType.DMA]
    arrays, specs = [a], [vmem]
    if total is not None:
        arrays, specs = arrays + [total], specs + [vmem]
    if cols is not None:
        arrays, specs = arrays + [cols], specs + [hbm]
        scratch += [
            SMEM(cols.shape, cols.dtype),
            VMEM(out.shape, out.dtype),
            pltpu.SemaphoreType.DMA,
            pltpu.SemaphoreType.DMA(out.shape[:1]),
        ]
    return pl.pallas_call(
        functools.partial(kernel, sources),
        out_shape=out,
        in_specs=specs + [vmem] * len(parts),
        out_specs=vmem if cols is None else hbm,
        scratch_shapes=scratch,
        input_output_aliases={1: 0} if total is not None and cols is None else {},
        compiler_params=params(),
        cost_estimate=cost(2 * len(arrived) * a.shape[2] * math.prod(out.shape), 0),
    )(*arrays, *parts)


def local(order, a_vals, b_vals, cols):
    sources = len(order)
    rows, slots, bs, _ = a_vals.shape
    half = sources * rows // 2
    hops = {1: sources // 2, -1: (sources - 1) // 2}

    def ring(way):
        return [
            (order[r] * 2 + c, order[(r + (way if c == 0 else -way)) % sources] * 2 + c)
            for r in range(sources)
            for c in range(2)
        ]

    parts = pack(half, cols, b_vals)
    _, *mine = lax.optimization_barrier((parts[0], a_vals, cols))
    swap = [(0, 1), (1, 0)]
    a_other, others = (lax.ppermute(x, "col", swap) for x in mine)
    a = dense_rows(sources, cols, others, a_vals, a_other)
    total_shape = jax.ShapeDtypeStruct((half // 4, 2, rows * bs, 2 * bs), jnp.float32)
    total = None
    held = {way: parts for way in hops}
    rounds = [[(1, 0, parts)]]
    for step in range(1, hops[1] + 1):
        ways = [way for way in hops if step <= hops[way]]
        for way in ways:
            sent = list(held[way])
            if (step, way) == (2, -1):
                sent = [lax.optimization_barrier((part, a))[0] for part in sent]
            elif (step, way) == (3, 1):
                total = product(order, rounds.pop(0), a, total, total_shape)
                sent[0], total = lax.optimization_barrier((sent[0], total))
            elif step > 2 and way == -1:
                total = product(order, rounds.pop(0), a, total, total_shape)
                for k, part in enumerate(sent):
                    sent[k], total = lax.optimization_barrier((part, total))
            held[way] = [lax.ppermute(part, ("row", "col"), ring(way)) for part in sent]
        rounds.append([(way, step, held[way]) for way in ways])
    *_, late, last = rounds
    for some in [*rounds[:-2], late[:1]]:
        total = product(order, some, a, total, total_shape)
    out = jax.ShapeDtypeStruct(a_vals.shape, a_vals.dtype)
    return product(order, late[1:] + last, a, total, out, cols)


def ring_order(mesh):
    count = mesh.shape["row"]
    coords = [getattr(d, "coords", None) for d in mesh.devices[0, :, 0]]
    loop = [*range(0, count, 2), *range(count - 1 - count % 2, 0, -2)]
    if None not in coords:
        steps = [
            sum(abs(x - y) for x, y in zip(coords[loop[k - 1]], coords[loop[k]]))
            for k in range(count)
        ]
        if max(steps) <= 1:
            return loop
    return list(range(count))


def solution(mesh):
    return jax.shard_map(
        functools.partial(local, ring_order(mesh)),
        mesh=mesh,
        in_specs=(
            P(("groups", "row"), "col", None, None),
            P(("groups", "row"), "col", None, None),
            P(("groups", "row"), "col"),
        ),
        out_specs=P(("groups", "row"), "col", None, None),
        check_vma=False,
    )
```

```python
import functools
import math

import jax
import jax.numpy as jnp
import numpy as np
from jax import lax
from jax.experimental import pallas as pl
from jax.experimental.pallas import tpu as pltpu
from jax.sharding import PartitionSpec as P

VMEM = pltpu.VMEM
SMEM = pltpu.SMEM
LIMIT = 48 * 1024 * 1024
WHOLE = 63 * 1024 * 1024
STRIDE = 5
FOOT = 16


def params(limit=LIMIT):
    return pltpu.CompilerParams(vmem_limit_bytes=limit)


def cost(flops, size):
    return pl.CostEstimate(flops=flops, bytes_accessed=size, transcendentals=0)


def pack_kernel(half, cols_hbm, b_hbm, *refs):
    pairs = b_hbm.shape[0] // 2
    o_hbms, refs = refs[:pairs], refs[pairs:]
    o_refs, (cols_ref, b_ref, sem, sems, o_sems) = refs[:pairs], refs[pairs:]
    rows, slots, bs, _ = b_ref.shape
    copies = [pltpu.make_async_copy(b_hbm.at[r], b_ref.at[r], sems.at[r]) for r in range(rows)]
    fetch = pltpu.make_async_copy(cols_hbm, cols_ref, sem)
    fetch.start()
    for copy in copies:
        copy.start()
    row = lax.broadcasted_iota(jnp.int32, (FOOT, 2 * bs), 0)
    lane = lax.broadcasted_iota(jnp.int32, (FOOT, 2 * bs), 1)
    fetch.wait()
    foot = jnp.full((FOOT, 2 * bs), slots, jnp.int32)
    for r in range(rows):
        for n in range(slots):
            here = (row == r) & (lane == lax.rem(cols_ref[r, n], half))
            foot = jnp.where(here, n, foot)
    o_refs[0][slots * bs :, :] = foot.astype(jnp.float32).astype(b_ref.dtype)
    writes = [pltpu.make_async_copy(o_refs[p], o_hbms[p], o_sems.at[p]) for p in range(pairs)]
    for p in range(pairs):
        copies[2 * p].wait()
        copies[2 * p + 1].wait()
        for n in range(slots):
            o_refs[p][n * bs : (n + 1) * bs, :] = jnp.concatenate([b_ref[2 * p, n], b_ref[2 * p + 1, n]], axis=-1)
        writes[p].start()
    for write in writes:
        write.wait()


def pack(half, cols, b_vals):
    rows, slots, bs, _ = b_vals.shape
    shapes = [(slots * bs + (FOOT if p == 0 else 0), 2 * bs) for p in range(rows // 2)]
    return pl.pallas_call(
        functools.partial(pack_kernel, half),
        out_shape=[jax.ShapeDtypeStruct(shape, b_vals.dtype) for shape in shapes],
        in_specs=[pl.BlockSpec(memory_space=pl.ANY)] * 2,
        out_specs=[pl.BlockSpec(memory_space=pl.ANY)] * len(shapes),
        scratch_shapes=[
            *(VMEM(shape, b_vals.dtype) for shape in shapes),
            SMEM(cols.shape, cols.dtype),
            VMEM(b_vals.shape, b_vals.dtype),
            pltpu.SemaphoreType.DMA,
            pltpu.SemaphoreType.DMA((rows,)),
            pltpu.SemaphoreType.DMA((len(shapes),)),
        ],
        compiler_params=params(WHOLE),
        cost_estimate=cost(0, 2 * b_vals.size * 2),
    )(cols, b_vals)


def dense_kernel(cols_ref, others_ref, own_ref, other_ref, o_ref, blocks, where):
    rows, slots, bs, _ = own_ref.shape
    sources, pairs = o_ref.shape[:2]
    blocks[:, :slots] = own_ref[...]
    blocks[:, slots : 2 * slots] = other_ref[...]
    blocks[:, 2 * slots] = jnp.zeros_like(blocks[:, 2 * slots])
    for i in range(rows):
        def clear(j, carry):
            where[i, j] = 2 * slots
            return carry

        lax.fori_loop(0, 2 * sources * pairs, clear, 0, unroll=8)
        for m in range(slots):
            where[i, cols_ref[i, m]] = m
            where[i, others_ref[i, m]] = slots + m

    def body(s, carry):
        for p in range(pairs):
            j = (s * pairs + p) * 2
            for i in range(rows):
                left = blocks[i, where[i, j]]
                right = blocks[i, where[i, j + 1]]
                o_ref[s, p, i * bs : (i + 1) * bs, :] = jnp.concatenate([left, right], axis=-1)
        return carry

    lax.fori_loop(0, sources, body, 0, unroll=2)


def dense_rows(sources, cols, others, own, other):
    rows, slots, bs, _ = own.shape
    return pl.pallas_call(
        dense_kernel,
        out_shape=jax.ShapeDtypeStruct((sources, rows // 2, rows * bs, 2 * bs), own.dtype),
        grid_spec=pltpu.PrefetchScalarGridSpec(
            num_scalar_prefetch=2,
            grid=(),
            in_specs=[pl.BlockSpec(memory_space=VMEM)] * 2,
            out_specs=pl.BlockSpec(memory_space=VMEM),
            scratch_shapes=[
                VMEM((rows, 2 * slots + 1, bs, bs), own.dtype),
                SMEM((rows, sources * rows), jnp.int32),
            ],
        ),
        compiler_params=params(),
        cost_estimate=cost(0, 8 * own.size),
    )(cols, others, own, other)


def look_up(table, k):
    value = jnp.int32(table[0])
    for n, entry in enumerate(table[1:], 1):
        value = jnp.where(k == n, entry, value)
    return value


def arrived_from(order, way, steps):
    spots = [order.index(r) for r in range(len(order))]
    ahead = jnp.where(lax.axis_index("col") == 0, way, -way) * steps
    return look_up(order, lax.rem(look_up(spots, lax.axis_index("row")) - ahead + len(order), len(order)))


def add_products(panels, parts, total, first, feet, where, sem):
    groups, bs = total.shape[0], total.shape[3] // 2
    pairs = len(parts) // feet.shape[0]
    slots = (parts[0].shape[0] - FOOT) // bs
    for k in range(feet.shape[0]):
        feet[k] = parts[k * pairs][slots * bs :, :].astype(jnp.float32).astype(jnp.int32)
    copy = pltpu.make_async_copy(feet, where, sem)
    copy.start()
    copy.wait()
    low = lax.broadcasted_iota(jnp.int32, (bs, 2 * bs), 1) < bs
    left_side = jnp.concatenate([panel[...] for panel in panels], axis=-1)

    def block(part, slot):
        at = pl.multiple_of(jnp.minimum(slot, slots - 1) * bs, bs)
        return jnp.where(slot < slots, part[pl.ds(at, bs), :], jnp.zeros((bs, 2 * bs), part.dtype))

    def body(g, carry):
        rows = []
        for k, part in enumerate(parts):
            for h in range(2):
                tiles = []
                for q in (2 * g, 2 * g + 1):
                    left = block(part, where[k // pairs, k % pairs * 2 + h, 2 * q])
                    right = block(part, where[k // pairs, k % pairs * 2 + h, 2 * q + 1])
                    if h == 0:
                        right = pltpu.roll(right, bs, 1)
                    else:
                        left = pltpu.roll(left, bs, 1)
                    tiles.append(jnp.where(low, left, right))
                rows.append(jnp.concatenate(tiles, axis=-1))
        sums = jnp.dot(left_side, jnp.concatenate(rows, axis=0), preferred_element_type=jnp.float32)
        for t in range(2):
            piece = sums[:, t * 2 * bs : (t + 1) * 2 * bs]
            if first:
                total[g, t] = piece
            else:
                total[g, t] += piece
        return carry

    lax.fori_loop(0, groups, body, 0, unroll=min(groups, 4))


def split(a_ref, sources, parts):
    return [a_ref.at[place, p] for place in [source() for source in sources] for p in range(a_ref.shape[1])], parts


def first_kernel(sources, a_ref, *refs):
    *parts, total, feet, where, sem = refs
    add_products(*split(a_ref, sources, parts), total, True, feet, where, sem)


def middle_kernel(sources, a_ref, before, *refs):
    *parts, total, feet, where, sem = refs
    add_products(*split(a_ref, sources, parts), total, False, feet, where, sem)


def last_kernel(sources, a_ref, total, cols_hbm, *refs):
    *parts, o_hbm, feet, where, sem, cols_ref, o_ref, cols_sem, sems = refs
    fetch = pltpu.make_async_copy(cols_hbm, cols_ref, cols_sem)
    fetch.start()
    add_products(*split(a_ref, sources, parts), total, False, feet, where, sem)
    fetch.wait()
    rows, slots, bs, _ = o_ref.shape
    half = total.shape[0] * 4
    copies = []
    for i in range(rows):
        for k in range(slots):
            l = lax.rem(cols_ref[i, k], half)
            tile = total[l // 4, (l // 2) % 2, i * bs : (i + 1) * bs, :].astype(o_ref.dtype)
            tile = jnp.where(l % 2 == 0, tile, pltpu.roll(tile, bs, 1))
            o_ref[i, k] = tile[:, :bs]
            if k % STRIDE == STRIDE - 1 or k == slots - 1:
                some = pl.ds(k // STRIDE * STRIDE, k % STRIDE + 1)
                copies.append(pltpu.make_async_copy(o_ref.at[i, some], o_hbm.at[i, some], sems.at[i, k // STRIDE]))
                copies[-1].start()
    for copy in copies:
        copy.wait()


def product(order, arrived, a, total, out, cols=None):
    hbm, vmem = pl.BlockSpec(memory_space=pl.ANY), pl.BlockSpec(memory_space=VMEM)
    kernel = first_kernel if total is None else middle_kernel if cols is None else last_kernel
    sources = [functools.partial(arrived_from, order, way, steps) for way, steps, _ in arrived]
    parts = [ref for _, _, refs in arrived for ref in refs]
    feet = (len(arrived), FOOT, parts[0].shape[1])
    scratch = [VMEM(feet, jnp.int32), SMEM(feet, jnp.int32), pltpu.SemaphoreType.DMA]
    arrays, specs = [a], [vmem]
    if total is not None:
        arrays, specs = arrays + [total], specs + [vmem]
    if cols is not None:
        arrays, specs = arrays + [cols], specs + [hbm]
        scratch += [
            SMEM(cols.shape, cols.dtype),
            VMEM(out.shape, out.dtype),
            pltpu.SemaphoreType.DMA,
            pltpu.SemaphoreType.DMA((out.shape[0], -(-out.shape[1] // STRIDE))),
        ]
    return pl.pallas_call(
        functools.partial(kernel, sources),
        out_shape=out,
        in_specs=specs + [vmem] * len(parts),
        out_specs=vmem if cols is None else hbm,
        scratch_shapes=scratch,
        input_output_aliases={1: 0} if total is not None and cols is None else {},
        compiler_params=params(),
        cost_estimate=cost(2 * len(arrived) * a.shape[2] * math.prod(out.shape), 0),
    )(*arrays, *parts)


def local(order, a_vals, b_vals, cols):
    sources = len(order)
    rows, slots, bs, _ = a_vals.shape
    half = sources * rows // 2
    hops = {1: sources // 2, -1: (sources - 1) // 2}

    def ring(way):
        return [
            (order[r] * 2 + c, order[(r + (way if c == 0 else -way)) % sources] * 2 + c)
            for r in range(sources)
            for c in range(2)
        ]

    parts = pack(half, cols, b_vals)
    _, *mine = lax.optimization_barrier((parts[0], a_vals, cols))
    swap = [(0, 1), (1, 0)]
    a_other, others = (lax.ppermute(x, "col", swap) for x in mine)
    a = dense_rows(sources, cols, others, a_vals, a_other)
    total_shape = jax.ShapeDtypeStruct((half // 4, 2, rows * bs, 2 * bs), jnp.float32)
    total = None
    held = {way: parts for way in hops}
    rounds = [[(1, 0, parts)]]
    for step in range(1, hops[1] + 1):
        ways = [way for way in hops if step <= hops[way]]
        for way in ways:
            sent = list(held[way])
            if step == 3:
                sent = [lax.optimization_barrier((part, a))[0] for part in sent]
            if (step, way) == (3, -1):
                total = product(order, rounds.pop(0), a, total, total_shape)
                sent[0], total = lax.optimization_barrier((sent[0], total))
            elif step > 3 and way == 1:
                total = product(order, rounds.pop(0), a, total, total_shape)
                sent[-1], total = lax.optimization_barrier((sent[-1], total))
            held[way] = [lax.ppermute(part, ("row", "col"), ring(way)) for part in sent]
        rounds.append([(way, step, held[way]) for way in ways])
    *_, late, last = rounds
    for some in [*rounds[:-2], late[:1]]:
        total = product(order, some, a, total, total_shape)
    out = jax.ShapeDtypeStruct(a_vals.shape, a_vals.dtype)
    return product(order, late[1:] + last, a, total, out, cols)


def ring_order(mesh):
    count = mesh.shape["row"]
    coords = [getattr(d, "coords", None) for d in mesh.devices[0, :, 0]]
    loop = [*range(0, count, 2), *range(count - 1 - count % 2, 0, -2)]
    if None not in coords:
        steps = [
            sum(abs(x - y) for x, y in zip(coords[loop[k - 1]], coords[loop[k]]))
            for k in range(count)
        ]
        if max(steps) <= 1:
            return loop
    return list(range(count))


def solution(mesh):
    return jax.shard_map(
        functools.partial(local, ring_order(mesh)),
        mesh=mesh,
        in_specs=(
            P(("groups", "row"), "col", None, None),
            P(("groups", "row"), "col", None, None),
            P(("groups", "row"), "col"),
        ),
        out_specs=P(("groups", "row"), "col", None, None),
        check_vma=False,
    )
```

```python
import functools
import math

import jax
import jax.numpy as jnp
import numpy as np
from jax import lax
from jax.experimental import pallas as pl
from jax.experimental.pallas import tpu as pltpu
from jax.sharding import PartitionSpec as P

VMEM = pltpu.VMEM
SMEM = pltpu.SMEM
LIMIT = 48 * 1024 * 1024
WHOLE = 63 * 1024 * 1024
STRIDE = 5
FOOT = 16


def params(limit=LIMIT):
    return pltpu.CompilerParams(vmem_limit_bytes=limit)


def within(col, half):
    return jnp.where(col >= half, col - half, col)


def cost(flops, size):
    return pl.CostEstimate(flops=flops, bytes_accessed=size, transcendentals=0)


def pack_kernel(half, cols_hbm, b_hbm, *refs):
    pairs = b_hbm.shape[0] // 2
    o_hbms, refs = refs[:pairs], refs[pairs:]
    o_refs, (cols_ref, b_ref, sem, sems, o_sems) = refs[:pairs], refs[pairs:]
    rows, slots, bs, _ = b_ref.shape
    copies = [pltpu.make_async_copy(b_hbm.at[r], b_ref.at[r], sems.at[r]) for r in range(rows)]
    fetch = pltpu.make_async_copy(cols_hbm, cols_ref, sem)
    fetch.start()
    for copy in copies:
        copy.start()
    row = lax.broadcasted_iota(jnp.int32, (FOOT, 2 * bs), 0)
    lane = lax.broadcasted_iota(jnp.int32, (FOOT, 2 * bs), 1)
    fetch.wait()
    foot = jnp.full((FOOT, 2 * bs), slots, jnp.int32)
    for r in range(rows):
        for n in range(slots):
            here = (row == r) & (lane == within(cols_ref[r, n], half))
            foot = jnp.where(here, n, foot)
    o_refs[0][slots * bs :, :] = foot.astype(jnp.float32).astype(b_ref.dtype)
    writes = [pltpu.make_async_copy(o_refs[p], o_hbms[p], o_sems.at[p]) for p in range(pairs)]
    for p in range(pairs):
        copies[2 * p].wait()
        copies[2 * p + 1].wait()
        for n in range(slots):
            o_refs[p][n * bs : (n + 1) * bs, :] = jnp.concatenate([b_ref[2 * p, n], b_ref[2 * p + 1, n]], axis=-1)
        writes[p].start()
    for write in writes:
        write.wait()


def pack(half, cols, b_vals):
    rows, slots, bs, _ = b_vals.shape
    shapes = [(slots * bs + (FOOT if p == 0 else 0), 2 * bs) for p in range(rows // 2)]
    return pl.pallas_call(
        functools.partial(pack_kernel, half),
        out_shape=[jax.ShapeDtypeStruct(shape, b_vals.dtype) for shape in shapes],
        in_specs=[pl.BlockSpec(memory_space=pl.ANY)] * 2,
        out_specs=[pl.BlockSpec(memory_space=pl.ANY)] * len(shapes),
        scratch_shapes=[
            *(VMEM(shape, b_vals.dtype) for shape in shapes),
            SMEM(cols.shape, cols.dtype),
            VMEM(b_vals.shape, b_vals.dtype),
            pltpu.SemaphoreType.DMA,
            pltpu.SemaphoreType.DMA((rows,)),
            pltpu.SemaphoreType.DMA((len(shapes),)),
        ],
        compiler_params=params(WHOLE),
        cost_estimate=cost(0, 2 * b_vals.size * 2),
    )(cols, b_vals)


def dense_kernel(cols_ref, others_ref, own_ref, other_ref, o_ref, blocks, where):
    rows, slots, bs, _ = own_ref.shape
    sources, pairs = o_ref.shape[:2]
    blocks[:, :slots] = own_ref[...]
    blocks[:, slots : 2 * slots] = other_ref[...]
    blocks[:, 2 * slots] = jnp.zeros_like(blocks[:, 2 * slots])
    for i in range(rows):
        def clear(j, carry):
            where[i, j] = 2 * slots
            return carry

        lax.fori_loop(0, 2 * sources * pairs, clear, 0, unroll=8)
        for m in range(slots):
            where[i, cols_ref[i, m]] = m
            where[i, others_ref[i, m]] = slots + m

    def body(s, carry):
        for p in range(pairs):
            j = (s * pairs + p) * 2
            for i in range(rows):
                left = blocks[i, where[i, j]]
                right = blocks[i, where[i, j + 1]]
                o_ref[s, p, i * bs : (i + 1) * bs, :] = jnp.concatenate([left, right], axis=-1)
        return carry

    lax.fori_loop(0, sources, body, 0, unroll=2)


def dense_rows(sources, cols, others, own, other):
    rows, slots, bs, _ = own.shape
    return pl.pallas_call(
        dense_kernel,
        out_shape=jax.ShapeDtypeStruct((sources, rows // 2, rows * bs, 2 * bs), own.dtype),
        grid_spec=pltpu.PrefetchScalarGridSpec(
            num_scalar_prefetch=2,
            grid=(),
            in_specs=[pl.BlockSpec(memory_space=VMEM)] * 2,
            out_specs=pl.BlockSpec(memory_space=VMEM),
            scratch_shapes=[
                VMEM((rows, 2 * slots + 1, bs, bs), own.dtype),
                SMEM((rows, sources * rows), jnp.int32),
            ],
        ),
        compiler_params=params(),
        cost_estimate=cost(0, 8 * own.size),
    )(cols, others, own, other)


def look_up(table, k):
    value = jnp.int32(table[0])
    for n, entry in enumerate(table[1:], 1):
        value = jnp.where(k == n, entry, value)
    return value


def arrived_from(order, way, steps):
    spots = [order.index(r) for r in range(len(order))]
    ahead = jnp.where(lax.axis_index("col") == 0, way, -way) * steps
    return look_up(order, lax.rem(look_up(spots, lax.axis_index("row")) - ahead + len(order), len(order)))


def add_products(panels, parts, total, first, feet, where, sem):
    groups, bs = total.shape[0], total.shape[3] // 2
    pairs = len(parts) // feet.shape[0]
    slots = (parts[0].shape[0] - FOOT) // bs
    for k in range(feet.shape[0]):
        feet[k] = parts[k * pairs][slots * bs :, :].astype(jnp.float32).astype(jnp.int32)
    copy = pltpu.make_async_copy(feet, where, sem)
    copy.start()
    copy.wait()
    low = lax.broadcasted_iota(jnp.int32, (bs, 2 * bs), 1) < bs
    left_side = jnp.concatenate([panel[...] for panel in panels], axis=-1)

    def block(part, slot):
        at = pl.multiple_of(jnp.minimum(slot, slots - 1) * bs, bs)
        return jnp.where(slot < slots, part[pl.ds(at, bs), :], jnp.zeros((bs, 2 * bs), part.dtype))

    def body(g, carry):
        rows = []
        for k, part in enumerate(parts):
            for h in range(2):
                tiles = []
                for q in (2 * g, 2 * g + 1):
                    left = block(part, where[k // pairs, k % pairs * 2 + h, 2 * q])
                    right = block(part, where[k // pairs, k % pairs * 2 + h, 2 * q + 1])
                    if h == 0:
                        right = pltpu.roll(right, bs, 1)
                    else:
                        left = pltpu.roll(left, bs, 1)
                    tiles.append(jnp.where(low, left, right))
                rows.append(jnp.concatenate(tiles, axis=-1))
        sums = jnp.dot(left_side, jnp.concatenate(rows, axis=0), preferred_element_type=jnp.float32)
        for t in range(2):
            piece = sums[:, t * 2 * bs : (t + 1) * 2 * bs]
            if first:
                total[g, t] = piece
            else:
                total[g, t] += piece
        return carry

    lax.fori_loop(0, groups, body, 0, unroll=min(groups, 4))


def split(a_ref, sources, parts):
    return [a_ref.at[place, p] for place in [source() for source in sources] for p in range(a_ref.shape[1])], parts


def first_kernel(sources, a_ref, *refs):
    *parts, total, feet, where, sem = refs
    add_products(*split(a_ref, sources, parts), total, True, feet, where, sem)


def middle_kernel(sources, a_ref, before, *refs):
    *parts, total, feet, where, sem = refs
    add_products(*split(a_ref, sources, parts), total, False, feet, where, sem)


def last_kernel(sources, a_ref, total, cols_hbm, *refs):
    *parts, o_hbm, feet, where, sem, cols_ref, o_ref, cols_sem, sems = refs
    fetch = pltpu.make_async_copy(cols_hbm, cols_ref, cols_sem)
    fetch.start()
    add_products(*split(a_ref, sources, parts), total, False, feet, where, sem)
    fetch.wait()
    rows, slots, bs, _ = o_ref.shape
    half = total.shape[0] * 4
    copies = []
    for i in range(rows):
        for k in range(slots):
            l = within(cols_ref[i, k], half)
            tile = total[l >> 2, (l >> 1) & 1, i * bs : (i + 1) * bs, :].astype(o_ref.dtype)
            tile = jnp.where(l & 1 == 0, tile, pltpu.roll(tile, bs, 1))
            o_ref[i, k] = tile[:, :bs]
            if k % STRIDE == STRIDE - 1 or k == slots - 1:
                some = pl.ds(k // STRIDE * STRIDE, k % STRIDE + 1)
                copies.append(pltpu.make_async_copy(o_ref.at[i, some], o_hbm.at[i, some], sems.at[i, k // STRIDE]))
                copies[-1].start()
    for copy in copies:
        copy.wait()


def product(order, arrived, a, total, out, cols=None):
    hbm, vmem = pl.BlockSpec(memory_space=pl.ANY), pl.BlockSpec(memory_space=VMEM)
    kernel = first_kernel if total is None else middle_kernel if cols is None else last_kernel
    sources = [functools.partial(arrived_from, order, way, steps) for way, steps, _ in arrived]
    parts = [ref for _, _, refs in arrived for ref in refs]
    feet = (len(arrived), FOOT, parts[0].shape[1])
    scratch = [VMEM(feet, jnp.int32), SMEM(feet, jnp.int32), pltpu.SemaphoreType.DMA]
    arrays, specs = [a], [vmem]
    if total is not None:
        arrays, specs = arrays + [total], specs + [vmem]
    if cols is not None:
        arrays, specs = arrays + [cols], specs + [hbm]
        scratch += [
            SMEM(cols.shape, cols.dtype),
            VMEM(out.shape, out.dtype),
            pltpu.SemaphoreType.DMA,
            pltpu.SemaphoreType.DMA((out.shape[0], -(-out.shape[1] // STRIDE))),
        ]
    return pl.pallas_call(
        functools.partial(kernel, sources),
        out_shape=out,
        in_specs=specs + [vmem] * len(parts),
        out_specs=vmem if cols is None else hbm,
        scratch_shapes=scratch,
        input_output_aliases={1: 0} if total is not None and cols is None else {},
        compiler_params=params(),
        cost_estimate=cost(2 * len(arrived) * a.shape[2] * math.prod(out.shape), 0),
    )(*arrays, *parts)


def local(order, a_vals, b_vals, cols):
    sources = len(order)
    rows, slots, bs, _ = a_vals.shape
    half = sources * rows // 2
    hops = {1: sources // 2, -1: (sources - 1) // 2}

    def ring(way):
        return [
            (order[r] * 2 + c, order[(r + (way if c == 0 else -way)) % sources] * 2 + c)
            for r in range(sources)
            for c in range(2)
        ]

    parts = pack(half, cols, b_vals)
    _, *mine = lax.optimization_barrier((parts[0], a_vals, cols))
    swap = [(0, 1), (1, 0)]
    a_other, others = (lax.ppermute(x, "col", swap) for x in mine)
    a = dense_rows(sources, cols, others, a_vals, a_other)
    total_shape = jax.ShapeDtypeStruct((half // 4, 2, rows * bs, 2 * bs), jnp.float32)
    total = None
    held = {way: parts for way in hops}
    rounds = [[(1, 0, parts)]]
    for step in range(1, hops[1] + 1):
        ways = [way for way in hops if step <= hops[way]]
        for way in ways:
            sent = list(held[way])
            if (step, way) == (1, -1):
                sent = [lax.optimization_barrier((part, others))[0] for part in sent]
            if step == 3:
                sent = [lax.optimization_barrier((part, a))[0] for part in sent]
            if step > 2 and way == -1:
                total = product(order, rounds.pop(0), a, total, total_shape)
                sent[0], total = lax.optimization_barrier((sent[0], total))
            held[way] = [lax.ppermute(part, ("row", "col"), ring(way)) for part in sent]
        rounds.append([(way, step, held[way]) for way in ways])
    *_, late, last = rounds
    total = product(order, sum(rounds[:-2], late[:1]), a, total, total_shape)
    out = jax.ShapeDtypeStruct(a_vals.shape, a_vals.dtype)
    return product(order, late[1:] + last, a, total, out, cols)


def ring_order(mesh):
    count = mesh.shape["row"]
    coords = [getattr(d, "coords", None) for d in mesh.devices[0, :, 0]]
    loop = [*range(0, count, 2), *range(count - 1 - count % 2, 0, -2)]
    if None not in coords:
        steps = [
            sum(abs(x - y) for x, y in zip(coords[loop[k - 1]], coords[loop[k]]))
            for k in range(count)
        ]
        if max(steps) <= 1:
            return loop
    return list(range(count))


def solution(mesh):
    return jax.shard_map(
        functools.partial(local, ring_order(mesh)),
        mesh=mesh,
        in_specs=(
            P(("groups", "row"), "col", None, None),
            P(("groups", "row"), "col", None, None),
            P(("groups", "row"), "col"),
        ),
        out_specs=P(("groups", "row"), "col", None, None),
        check_vma=False,
    )
```

```python
import functools
import math

import jax
import jax.numpy as jnp
import numpy as np
from jax import lax
from jax.experimental import pallas as pl
from jax.experimental.pallas import tpu as pltpu
from jax.sharding import PartitionSpec as P

VMEM = pltpu.VMEM
SMEM = pltpu.SMEM
LIMIT = 48 * 1024 * 1024
STRIDE = 5
FOOT = 16


def params():
    return pltpu.CompilerParams(vmem_limit_bytes=LIMIT)


def within(col, half):
    return jnp.where(col >= half, col - half, col)


def cost(flops, size):
    return pl.CostEstimate(flops=flops, bytes_accessed=size, transcendentals=0)


def pack_kernel(half, cols_hbm, b_hbm, *refs):
    *o_refs, cols_ref, b_ref, sem, sems = refs
    rows, slots, bs, _ = b_ref.shape
    copies = [pltpu.make_async_copy(b_hbm.at[r], b_ref.at[r], sems.at[r]) for r in range(rows)]
    fetch = pltpu.make_async_copy(cols_hbm, cols_ref, sem)
    fetch.start()
    for copy in copies:
        copy.start()
    row = lax.broadcasted_iota(jnp.int32, (FOOT, 2 * bs), 0)
    lane = lax.broadcasted_iota(jnp.int32, (FOOT, 2 * bs), 1)
    fetch.wait()
    foot = jnp.full((FOOT, 2 * bs), slots, jnp.int32)
    for r in range(rows):
        for n in range(slots):
            here = (row == r) & (lane == within(cols_ref[r, n], half))
            foot = jnp.where(here, n, foot)
    o_refs[0][slots * bs :, :] = foot.astype(jnp.float32).astype(b_ref.dtype)
    for p, o_ref in enumerate(o_refs):
        copies[2 * p].wait()
        copies[2 * p + 1].wait()
        for n in range(slots):
            o_ref[n * bs : (n + 1) * bs, :] = jnp.concatenate([b_ref[2 * p, n], b_ref[2 * p + 1, n]], axis=-1)


def pack(half, cols, b_vals):
    rows, slots, bs, _ = b_vals.shape
    shapes = [(slots * bs + (FOOT if p == 0 else 0), 2 * bs) for p in range(rows // 2)]
    cols, b_vals = (pltpu.with_memory_space_constraint(x, pltpu.HBM) for x in (cols, b_vals))
    return pl.pallas_call(
        functools.partial(pack_kernel, half),
        out_shape=[jax.ShapeDtypeStruct(shape, b_vals.dtype) for shape in shapes],
        in_specs=[pl.BlockSpec(memory_space=pl.ANY)] * 2,
        out_specs=[pl.BlockSpec(memory_space=VMEM)] * len(shapes),
        scratch_shapes=[
            SMEM(cols.shape, cols.dtype),
            VMEM(b_vals.shape, b_vals.dtype),
            pltpu.SemaphoreType.DMA,
            pltpu.SemaphoreType.DMA((rows,)),
        ],
        compiler_params=params(),
        cost_estimate=cost(0, 2 * b_vals.size * 2),
    )(cols, b_vals)


def dense_kernel(cols_ref, others_ref, own_ref, other_ref, o_ref, blocks, where):
    rows, slots, bs, _ = own_ref.shape
    sources, pairs = o_ref.shape[:2]
    blocks[:, :slots] = own_ref[...]
    blocks[:, slots : 2 * slots] = other_ref[...]
    blocks[:, 2 * slots] = jnp.zeros_like(blocks[:, 2 * slots])
    for i in range(rows):
        def clear(j, carry):
            where[i, j] = 2 * slots
            return carry

        lax.fori_loop(0, 2 * sources * pairs, clear, 0, unroll=8)
        for m in range(slots):
            where[i, cols_ref[i, m]] = m
            where[i, others_ref[i, m]] = slots + m

    def body(s, carry):
        for p in range(pairs):
            j = (s * pairs + p) * 2
            for i in range(rows):
                left = blocks[i, where[i, j]]
                right = blocks[i, where[i, j + 1]]
                o_ref[s, p, i * bs : (i + 1) * bs, :] = jnp.concatenate([left, right], axis=-1)
        return carry

    lax.fori_loop(0, sources, body, 0, unroll=2)


def dense_rows(sources, cols, others, own, other):
    rows, slots, bs, _ = own.shape
    return pl.pallas_call(
        dense_kernel,
        out_shape=jax.ShapeDtypeStruct((sources, rows // 2, rows * bs, 2 * bs), own.dtype),
        grid_spec=pltpu.PrefetchScalarGridSpec(
            num_scalar_prefetch=2,
            grid=(),
            in_specs=[pl.BlockSpec(memory_space=VMEM)] * 2,
            out_specs=pl.BlockSpec(memory_space=VMEM),
            scratch_shapes=[
                VMEM((rows, 2 * slots + 1, bs, bs), own.dtype),
                SMEM((rows, sources * rows), jnp.int32),
            ],
        ),
        compiler_params=params(),
        cost_estimate=cost(0, 8 * own.size),
    )(cols, others, own, other)


def look_up(table, k):
    value = jnp.int32(table[0])
    for n, entry in enumerate(table[1:], 1):
        value = jnp.where(k == n, entry, value)
    return value


def arrived_from(order, way, steps):
    spots = [order.index(r) for r in range(len(order))]
    ahead = jnp.where(lax.axis_index("col") == 0, way, -way) * steps
    return look_up(order, lax.rem(look_up(spots, lax.axis_index("row")) - ahead + len(order), len(order)))


def add_products(panels, parts, total, first, feet, where, sem):
    groups, bs = total.shape[0], total.shape[3] // 2
    pairs = len(parts) // feet.shape[0]
    slots = (parts[0].shape[0] - FOOT) // bs
    for k in range(feet.shape[0]):
        feet[k] = parts[k * pairs][slots * bs :, :].astype(jnp.float32).astype(jnp.int32)
    copy = pltpu.make_async_copy(feet, where, sem)
    copy.start()
    copy.wait()
    low = lax.broadcasted_iota(jnp.int32, (bs, 2 * bs), 1) < bs
    left_side = jnp.concatenate([panel[...] for panel in panels], axis=-1)

    def block(part, slot):
        at = pl.multiple_of(jnp.minimum(slot, slots - 1) * bs, bs)
        return jnp.where(slot < slots, part[pl.ds(at, bs), :], jnp.zeros((bs, 2 * bs), part.dtype))

    def body(g, carry):
        rows = []
        for k, part in enumerate(parts):
            for h in range(2):
                tiles = []
                for q in (2 * g, 2 * g + 1):
                    left = block(part, where[k // pairs, k % pairs * 2 + h, 2 * q])
                    right = block(part, where[k // pairs, k % pairs * 2 + h, 2 * q + 1])
                    if h == 0:
                        right = pltpu.roll(right, bs, 1)
                    else:
                        left = pltpu.roll(left, bs, 1)
                    tiles.append(jnp.where(low, left, right))
                rows.append(jnp.concatenate(tiles, axis=-1))
        sums = jnp.dot(left_side, jnp.concatenate(rows, axis=0), preferred_element_type=jnp.float32)
        for t in range(2):
            piece = sums[:, t * 2 * bs : (t + 1) * 2 * bs]
            if first:
                total[g, t] = piece
            else:
                total[g, t] += piece
        return carry

    lax.fori_loop(0, groups, body, 0, unroll=min(groups, 4))


def split(a_ref, sources, parts):
    return [a_ref.at[place, p] for place in [source() for source in sources] for p in range(a_ref.shape[1])], parts


def first_kernel(sources, a_ref, *refs):
    *parts, total, feet, where, sem = refs
    add_products(*split(a_ref, sources, parts), total, True, feet, where, sem)


def middle_kernel(sources, a_ref, before, *refs):
    *parts, total, feet, where, sem = refs
    add_products(*split(a_ref, sources, parts), total, False, feet, where, sem)


def last_kernel(sources, a_ref, total, cols_hbm, *refs):
    *parts, o_hbm, feet, where, sem, cols_ref, o_ref, cols_sem, sems = refs
    fetch = pltpu.make_async_copy(cols_hbm, cols_ref, cols_sem)
    fetch.start()
    add_products(*split(a_ref, sources, parts), total, False, feet, where, sem)
    fetch.wait()
    rows, slots, bs, _ = o_ref.shape
    half = total.shape[0] * 4
    copies = []
    for i in range(rows):
        for k in range(slots):
            l = within(cols_ref[i, k], half)
            tile = total[l >> 2, (l >> 1) & 1, i * bs : (i + 1) * bs, :].astype(o_ref.dtype)
            tile = jnp.where(l & 1 == 0, tile, pltpu.roll(tile, bs, 1))
            o_ref[i, k] = tile[:, :bs]
            if k % STRIDE == STRIDE - 1 or k == slots - 1:
                some = pl.ds(k // STRIDE * STRIDE, k % STRIDE + 1)
                copies.append(pltpu.make_async_copy(o_ref.at[i, some], o_hbm.at[i, some], sems.at[i, k // STRIDE]))
                copies[-1].start()
    for copy in copies:
        copy.wait()


def product(order, arrived, a, total, out, cols=None):
    hbm, vmem = pl.BlockSpec(memory_space=pl.ANY), pl.BlockSpec(memory_space=VMEM)
    kernel = first_kernel if total is None else middle_kernel if cols is None else last_kernel
    sources = [functools.partial(arrived_from, order, way, steps) for way, steps, _ in arrived]
    parts = [ref for _, _, refs in arrived for ref in refs]
    feet = (len(arrived), FOOT, parts[0].shape[1])
    scratch = [VMEM(feet, jnp.int32), SMEM(feet, jnp.int32), pltpu.SemaphoreType.DMA]
    arrays, specs = [a], [vmem]
    if total is not None:
        arrays, specs = arrays + [total], specs + [vmem]
    if cols is not None:
        arrays, specs = arrays + [cols], specs + [hbm]
        scratch += [
            SMEM(cols.shape, cols.dtype),
            VMEM(out.shape, out.dtype),
            pltpu.SemaphoreType.DMA,
            pltpu.SemaphoreType.DMA((out.shape[0], -(-out.shape[1] // STRIDE))),
        ]
    return pl.pallas_call(
        functools.partial(kernel, sources),
        out_shape=out,
        in_specs=specs + [vmem] * len(parts),
        out_specs=vmem if cols is None else hbm,
        scratch_shapes=scratch,
        input_output_aliases={1: 0} if total is not None and cols is None else {},
        compiler_params=params(),
        cost_estimate=cost(2 * len(arrived) * a.shape[2] * math.prod(out.shape), 0),
    )(*arrays, *parts)


def local(order, a_vals, b_vals, cols):
    sources = len(order)
    rows, slots, bs, _ = a_vals.shape
    half = sources * rows // 2
    hops = {1: sources // 2, -1: (sources - 1) // 2}

    def ring(way):
        return [
            (order[r] * 2 + c, order[(r + (way if c == 0 else -way)) % sources] * 2 + c)
            for r in range(sources)
            for c in range(2)
        ]

    parts = pack(half, cols, b_vals)
    _, *mine = lax.optimization_barrier((parts[0], a_vals, cols))
    swap = [(0, 1), (1, 0)]
    a_other, others = (lax.ppermute(x, "col", swap) for x in mine)
    a = dense_rows(sources, cols, others, a_vals, a_other)
    total_shape = jax.ShapeDtypeStruct((half // 4, 2, rows * bs, 2 * bs), jnp.float32)
    total = None
    held = {way: parts for way in hops}
    rounds = [[(1, 0, parts)]]
    for step in range(1, hops[1] + 1):
        ways = [way for way in hops if step <= hops[way]]
        for way in ways:
            sent = list(held[way])
            if (step, way) == (1, -1):
                sent = [lax.optimization_barrier((part, others))[0] for part in sent]
            if step == 3:
                sent = [lax.optimization_barrier((part, a))[0] for part in sent]
            if step > 2 and way == -1:
                total = product(order, rounds.pop(0), a, total, total_shape)
                sent[0], total = lax.optimization_barrier((sent[0], total))
            held[way] = [lax.ppermute(part, ("row", "col"), ring(way)) for part in sent]
        rounds.append([(way, step, held[way]) for way in ways])
    *_, late, last = rounds
    total = product(order, sum(rounds[:-2], late[:1]), a, total, total_shape)
    out = jax.ShapeDtypeStruct(a_vals.shape, a_vals.dtype)
    return product(order, late[1:] + last, a, total, out, cols)


def ring_order(mesh):
    count = mesh.shape["row"]
    coords = [getattr(d, "coords", None) for d in mesh.devices[0, :, 0]]
    loop = [*range(0, count, 2), *range(count - 1 - count % 2, 0, -2)]
    if None not in coords:
        steps = [
            sum(abs(x - y) for x, y in zip(coords[loop[k - 1]], coords[loop[k]]))
            for k in range(count)
        ]
        if max(steps) <= 1:
            return loop
    return list(range(count))


def solution(mesh):
    return jax.shard_map(
        functools.partial(local, ring_order(mesh)),
        mesh=mesh,
        in_specs=(
            P(("groups", "row"), "col", None, None),
            P(("groups", "row"), "col", None, None),
            P(("groups", "row"), "col"),
        ),
        out_specs=P(("groups", "row"), "col", None, None),
        check_vma=False,
    )
```

```python
import functools
import math

import jax
import jax.numpy as jnp
import numpy as np
from jax import lax
from jax.experimental import pallas as pl
from jax.experimental.pallas import tpu as pltpu
from jax.sharding import PartitionSpec as P

VMEM = pltpu.VMEM
SMEM = pltpu.SMEM
LIMIT = 48 * 1024 * 1024
STRIDE = 5
FOOT = 16


def params():
    return pltpu.CompilerParams(vmem_limit_bytes=LIMIT)


def within(col, half):
    return jnp.where(col >= half, col - half, col)


def cost(flops, size):
    return pl.CostEstimate(flops=flops, bytes_accessed=size, transcendentals=0)


def pack_kernel(half, cols_hbm, b_hbm, *refs):
    *o_refs, cols_ref, b_ref, sem, sems = refs
    rows, slots, bs, _ = b_ref.shape
    copies = [pltpu.make_async_copy(b_hbm.at[r], b_ref.at[r], sems.at[r]) for r in range(rows)]
    fetch = pltpu.make_async_copy(cols_hbm, cols_ref, sem)
    fetch.start()
    for copy in copies:
        copy.start()
    row = lax.broadcasted_iota(jnp.int32, (FOOT, 2 * bs), 0)
    lane = lax.broadcasted_iota(jnp.int32, (FOOT, 2 * bs), 1)
    fetch.wait()
    foot = jnp.full((FOOT, 2 * bs), slots, jnp.int32)
    for r in range(rows):
        for n in range(slots):
            here = (row == r) & (lane == within(cols_ref[r, n], half))
            foot = jnp.where(here, n, foot)
    o_refs[0][slots * bs :, :] = foot.astype(jnp.float32).astype(b_ref.dtype)
    for p, o_ref in enumerate(o_refs):
        copies[2 * p].wait()
        copies[2 * p + 1].wait()
        for n in range(slots):
            o_ref[n * bs : (n + 1) * bs, :] = jnp.concatenate([b_ref[2 * p, n], b_ref[2 * p + 1, n]], axis=-1)


def pack(half, cols, b_vals):
    rows, slots, bs, _ = b_vals.shape
    shapes = [(slots * bs + (FOOT if p == 0 else 0), 2 * bs) for p in range(rows // 2)]
    cols, b_vals = (pltpu.with_memory_space_constraint(x, pltpu.HBM) for x in (cols, b_vals))
    return pl.pallas_call(
        functools.partial(pack_kernel, half),
        out_shape=[jax.ShapeDtypeStruct(shape, b_vals.dtype) for shape in shapes],
        in_specs=[pl.BlockSpec(memory_space=pl.ANY)] * 2,
        out_specs=[pl.BlockSpec(memory_space=VMEM)] * len(shapes),
        scratch_shapes=[
            SMEM(cols.shape, cols.dtype),
            VMEM(b_vals.shape, b_vals.dtype),
            pltpu.SemaphoreType.DMA,
            pltpu.SemaphoreType.DMA((rows,)),
        ],
        compiler_params=params(),
        cost_estimate=cost(0, 2 * b_vals.size * 2),
    )(cols, b_vals)


def dense_kernel(cols_ref, others_ref, own_ref, other_ref, o_ref, blocks, where):
    rows, slots, bs, _ = own_ref.shape
    sources, pairs = o_ref.shape[:2]
    blocks[:, :slots] = own_ref[...]
    blocks[:, slots : 2 * slots] = other_ref[...]
    blocks[:, 2 * slots] = jnp.zeros_like(blocks[:, 2 * slots])
    for i in range(rows):
        def clear(j, carry):
            where[i, j] = 2 * slots
            return carry

        lax.fori_loop(0, 2 * sources * pairs, clear, 0, unroll=8)
        for m in range(slots):
            where[i, cols_ref[i, m]] = m
            where[i, others_ref[i, m]] = slots + m

    def body(s, carry):
        for p in range(pairs):
            j = (s * pairs + p) * 2
            for i in range(rows):
                left = blocks[i, where[i, j]]
                right = blocks[i, where[i, j + 1]]
                o_ref[s, p, i * bs : (i + 1) * bs, :] = jnp.concatenate([left, right], axis=-1)
        return carry

    lax.fori_loop(0, sources, body, 0, unroll=2)


def dense_rows(sources, cols, others, own, other):
    rows, slots, bs, _ = own.shape
    return pl.pallas_call(
        dense_kernel,
        out_shape=jax.ShapeDtypeStruct((sources, rows // 2, rows * bs, 2 * bs), own.dtype),
        grid_spec=pltpu.PrefetchScalarGridSpec(
            num_scalar_prefetch=2,
            grid=(),
            in_specs=[pl.BlockSpec(memory_space=VMEM)] * 2,
            out_specs=pl.BlockSpec(memory_space=VMEM),
            scratch_shapes=[
                VMEM((rows, 2 * slots + 1, bs, bs), own.dtype),
                SMEM((rows, sources * rows), jnp.int32),
            ],
        ),
        compiler_params=params(),
        cost_estimate=cost(0, 8 * own.size),
    )(cols, others, own, other)


def look_up(table, k):
    value = jnp.int32(table[0])
    for n, entry in enumerate(table[1:], 1):
        value = jnp.where(k == n, entry, value)
    return value


def arrived_from(order, way, steps):
    spots = [order.index(r) for r in range(len(order))]
    ahead = jnp.where(lax.axis_index("col") == 0, way, -way) * steps
    return look_up(order, lax.rem(look_up(spots, lax.axis_index("row")) - ahead + len(order), len(order)))


def add_products(panels, parts, total, first, feet, where, sem):
    groups, bs = total.shape[0], total.shape[3] // 2
    pairs = len(parts) // feet.shape[0]
    slots = (parts[0].shape[0] - FOOT) // bs
    for k in range(feet.shape[0]):
        feet[k] = parts[k * pairs][slots * bs :, :].astype(jnp.float32).astype(jnp.int32)
    copy = pltpu.make_async_copy(feet, where, sem)
    copy.start()
    copy.wait()
    low = lax.broadcasted_iota(jnp.int32, (bs, 2 * bs), 1) < bs
    left_side = jnp.concatenate([panel[...] for panel in panels], axis=-1)

    def block(part, slot):
        at = pl.multiple_of(jnp.minimum(slot, slots - 1) * bs, bs)
        return jnp.where(slot < slots, part[pl.ds(at, bs), :], jnp.zeros((bs, 2 * bs), part.dtype))

    def body(g, carry):
        rows = []
        for k, part in enumerate(parts):
            for h in range(2):
                tiles = []
                for q in (2 * g, 2 * g + 1):
                    left = block(part, where[k // pairs, k % pairs * 2 + h, 2 * q])
                    right = block(part, where[k // pairs, k % pairs * 2 + h, 2 * q + 1])
                    if h == 0:
                        right = pltpu.roll(right, bs, 1)
                    else:
                        left = pltpu.roll(left, bs, 1)
                    tiles.append(jnp.where(low, left, right))
                rows.append(jnp.concatenate(tiles, axis=-1))
        sums = jnp.dot(left_side, jnp.concatenate(rows, axis=0), preferred_element_type=jnp.float32)
        for t in range(2):
            piece = sums[:, t * 2 * bs : (t + 1) * 2 * bs]
            if first:
                total[g, t] = piece
            else:
                total[g, t] += piece
        return carry

    lax.fori_loop(0, groups, body, 0, unroll=min(groups, 4))


def split(a_ref, sources, parts):
    return [a_ref.at[place, p] for place in [source() for source in sources] for p in range(a_ref.shape[1])], parts


def first_kernel(sources, a_ref, *refs):
    *parts, total, feet, where, sem = refs
    add_products(*split(a_ref, sources, parts), total, True, feet, where, sem)


def middle_kernel(sources, a_ref, before, *refs):
    *parts, total, feet, where, sem = refs
    add_products(*split(a_ref, sources, parts), total, False, feet, where, sem)


def last_kernel(sources, a_ref, total, cols_hbm, *refs):
    *parts, o_hbm, feet, where, sem, cols_ref, o_ref, cols_sem, sems = refs
    fetch = pltpu.make_async_copy(cols_hbm, cols_ref, cols_sem)
    fetch.start()
    add_products(*split(a_ref, sources, parts), total, False, feet, where, sem)
    fetch.wait()
    rows, slots, bs, _ = o_ref.shape
    half = total.shape[0] * 4
    copies = []
    for i in range(rows):
        for k in range(slots):
            l = within(cols_ref[i, k], half)
            tile = total[l >> 2, (l >> 1) & 1, i * bs : (i + 1) * bs, :].astype(o_ref.dtype)
            tile = jnp.where(l & 1 == 0, tile, pltpu.roll(tile, bs, 1))
            o_ref[i, k] = tile[:, :bs]
            if k % STRIDE == STRIDE - 1 or k == slots - 1:
                some = pl.ds(k // STRIDE * STRIDE, k % STRIDE + 1)
                copies.append(pltpu.make_async_copy(o_ref.at[i, some], o_hbm.at[i, some], sems.at[i, k // STRIDE]))
                copies[-1].start()
    for copy in copies:
        copy.wait()


def product(order, arrived, a, total, out, cols=None):
    hbm, vmem = pl.BlockSpec(memory_space=pl.ANY), pl.BlockSpec(memory_space=VMEM)
    kernel = first_kernel if total is None else middle_kernel if cols is None else last_kernel
    sources = [functools.partial(arrived_from, order, way, steps) for way, steps, _ in arrived]
    parts = [ref for _, _, refs in arrived for ref in refs]
    feet = (len(arrived), FOOT, parts[0].shape[1])
    scratch = [VMEM(feet, jnp.int32), SMEM(feet, jnp.int32), pltpu.SemaphoreType.DMA]
    arrays, specs = [a], [vmem]
    if total is not None:
        arrays, specs = arrays + [total], specs + [vmem]
    if cols is not None:
        arrays, specs = arrays + [cols], specs + [hbm]
        scratch += [
            SMEM(cols.shape, cols.dtype),
            VMEM(out.shape, out.dtype),
            pltpu.SemaphoreType.DMA,
            pltpu.SemaphoreType.DMA((out.shape[0], -(-out.shape[1] // STRIDE))),
        ]
    return pl.pallas_call(
        functools.partial(kernel, sources),
        out_shape=out,
        in_specs=specs + [vmem] * len(parts),
        out_specs=vmem if cols is None else hbm,
        scratch_shapes=scratch,
        input_output_aliases={1: 0} if total is not None and cols is None else {},
        compiler_params=params(),
        cost_estimate=cost(2 * len(arrived) * a.shape[2] * math.prod(out.shape), 0),
    )(*arrays, *parts)


def local(order, a_vals, b_vals, cols):
    sources = len(order)
    rows, slots, bs, _ = a_vals.shape
    half = sources * rows // 2
    hops = {1: sources // 2, -1: (sources - 1) // 2}

    def ring(way):
        return [
            (order[r] * 2 + c, order[(r + (way if c == 0 else -way)) % sources] * 2 + c)
            for r in range(sources)
            for c in range(2)
        ]

    parts = pack(half, cols, b_vals)
    _, *mine = lax.optimization_barrier((parts[0], a_vals, cols))
    swap = [(0, 1), (1, 0)]
    a_other, others = (lax.ppermute(x, "col", swap) for x in mine)
    a = dense_rows(sources, cols, others, a_vals, a_other)
    total_shape = jax.ShapeDtypeStruct((half // 4, 2, rows * bs, 2 * bs), jnp.float32)
    total = None
    held = {way: parts for way in hops}
    rounds = [[(1, 0, parts)]]
    for step in range(1, hops[1] + 1):
        ways = [way for way in hops if step <= hops[way]]
        for way in ways:
            sent = list(held[way])
            if (step, way) == (1, -1):
                sent = [lax.optimization_barrier((part, others))[0] for part in sent]
            if (step, way) == (2, -1):
                sent[-1], _ = lax.optimization_barrier((sent[-1], a))
            if step > 2 and way == -1:
                total = product(order, rounds.pop(0), a, total, total_shape)
                sent[0], total = lax.optimization_barrier((sent[0], total))
            held[way] = [lax.ppermute(part, ("row", "col"), ring(way)) for part in sent]
        rounds.append([(way, step, held[way]) for way in ways])
    *_, late, last = rounds
    total = product(order, sum(rounds[:-2], late[:1]), a, total, total_shape)
    out = jax.ShapeDtypeStruct(a_vals.shape, a_vals.dtype)
    return product(order, late[1:] + last, a, total, out, cols)


def ring_order(mesh):
    count = mesh.shape["row"]
    coords = [getattr(d, "coords", None) for d in mesh.devices[0, :, 0]]
    loop = [*range(0, count, 2), *range(count - 1 - count % 2, 0, -2)]
    if None not in coords:
        steps = [
            sum(abs(x - y) for x, y in zip(coords[loop[k - 1]], coords[loop[k]]))
            for k in range(count)
        ]
        if max(steps) <= 1:
            return loop
    return list(range(count))


def solution(mesh):
    return jax.shard_map(
        functools.partial(local, ring_order(mesh)),
        mesh=mesh,
        in_specs=(
            P(("groups", "row"), "col", None, None),
            P(("groups", "row"), "col", None, None),
            P(("groups", "row"), "col"),
        ),
        out_specs=P(("groups", "row"), "col", None, None),
        check_vma=False,
    )
```

```python
import functools
import math

import jax
import jax.numpy as jnp
import numpy as np
from jax import lax
from jax.experimental import pallas as pl
from jax.experimental.pallas import tpu as pltpu
from jax.sharding import PartitionSpec as P

VMEM = pltpu.VMEM
SMEM = pltpu.SMEM
LIMIT = 48 * 1024 * 1024
STRIDE = 5
FOOT = 16


def params():
    return pltpu.CompilerParams(vmem_limit_bytes=LIMIT)


def within(col, half):
    return jnp.where(col >= half, col - half, col)


def cost(flops, size):
    return pl.CostEstimate(flops=flops, bytes_accessed=size, transcendentals=0)


def pack_kernel(half, cols_hbm, b_hbm, *refs):
    *o_refs, cols_ref, b_ref, sem, sems = refs
    rows, slots, bs, _ = b_ref.shape
    copies = [pltpu.make_async_copy(b_hbm.at[r], b_ref.at[r], sems.at[r]) for r in range(rows)]
    fetch = pltpu.make_async_copy(cols_hbm, cols_ref, sem)
    fetch.start()
    for copy in copies:
        copy.start()
    row = lax.broadcasted_iota(jnp.int32, (FOOT, 2 * bs), 0)
    lane = lax.broadcasted_iota(jnp.int32, (FOOT, 2 * bs), 1)
    fetch.wait()
    foot = jnp.full((FOOT, 2 * bs), slots, jnp.int32)
    for r in range(rows):
        for n in range(slots):
            here = (row == r) & (lane == within(cols_ref[r, n], half))
            foot = jnp.where(here, n, foot)
    o_refs[0][slots * bs :, :] = foot.astype(jnp.float32).astype(b_ref.dtype)
    for p, o_ref in enumerate(o_refs):
        copies[2 * p].wait()
        copies[2 * p + 1].wait()
        for n in range(slots):
            o_ref[n * bs : (n + 1) * bs, :] = jnp.concatenate([b_ref[2 * p, n], b_ref[2 * p + 1, n]], axis=-1)


def pack(half, cols, b_vals):
    rows, slots, bs, _ = b_vals.shape
    shapes = [(slots * bs + (FOOT if p == 0 else 0), 2 * bs) for p in range(rows // 2)]
    cols, b_vals = (pltpu.with_memory_space_constraint(x, pltpu.HBM) for x in (cols, b_vals))
    return pl.pallas_call(
        functools.partial(pack_kernel, half),
        out_shape=[jax.ShapeDtypeStruct(shape, b_vals.dtype) for shape in shapes],
        in_specs=[pl.BlockSpec(memory_space=pl.ANY)] * 2,
        out_specs=[pl.BlockSpec(memory_space=VMEM)] * len(shapes),
        scratch_shapes=[
            SMEM(cols.shape, cols.dtype),
            VMEM(b_vals.shape, b_vals.dtype),
            pltpu.SemaphoreType.DMA,
            pltpu.SemaphoreType.DMA((rows,)),
        ],
        compiler_params=params(),
        cost_estimate=cost(0, 2 * b_vals.size * 2),
    )(cols, b_vals)


def dense_kernel(cols_ref, others_ref, own_ref, other_ref, o_ref, blocks, where):
    rows, slots, bs, _ = own_ref.shape
    sources, pairs = o_ref.shape[:2]
    blocks[:, :slots] = own_ref[...]
    blocks[:, slots : 2 * slots] = other_ref[...]
    blocks[:, 2 * slots] = jnp.zeros_like(blocks[:, 2 * slots])
    for i in range(rows):
        def clear(j, carry):
            where[i, j] = 2 * slots
            return carry

        lax.fori_loop(0, 2 * sources * pairs, clear, 0, unroll=8)
        for m in range(slots):
            where[i, cols_ref[i, m]] = m
            where[i, others_ref[i, m]] = slots + m

    def body(s, carry):
        for p in range(pairs):
            j = (s * pairs + p) * 2
            for i in range(rows):
                left = blocks[i, where[i, j]]
                right = blocks[i, where[i, j + 1]]
                o_ref[s, p, i * bs : (i + 1) * bs, :] = jnp.concatenate([left, right], axis=-1)
        return carry

    lax.fori_loop(0, sources, body, 0, unroll=2)


def dense_rows(sources, cols, others, own, other):
    rows, slots, bs, _ = own.shape
    return pl.pallas_call(
        dense_kernel,
        out_shape=jax.ShapeDtypeStruct((sources, rows // 2, rows * bs, 2 * bs), own.dtype),
        grid_spec=pltpu.PrefetchScalarGridSpec(
            num_scalar_prefetch=2,
            grid=(),
            in_specs=[pl.BlockSpec(memory_space=VMEM)] * 2,
            out_specs=pl.BlockSpec(memory_space=VMEM),
            scratch_shapes=[
                VMEM((rows, 2 * slots + 1, bs, bs), own.dtype),
                SMEM((rows, sources * rows), jnp.int32),
            ],
        ),
        compiler_params=params(),
        cost_estimate=cost(0, 8 * own.size),
    )(cols, others, own, other)


def look_up(table, k):
    value = jnp.int32(table[0])
    for n, entry in enumerate(table[1:], 1):
        value = jnp.where(k == n, entry, value)
    return value


def arrived_from(order, way, steps):
    spots = [order.index(r) for r in range(len(order))]
    ahead = jnp.where(lax.axis_index("col") == 0, way, -way) * steps
    return look_up(order, lax.rem(look_up(spots, lax.axis_index("row")) - ahead + len(order), len(order)))


def add_products(panels, parts, total, first, feet, where, sem):
    groups, bs = total.shape[0], total.shape[3] // 2
    pairs = len(parts) // feet.shape[0]
    slots = (parts[0].shape[0] - FOOT) // bs
    for k in range(feet.shape[0]):
        feet[k] = parts[k * pairs][slots * bs :, :].astype(jnp.float32).astype(jnp.int32)
    copy = pltpu.make_async_copy(feet, where, sem)
    copy.start()
    copy.wait()
    low = lax.broadcasted_iota(jnp.int32, (bs, 2 * bs), 1) < bs
    left_side = jnp.concatenate([panel[...] for panel in panels], axis=-1)

    def block(part, slot):
        at = pl.multiple_of(jnp.minimum(slot, slots - 1) * bs, bs)
        return jnp.where(slot < slots, part[pl.ds(at, bs), :], jnp.zeros((bs, 2 * bs), part.dtype))

    def body(g, carry):
        rows = []
        for k, part in enumerate(parts):
            for h in range(2):
                tiles = []
                for q in (2 * g, 2 * g + 1):
                    left = block(part, where[k // pairs, k % pairs * 2 + h, 2 * q])
                    right = block(part, where[k // pairs, k % pairs * 2 + h, 2 * q + 1])
                    if h == 0:
                        right = pltpu.roll(right, bs, 1)
                    else:
                        left = pltpu.roll(left, bs, 1)
                    tiles.append(jnp.where(low, left, right))
                rows.append(jnp.concatenate(tiles, axis=-1))
        sums = jnp.dot(left_side, jnp.concatenate(rows, axis=0), preferred_element_type=jnp.float32)
        for t in range(2):
            piece = sums[:, t * 2 * bs : (t + 1) * 2 * bs]
            if first:
                total[g, t] = piece
            else:
                total[g, t] += piece
        return carry

    lax.fori_loop(0, groups, body, 0, unroll=min(groups, 4))


def split(a_ref, sources, parts):
    return [a_ref.at[place, p] for place in [source() for source in sources] for p in range(a_ref.shape[1])], parts


def first_kernel(sources, a_ref, *refs):
    *parts, total, feet, where, sem = refs
    add_products(*split(a_ref, sources, parts), total, True, feet, where, sem)


def middle_kernel(sources, a_ref, before, *refs):
    *parts, total, feet, where, sem = refs
    add_products(*split(a_ref, sources, parts), total, False, feet, where, sem)


def last_kernel(sources, a_ref, total, cols_hbm, *refs):
    *parts, o_hbm, feet, where, sem, cols_ref, o_ref, cols_sem, sems = refs
    fetch = pltpu.make_async_copy(cols_hbm, cols_ref, cols_sem)
    fetch.start()
    add_products(*split(a_ref, sources, parts), total, False, feet, where, sem)
    fetch.wait()
    rows, slots, bs, _ = o_ref.shape
    half = total.shape[0] * 4
    copies = []
    for i in range(rows):
        for k in range(slots):
            l = within(cols_ref[i, k], half)
            tile = total[l >> 2, (l >> 1) & 1, i * bs : (i + 1) * bs, :].astype(o_ref.dtype)
            tile = jnp.where(l & 1 == 0, tile, pltpu.roll(tile, bs, 1))
            o_ref[i, k] = tile[:, :bs]
            if k % STRIDE == STRIDE - 1 or k == slots - 1:
                some = pl.ds(k // STRIDE * STRIDE, k % STRIDE + 1)
                copies.append(pltpu.make_async_copy(o_ref.at[i, some], o_hbm.at[i, some], sems.at[i, k // STRIDE]))
                copies[-1].start()
    for copy in copies:
        copy.wait()


def product(order, arrived, a, total, out, cols=None):
    hbm, vmem = pl.BlockSpec(memory_space=pl.ANY), pl.BlockSpec(memory_space=VMEM)
    kernel = first_kernel if total is None else middle_kernel if cols is None else last_kernel
    sources = [functools.partial(arrived_from, order, way, steps) for way, steps, _ in arrived]
    parts = [ref for _, _, refs in arrived for ref in refs]
    feet = (len(arrived), FOOT, parts[0].shape[1])
    scratch = [VMEM(feet, jnp.int32), SMEM(feet, jnp.int32), pltpu.SemaphoreType.DMA]
    arrays, specs = [a], [vmem]
    if total is not None:
        arrays, specs = arrays + [total], specs + [vmem]
    if cols is not None:
        arrays, specs = arrays + [cols], specs + [hbm]
        scratch += [
            SMEM(cols.shape, cols.dtype),
            VMEM(out.shape, out.dtype),
            pltpu.SemaphoreType.DMA,
            pltpu.SemaphoreType.DMA((out.shape[0], -(-out.shape[1] // STRIDE))),
        ]
    return pl.pallas_call(
        functools.partial(kernel, sources),
        out_shape=out,
        in_specs=specs + [vmem] * len(parts),
        out_specs=vmem if cols is None else hbm,
        scratch_shapes=scratch,
        input_output_aliases={1: 0} if total is not None and cols is None else {},
        compiler_params=params(),
        cost_estimate=cost(2 * len(arrived) * a.shape[2] * math.prod(out.shape), 0),
    )(*arrays, *parts)


def local(order, a_vals, b_vals, cols):
    sources = len(order)
    rows, slots, bs, _ = a_vals.shape
    half = sources * rows // 2
    hops = {1: sources // 2, -1: (sources - 1) // 2}

    def ring(way):
        return [
            (order[r] * 2 + c, order[(r + (way if c == 0 else -way)) % sources] * 2 + c)
            for r in range(sources)
            for c in range(2)
        ]

    parts = pack(half, cols, b_vals)
    _, *mine = lax.optimization_barrier((parts[0], a_vals, cols))
    swap = [(0, 1), (1, 0)]
    a_other, others = (lax.ppermute(x, "col", swap) for x in mine)
    a = dense_rows(sources, cols, others, a_vals, a_other)
    total_shape = jax.ShapeDtypeStruct((half // 4, 2, rows * bs, 2 * bs), jnp.float32)
    total = None
    held = {way: parts for way in hops}
    rounds = [[(1, 0, parts)]]
    for step in range(1, hops[1] + 1):
        ways = [way for way in hops if step <= hops[way]]
        for way in ways:
            sent = list(held[way])
            if (step, way) == (1, -1):
                sent = [lax.optimization_barrier((part, others))[0] for part in sent]
            if (step, way) == (2, -1):
                sent[0], _ = lax.optimization_barrier((sent[0], a))
            if step > 2 and way == -1:
                total = product(order, rounds.pop(0), a, total, total_shape)
                sent[0], total = lax.optimization_barrier((sent[0], total))
            held[way] = [lax.ppermute(part, ("row", "col"), ring(way)) for part in sent]
        rounds.append([(way, step, held[way]) for way in ways])
    *_, late, last = rounds
    total = product(order, sum(rounds[:-2], late[:1]), a, total, total_shape)
    out = jax.ShapeDtypeStruct(a_vals.shape, a_vals.dtype)
    return product(order, late[1:] + last, a, total, out, cols)


def ring_order(mesh):
    count = mesh.shape["row"]
    coords = [getattr(d, "coords", None) for d in mesh.devices[0, :, 0]]
    loop = [*range(0, count, 2), *range(count - 1 - count % 2, 0, -2)]
    if None not in coords:
        steps = [
            sum(abs(x - y) for x, y in zip(coords[loop[k - 1]], coords[loop[k]]))
            for k in range(count)
        ]
        if max(steps) <= 1:
            return loop
    return list(range(count))


def solution(mesh):
    return jax.shard_map(
        functools.partial(local, ring_order(mesh)),
        mesh=mesh,
        in_specs=(
            P(("groups", "row"), "col", None, None),
            P(("groups", "row"), "col", None, None),
            P(("groups", "row"), "col"),
        ),
        out_specs=P(("groups", "row"), "col", None, None),
        check_vma=False,
    )
```

```python
import functools
import math

import jax
import jax.numpy as jnp
import numpy as np
from jax import lax
from jax.experimental import pallas as pl
from jax.experimental.pallas import tpu as pltpu
from jax.sharding import PartitionSpec as P

VMEM = pltpu.VMEM
SMEM = pltpu.SMEM
LIMIT = 48 * 1024 * 1024
STRIDE = 5
FOOT = 16


def params():
    return pltpu.CompilerParams(vmem_limit_bytes=LIMIT)


def within(col, half):
    return jnp.where(col >= half, col - half, col)


def cost(flops, size):
    return pl.CostEstimate(flops=flops, bytes_accessed=size, transcendentals=0)


def pack_kernel(half, cols_hbm, b_hbm, *refs):
    *o_refs, cols_ref, b_ref, sem, sems = refs
    rows, slots, bs, _ = b_ref.shape
    copies = [pltpu.make_async_copy(b_hbm.at[r], b_ref.at[r], sems.at[r]) for r in range(rows)]
    fetch = pltpu.make_async_copy(cols_hbm, cols_ref, sem)
    fetch.start()
    for copy in copies:
        copy.start()
    row = lax.broadcasted_iota(jnp.int32, (FOOT, 2 * bs), 0)
    lane = lax.broadcasted_iota(jnp.int32, (FOOT, 2 * bs), 1)
    fetch.wait()
    foot = jnp.full((FOOT, 2 * bs), slots, jnp.int32)
    for r in range(rows):
        for n in range(slots):
            here = (row == r) & (lane == within(cols_ref[r, n], half))
            foot = jnp.where(here, n, foot)
    o_refs[0][slots * bs :, :] = foot.astype(jnp.float32).astype(b_ref.dtype)
    for p, o_ref in enumerate(o_refs):
        copies[2 * p].wait()
        copies[2 * p + 1].wait()
        for n in range(slots):
            o_ref[n * bs : (n + 1) * bs, :] = jnp.concatenate([b_ref[2 * p, n], b_ref[2 * p + 1, n]], axis=-1)


def pack(half, cols, b_vals):
    rows, slots, bs, _ = b_vals.shape
    shapes = [(slots * bs + (FOOT if p == 0 else 0), 2 * bs) for p in range(rows // 2)]
    cols, b_vals = (pltpu.with_memory_space_constraint(x, pltpu.HBM) for x in (cols, b_vals))
    return pl.pallas_call(
        functools.partial(pack_kernel, half),
        out_shape=[jax.ShapeDtypeStruct(shape, b_vals.dtype) for shape in shapes],
        in_specs=[pl.BlockSpec(memory_space=pl.ANY)] * 2,
        out_specs=[pl.BlockSpec(memory_space=VMEM)] * len(shapes),
        scratch_shapes=[
            SMEM(cols.shape, cols.dtype),
            VMEM(b_vals.shape, b_vals.dtype),
            pltpu.SemaphoreType.DMA,
            pltpu.SemaphoreType.DMA((rows,)),
        ],
        compiler_params=params(),
        cost_estimate=cost(0, 2 * b_vals.size * 2),
    )(cols, b_vals)


def dense_kernel(cols_ref, others_ref, own_ref, other_ref, o_ref, blocks, where):
    rows, slots, bs, _ = own_ref.shape
    sources, pairs = o_ref.shape[:2]
    blocks[:, :slots] = own_ref[...]
    blocks[:, slots : 2 * slots] = other_ref[...]
    blocks[:, 2 * slots] = jnp.zeros_like(blocks[:, 2 * slots])
    for i in range(rows):
        def clear(j, carry):
            where[i, j] = 2 * slots
            return carry

        lax.fori_loop(0, 2 * sources * pairs, clear, 0, unroll=8)
        for m in range(slots):
            where[i, cols_ref[i, m]] = m
            where[i, others_ref[i, m]] = slots + m

    def body(s, carry):
        for p in range(pairs):
            j = (s * pairs + p) * 2
            for i in range(rows):
                left = blocks[i, where[i, j]]
                right = blocks[i, where[i, j + 1]]
                o_ref[s, p, i * bs : (i + 1) * bs, :] = jnp.concatenate([left, right], axis=-1)
        return carry

    lax.fori_loop(0, sources, body, 0, unroll=2)


def dense_rows(sources, cols, others, own, other):
    rows, slots, bs, _ = own.shape
    return pl.pallas_call(
        dense_kernel,
        out_shape=jax.ShapeDtypeStruct((sources, rows // 2, rows * bs, 2 * bs), own.dtype),
        grid_spec=pltpu.PrefetchScalarGridSpec(
            num_scalar_prefetch=2,
            grid=(),
            in_specs=[pl.BlockSpec(memory_space=VMEM)] * 2,
            out_specs=pl.BlockSpec(memory_space=VMEM),
            scratch_shapes=[
                VMEM((rows, 2 * slots + 1, bs, bs), own.dtype),
                SMEM((rows, sources * rows), jnp.int32),
            ],
        ),
        compiler_params=params(),
        cost_estimate=cost(0, 8 * own.size),
    )(cols, others, own, other)


def look_up(table, k):
    value = jnp.int32(table[0])
    for n, entry in enumerate(table[1:], 1):
        value = jnp.where(k == n, entry, value)
    return value


def arrived_from(order, way, steps):
    spots = [order.index(r) for r in range(len(order))]
    ahead = jnp.where(lax.axis_index("col") == 0, way, -way) * steps
    return look_up(order, lax.rem(look_up(spots, lax.axis_index("row")) - ahead + len(order), len(order)))


def add_products(panels, parts, total, first, feet, where, sem):
    groups, bs = total.shape[0], total.shape[3] // 2
    pairs = len(parts) // feet.shape[0]
    slots = (parts[0].shape[0] - FOOT) // bs
    for k in range(feet.shape[0]):
        feet[k] = parts[k * pairs][slots * bs :, :].astype(jnp.float32).astype(jnp.int32)
    copy = pltpu.make_async_copy(feet, where, sem)
    copy.start()
    copy.wait()
    low = lax.broadcasted_iota(jnp.int32, (bs, 2 * bs), 1) < bs
    left_side = jnp.concatenate([panel[...] for panel in panels], axis=-1)

    def block(part, slot):
        at = pl.multiple_of(jnp.minimum(slot, slots - 1) * bs, bs)
        return jnp.where(slot < slots, part[pl.ds(at, bs), :], jnp.zeros((bs, 2 * bs), part.dtype))

    def body(g, carry):
        rows = []
        for k, part in enumerate(parts):
            for h in range(2):
                tiles = []
                for q in (2 * g, 2 * g + 1):
                    left = block(part, where[k // pairs, k % pairs * 2 + h, 2 * q])
                    right = block(part, where[k // pairs, k % pairs * 2 + h, 2 * q + 1])
                    if h == 0:
                        right = pltpu.roll(right, bs, 1)
                    else:
                        left = pltpu.roll(left, bs, 1)
                    tiles.append(jnp.where(low, left, right))
                rows.append(jnp.concatenate(tiles, axis=-1))
        sums = jnp.dot(left_side, jnp.concatenate(rows, axis=0), preferred_element_type=jnp.float32)
        for t in range(2):
            piece = sums[:, t * 2 * bs : (t + 1) * 2 * bs]
            if first:
                total[g, t] = piece
            else:
                total[g, t] += piece
        return carry

    lax.fori_loop(0, groups, body, 0, unroll=min(groups, 4))


def split(a_ref, sources, parts):
    return [a_ref.at[place, p] for place in [source() for source in sources] for p in range(a_ref.shape[1])], parts


def first_kernel(sources, a_ref, *refs):
    *parts, total, feet, where, sem = refs
    add_products(*split(a_ref, sources, parts), total, True, feet, where, sem)


def middle_kernel(sources, a_ref, before, *refs):
    *parts, total, feet, where, sem = refs
    add_products(*split(a_ref, sources, parts), total, False, feet, where, sem)


def last_kernel(sources, a_ref, total, cols_hbm, *refs):
    *parts, o_hbm, feet, where, sem, cols_ref, o_ref, cols_sem, sems = refs
    fetch = pltpu.make_async_copy(cols_hbm, cols_ref, cols_sem)
    fetch.start()
    add_products(*split(a_ref, sources, parts), total, False, feet, where, sem)
    fetch.wait()
    rows, slots, bs, _ = o_ref.shape
    half = total.shape[0] * 4
    copies = []
    for i in range(rows):
        for k in range(slots):
            l = within(cols_ref[i, k], half)
            tile = total[l >> 2, (l >> 1) & 1, i * bs : (i + 1) * bs, :].astype(o_ref.dtype)
            tile = jnp.where(l & 1 == 0, tile, pltpu.roll(tile, bs, 1))
            o_ref[i, k] = tile[:, :bs]
            if k % STRIDE == STRIDE - 1 or k == slots - 1:
                some = pl.ds(k // STRIDE * STRIDE, k % STRIDE + 1)
                copies.append(pltpu.make_async_copy(o_ref.at[i, some], o_hbm.at[i, some], sems.at[i, k // STRIDE]))
                copies[-1].start()
    for copy in copies:
        copy.wait()


def product(order, arrived, a, total, out, cols=None):
    hbm, vmem = pl.BlockSpec(memory_space=pl.ANY), pl.BlockSpec(memory_space=VMEM)
    kernel = first_kernel if total is None else middle_kernel if cols is None else last_kernel
    sources = [functools.partial(arrived_from, order, way, steps) for way, steps, _ in arrived]
    parts = [ref for _, _, refs in arrived for ref in refs]
    feet = (len(arrived), FOOT, parts[0].shape[1])
    scratch = [VMEM(feet, jnp.int32), SMEM(feet, jnp.int32), pltpu.SemaphoreType.DMA]
    arrays, specs = [a], [vmem]
    if total is not None:
        arrays, specs = arrays + [total], specs + [vmem]
    if cols is not None:
        arrays, specs = arrays + [cols], specs + [hbm]
        scratch += [
            SMEM(cols.shape, cols.dtype),
            VMEM(out.shape, out.dtype),
            pltpu.SemaphoreType.DMA,
            pltpu.SemaphoreType.DMA((out.shape[0], -(-out.shape[1] // STRIDE))),
        ]
    return pl.pallas_call(
        functools.partial(kernel, sources),
        out_shape=out,
        in_specs=specs + [vmem] * len(parts),
        out_specs=vmem if cols is None else hbm,
        scratch_shapes=scratch,
        input_output_aliases={1: 0} if total is not None and cols is None else {},
        compiler_params=params(),
        cost_estimate=cost(2 * len(arrived) * a.shape[2] * math.prod(out.shape), 0),
    )(*arrays, *parts)


def local(order, a_vals, b_vals, cols):
    sources = len(order)
    rows, slots, bs, _ = a_vals.shape
    half = sources * rows // 2
    hops = {1: sources // 2, -1: (sources - 1) // 2}

    def ring(way):
        return [
            (order[r] * 2 + c, order[(r + (way if c == 0 else -way)) % sources] * 2 + c)
            for r in range(sources)
            for c in range(2)
        ]

    parts = pack(half, cols, b_vals)
    _, *mine = lax.optimization_barrier((parts[0], a_vals, cols))
    swap = [(0, 1), (1, 0)]
    a_other, others = (lax.ppermute(x, "col", swap) for x in mine)
    a = dense_rows(sources, cols, others, a_vals, a_other)
    total_shape = jax.ShapeDtypeStruct((half // 4, 2, rows * bs, 2 * bs), jnp.float32)
    total = None
    held = {way: parts for way in hops}
    rounds = [[(1, 0, parts)]]
    for step in range(1, hops[1] + 1):
        ways = [way for way in hops if step <= hops[way]]
        for way in ways:
            sent = list(held[way])
            if (step, way) == (2, -1):
                sent[0], _ = lax.optimization_barrier((sent[0], a))
            if step > 2 and way == -1:
                total = product(order, rounds.pop(0), a, total, total_shape)
                sent[0], total = lax.optimization_barrier((sent[0], total))
            held[way] = [lax.ppermute(part, ("row", "col"), ring(way)) for part in sent]
        rounds.append([(way, step, held[way]) for way in ways])
    *_, late, last = rounds
    total = product(order, sum(rounds[:-2], late[:1]), a, total, total_shape)
    out = jax.ShapeDtypeStruct(a_vals.shape, a_vals.dtype)
    return product(order, late[1:] + last, a, total, out, cols)


def ring_order(mesh):
    count = mesh.shape["row"]
    coords = [getattr(d, "coords", None) for d in mesh.devices[0, :, 0]]
    loop = [*range(0, count, 2), *range(count - 1 - count % 2, 0, -2)]
    if None not in coords:
        steps = [
            sum(abs(x - y) for x, y in zip(coords[loop[k - 1]], coords[loop[k]]))
            for k in range(count)
        ]
        if max(steps) <= 1:
            return loop
    return list(range(count))


def solution(mesh):
    return jax.shard_map(
        functools.partial(local, ring_order(mesh)),
        mesh=mesh,
        in_specs=(
            P(("groups", "row"), "col", None, None),
            P(("groups", "row"), "col", None, None),
            P(("groups", "row"), "col"),
        ),
        out_specs=P(("groups", "row"), "col", None, None),
        check_vma=False,
    )
```

```python
import functools
import math

import jax
import jax.numpy as jnp
import numpy as np
from jax import lax
from jax.experimental import pallas as pl
from jax.experimental.pallas import tpu as pltpu
from jax.sharding import PartitionSpec as P

VMEM = pltpu.VMEM
SMEM = pltpu.SMEM
LIMIT = 48 * 1024 * 1024
STRIDE = 5
FOOT = 16


def params():
    return pltpu.CompilerParams(vmem_limit_bytes=LIMIT)


def within(col, half):
    return jnp.where(col >= half, col - half, col)


def cost(flops, size):
    return pl.CostEstimate(flops=flops, bytes_accessed=size, transcendentals=0)


def pack_kernel(half, cols_hbm, b_hbm, *refs):
    *o_refs, cols_ref, b_ref, sem, sems = refs
    rows, slots, bs, _ = b_ref.shape
    copies = [pltpu.make_async_copy(b_hbm.at[r], b_ref.at[r], sems.at[r]) for r in range(rows)]
    fetch = pltpu.make_async_copy(cols_hbm, cols_ref, sem)
    fetch.start()
    for copy in copies:
        copy.start()
    row = lax.broadcasted_iota(jnp.int32, (FOOT, 2 * bs), 0)
    lane = lax.broadcasted_iota(jnp.int32, (FOOT, 2 * bs), 1)
    fetch.wait()
    foot = jnp.full((FOOT, 2 * bs), slots, jnp.int32)
    for r in range(rows):
        for n in range(slots):
            here = (row == r) & (lane == within(cols_ref[r, n], half))
            foot = jnp.where(here, n, foot)
    o_refs[0][slots * bs :, :] = foot.astype(jnp.float32).astype(b_ref.dtype)
    for p, o_ref in enumerate(o_refs):
        copies[2 * p].wait()
        copies[2 * p + 1].wait()
        for n in range(slots):
            o_ref[n * bs : (n + 1) * bs, :] = jnp.concatenate([b_ref[2 * p, n], b_ref[2 * p + 1, n]], axis=-1)


def pack(half, cols, b_vals):
    rows, slots, bs, _ = b_vals.shape
    shapes = [(slots * bs + (FOOT if p == 0 else 0), 2 * bs) for p in range(rows // 2)]
    cols, b_vals = (pltpu.with_memory_space_constraint(x, pltpu.HBM) for x in (cols, b_vals))
    return pl.pallas_call(
        functools.partial(pack_kernel, half),
        out_shape=[jax.ShapeDtypeStruct(shape, b_vals.dtype) for shape in shapes],
        in_specs=[pl.BlockSpec(memory_space=pl.ANY)] * 2,
        out_specs=[pl.BlockSpec(memory_space=VMEM)] * len(shapes),
        scratch_shapes=[
            SMEM(cols.shape, cols.dtype),
            VMEM(b_vals.shape, b_vals.dtype),
            pltpu.SemaphoreType.DMA,
            pltpu.SemaphoreType.DMA((rows,)),
        ],
        compiler_params=params(),
        cost_estimate=cost(0, 2 * b_vals.size * 2),
    )(cols, b_vals)


def dense_kernel(cols_ref, others_ref, own_ref, other_ref, o_ref, blocks, where):
    rows, slots, bs, _ = own_ref.shape
    sources, pairs = o_ref.shape[:2]
    blocks[:, :slots] = own_ref[...]
    blocks[:, slots : 2 * slots] = other_ref[...]
    blocks[:, 2 * slots] = jnp.zeros_like(blocks[:, 2 * slots])
    for i in range(rows):
        def clear(j, carry):
            where[i, j] = 2 * slots
            return carry

        lax.fori_loop(0, 2 * sources * pairs, clear, 0, unroll=8)
        for m in range(slots):
            where[i, cols_ref[i, m]] = m
            where[i, others_ref[i, m]] = slots + m

    def body(s, carry):
        for p in range(pairs):
            j = (s * pairs + p) * 2
            for i in range(rows):
                left = blocks[i, where[i, j]]
                right = blocks[i, where[i, j + 1]]
                o_ref[s, p, i * bs : (i + 1) * bs, :] = jnp.concatenate([left, right], axis=-1)
        return carry

    lax.fori_loop(0, sources, body, 0, unroll=2)


def dense_rows(sources, cols, others, own, other):
    rows, slots, bs, _ = own.shape
    return pl.pallas_call(
        dense_kernel,
        out_shape=jax.ShapeDtypeStruct((sources, rows // 2, rows * bs, 2 * bs), own.dtype),
        grid_spec=pltpu.PrefetchScalarGridSpec(
            num_scalar_prefetch=2,
            grid=(),
            in_specs=[pl.BlockSpec(memory_space=VMEM)] * 2,
            out_specs=pl.BlockSpec(memory_space=VMEM),
            scratch_shapes=[
                VMEM((rows, 2 * slots + 1, bs, bs), own.dtype),
                SMEM((rows, sources * rows), jnp.int32),
            ],
        ),
        compiler_params=params(),
        cost_estimate=cost(0, 8 * own.size),
    )(cols, others, own, other)


def look_up(table, k):
    value = jnp.int32(table[0])
    for n, entry in enumerate(table[1:], 1):
        value = jnp.where(k == n, entry, value)
    return value


def arrived_from(order, way, steps):
    spots = [order.index(r) for r in range(len(order))]
    ahead = jnp.where(lax.axis_index("col") == 0, way, -way) * steps
    return look_up(order, lax.rem(look_up(spots, lax.axis_index("row")) - ahead + len(order), len(order)))


def add_products(panels, parts, total, first, feet, where, sem):
    groups, bs = total.shape[0], total.shape[3] // 2
    pairs = len(parts) // feet.shape[0]
    slots = (parts[0].shape[0] - FOOT) // bs
    for k in range(feet.shape[0]):
        feet[k] = parts[k * pairs][slots * bs :, :].astype(jnp.float32).astype(jnp.int32)
    copy = pltpu.make_async_copy(feet, where, sem)
    copy.start()
    copy.wait()
    low = lax.broadcasted_iota(jnp.int32, (bs, 2 * bs), 1) < bs
    left_side = jnp.concatenate([panel[...] for panel in panels], axis=-1)

    def block(part, slot):
        at = pl.multiple_of(jnp.minimum(slot, slots - 1) * bs, bs)
        return jnp.where(slot < slots, part[pl.ds(at, bs), :], jnp.zeros((bs, 2 * bs), part.dtype))

    def body(g, carry):
        rows = []
        for k, part in enumerate(parts):
            for h in range(2):
                tiles = []
                for q in (2 * g, 2 * g + 1):
                    left = block(part, where[k // pairs, k % pairs * 2 + h, 2 * q])
                    right = block(part, where[k // pairs, k % pairs * 2 + h, 2 * q + 1])
                    if h == 0:
                        right = pltpu.roll(right, bs, 1)
                    else:
                        left = pltpu.roll(left, bs, 1)
                    tiles.append(jnp.where(low, left, right))
                rows.append(jnp.concatenate(tiles, axis=-1))
        sums = jnp.dot(left_side, jnp.concatenate(rows, axis=0), preferred_element_type=jnp.float32)
        for t in range(2):
            piece = sums[:, t * 2 * bs : (t + 1) * 2 * bs]
            if first:
                total[g, t] = piece
            else:
                total[g, t] += piece
        return carry

    lax.fori_loop(0, groups, body, 0, unroll=min(groups, 4))


def split(a_ref, sources, parts):
    return [a_ref.at[place, p] for place in [source() for source in sources] for p in range(a_ref.shape[1])], parts


def first_kernel(sources, a_ref, *refs):
    *parts, total, feet, where, sem = refs
    add_products(*split(a_ref, sources, parts), total, True, feet, where, sem)


def middle_kernel(sources, a_ref, before, *refs):
    *parts, total, feet, where, sem = refs
    add_products(*split(a_ref, sources, parts), total, False, feet, where, sem)


def last_kernel(sources, a_ref, total, cols_hbm, *refs):
    *parts, o_hbm, feet, where, sem, cols_ref, o_ref, cols_sem, sems = refs
    fetch = pltpu.make_async_copy(cols_hbm, cols_ref, cols_sem)
    fetch.start()
    add_products(*split(a_ref, sources, parts), total, False, feet, where, sem)
    fetch.wait()
    rows, slots, bs, _ = o_ref.shape
    half = total.shape[0] * 4
    copies = []
    for i in range(rows):
        for k in range(slots):
            l = within(cols_ref[i, k], half)
            tile = total[l >> 2, (l >> 1) & 1, i * bs : (i + 1) * bs, :].astype(o_ref.dtype)
            tile = jnp.where(l & 1 == 0, tile, pltpu.roll(tile, bs, 1))
            o_ref[i, k] = tile[:, :bs]
            if k % STRIDE == STRIDE - 1 or k == slots - 1:
                some = pl.ds(k // STRIDE * STRIDE, k % STRIDE + 1)
                copies.append(pltpu.make_async_copy(o_ref.at[i, some], o_hbm.at[i, some], sems.at[i, k // STRIDE]))
                copies[-1].start()
    for copy in copies:
        copy.wait()


def product(order, arrived, a, total, out, cols=None):
    hbm, vmem = pl.BlockSpec(memory_space=pl.ANY), pl.BlockSpec(memory_space=VMEM)
    kernel = first_kernel if total is None else middle_kernel if cols is None else last_kernel
    sources = [functools.partial(arrived_from, order, way, steps) for way, steps, _ in arrived]
    parts = [ref for _, _, refs in arrived for ref in refs]
    feet = (len(arrived), FOOT, parts[0].shape[1])
    scratch = [VMEM(feet, jnp.int32), SMEM(feet, jnp.int32), pltpu.SemaphoreType.DMA]
    arrays, specs = [a], [vmem]
    if total is not None:
        arrays, specs = arrays + [total], specs + [vmem]
    if cols is not None:
        arrays, specs = arrays + [cols], specs + [hbm]
        scratch += [
            SMEM(cols.shape, cols.dtype),
            VMEM(out.shape, out.dtype),
            pltpu.SemaphoreType.DMA,
            pltpu.SemaphoreType.DMA((out.shape[0], -(-out.shape[1] // STRIDE))),
        ]
    return pl.pallas_call(
        functools.partial(kernel, sources),
        out_shape=out,
        in_specs=specs + [vmem] * len(parts),
        out_specs=vmem if cols is None else hbm,
        scratch_shapes=scratch,
        input_output_aliases={1: 0} if total is not None and cols is None else {},
        compiler_params=params(),
        cost_estimate=cost(2 * len(arrived) * a.shape[2] * math.prod(out.shape), 0),
    )(*arrays, *parts)


def local(order, a_vals, b_vals, cols):
    sources = len(order)
    rows, slots, bs, _ = a_vals.shape
    half = sources * rows // 2
    hops = {1: sources // 2, -1: (sources - 1) // 2}

    def ring(way):
        return [
            (order[r] * 2 + c, order[(r + (way if c == 0 else -way)) % sources] * 2 + c)
            for r in range(sources)
            for c in range(2)
        ]

    parts = pack(half, cols, b_vals)
    _, *mine = lax.optimization_barrier((parts[0], a_vals, cols))
    swap = [(0, 1), (1, 0)]
    a_other, others = (lax.ppermute(x, "col", swap) for x in mine)
    a = dense_rows(sources, cols, others, a_vals, a_other)
    total_shape = jax.ShapeDtypeStruct((half // 4, 2, rows * bs, 2 * bs), jnp.float32)
    total = None
    held = {way: parts for way in hops}
    rounds = [[(1, 0, parts)]]
    for step in range(1, hops[1] + 1):
        ways = [way for way in hops if step <= hops[way]]
        for way in ways:
            sent = list(held[way])
            if (step, way) == (3, 1):
                sent[-1], _, _ = lax.optimization_barrier((sent[-1], a, held[-1][-1]))
            if step > 2 and way == -1:
                total = product(order, rounds.pop(0), a, total, total_shape)
                sent[0], total = lax.optimization_barrier((sent[0], total))
            if (step, way) == (2, 1):
                sent[-1], _ = lax.optimization_barrier((sent[-1], rounds[1][1][2][-1]))
            held[way] = [lax.ppermute(part, ("row", "col"), ring(way)) for part in sent]
        rounds.append([(way, step, held[way]) for way in ways])
    *_, late, last = rounds
    total = product(order, sum(rounds[:-2], late[:1]), a, total, total_shape)
    out = jax.ShapeDtypeStruct(a_vals.shape, a_vals.dtype)
    return product(order, late[1:] + last, a, total, out, cols)


def ring_order(mesh):
    count = mesh.shape["row"]
    coords = [getattr(d, "coords", None) for d in mesh.devices[0, :, 0]]
    loop = [*range(0, count, 2), *range(count - 1 - count % 2, 0, -2)]
    if None not in coords:
        steps = [
            sum(abs(x - y) for x, y in zip(coords[loop[k - 1]], coords[loop[k]]))
            for k in range(count)
        ]
        if max(steps) <= 1:
            return loop
    return list(range(count))


def solution(mesh):
    return jax.shard_map(
        functools.partial(local, ring_order(mesh)),
        mesh=mesh,
        in_specs=(
            P(("groups", "row"), "col", None, None),
            P(("groups", "row"), "col", None, None),
            P(("groups", "row"), "col"),
        ),
        out_specs=P(("groups", "row"), "col", None, None),
        check_vma=False,
    )
```

```python
import functools
import math

import jax
import jax.numpy as jnp
import numpy as np
from jax import lax
from jax.experimental import pallas as pl
from jax.experimental.pallas import tpu as pltpu
from jax.sharding import PartitionSpec as P

VMEM = pltpu.VMEM
SMEM = pltpu.SMEM
LIMIT = 48 * 1024 * 1024
STRIDE = 5
FOOT = 16


def params():
    return pltpu.CompilerParams(vmem_limit_bytes=LIMIT)


def within(col, half):
    return jnp.where(col >= half, col - half, col)


def cost(flops, size):
    return pl.CostEstimate(flops=flops, bytes_accessed=size, transcendentals=0)


def pack_kernel(half, cols_hbm, b_hbm, *refs):
    *o_refs, cols_ref, b_ref, sem, sems = refs
    rows, slots, bs, _ = b_ref.shape
    copies = [pltpu.make_async_copy(b_hbm.at[r], b_ref.at[r], sems.at[r]) for r in range(rows)]
    fetch = pltpu.make_async_copy(cols_hbm, cols_ref, sem)
    fetch.start()
    for copy in copies:
        copy.start()
    row = lax.broadcasted_iota(jnp.int32, (FOOT, 2 * bs), 0)
    lane = lax.broadcasted_iota(jnp.int32, (FOOT, 2 * bs), 1)
    fetch.wait()
    foot = jnp.full((FOOT, 2 * bs), slots, jnp.int32)
    for r in range(rows):
        for n in range(slots):
            here = (row == r) & (lane == within(cols_ref[r, n], half))
            foot = jnp.where(here, n, foot)
    o_refs[0][slots * bs :, :] = foot.astype(jnp.float32).astype(b_ref.dtype)
    for p, o_ref in enumerate(o_refs):
        copies[2 * p].wait()
        copies[2 * p + 1].wait()
        for n in range(slots):
            o_ref[n * bs : (n + 1) * bs, :] = jnp.concatenate([b_ref[2 * p, n], b_ref[2 * p + 1, n]], axis=-1)


def pack(half, cols, b_vals):
    rows, slots, bs, _ = b_vals.shape
    shapes = [(slots * bs + (FOOT if p == 0 else 0), 2 * bs) for p in range(rows // 2)]
    cols, b_vals = (pltpu.with_memory_space_constraint(x, pltpu.HBM) for x in (cols, b_vals))
    return pl.pallas_call(
        functools.partial(pack_kernel, half),
        out_shape=[jax.ShapeDtypeStruct(shape, b_vals.dtype) for shape in shapes],
        in_specs=[pl.BlockSpec(memory_space=pl.ANY)] * 2,
        out_specs=[pl.BlockSpec(memory_space=VMEM)] * len(shapes),
        scratch_shapes=[
            SMEM(cols.shape, cols.dtype),
            VMEM(b_vals.shape, b_vals.dtype),
            pltpu.SemaphoreType.DMA,
            pltpu.SemaphoreType.DMA((rows,)),
        ],
        compiler_params=params(),
        cost_estimate=cost(0, 2 * b_vals.size * 2),
    )(cols, b_vals)


def dense_kernel(cols_ref, others_ref, own_ref, other_ref, o_ref, blocks, where):
    rows, slots, bs, _ = own_ref.shape
    sources, pairs = o_ref.shape[:2]
    blocks[:, :slots] = own_ref[...]
    blocks[:, slots : 2 * slots] = other_ref[...]
    blocks[:, 2 * slots] = jnp.zeros_like(blocks[:, 2 * slots])
    for i in range(rows):
        def clear(j, carry):
            where[i, j] = 2 * slots
            return carry

        lax.fori_loop(0, 2 * sources * pairs, clear, 0, unroll=8)
        for m in range(slots):
            where[i, cols_ref[i, m]] = m
            where[i, others_ref[i, m]] = slots + m

    def body(s, carry):
        for p in range(pairs):
            j = (s * pairs + p) * 2
            for i in range(rows):
                left = blocks[i, where[i, j]]
                right = blocks[i, where[i, j + 1]]
                o_ref[s, p, i * bs : (i + 1) * bs, :] = jnp.concatenate([left, right], axis=-1)
        return carry

    lax.fori_loop(0, sources, body, 0, unroll=2)


def dense_rows(sources, cols, others, own, other):
    rows, slots, bs, _ = own.shape
    return pl.pallas_call(
        dense_kernel,
        out_shape=jax.ShapeDtypeStruct((sources, rows // 2, rows * bs, 2 * bs), own.dtype),
        grid_spec=pltpu.PrefetchScalarGridSpec(
            num_scalar_prefetch=2,
            grid=(),
            in_specs=[pl.BlockSpec(memory_space=VMEM)] * 2,
            out_specs=pl.BlockSpec(memory_space=VMEM),
            scratch_shapes=[
                VMEM((rows, 2 * slots + 1, bs, bs), own.dtype),
                SMEM((rows, sources * rows), jnp.int32),
            ],
        ),
        compiler_params=params(),
        cost_estimate=cost(0, 8 * own.size),
    )(cols, others, own, other)


def look_up(table, k):
    value = jnp.int32(table[0])
    for n, entry in enumerate(table[1:], 1):
        value = jnp.where(k == n, entry, value)
    return value


def arrived_from(order, way, steps):
    spots = [order.index(r) for r in range(len(order))]
    ahead = jnp.where(lax.axis_index("col") == 0, way, -way) * steps
    return look_up(order, lax.rem(look_up(spots, lax.axis_index("row")) - ahead + len(order), len(order)))


def add_products(a_ref, sources, refs, total, first, feet, where, sem):
    groups, bs = total.shape[0], total.shape[3] // 2
    parts, panels, refs = [], [], list(refs)
    for k, (place, start, stop) in enumerate(sources):
        mine, refs, place = refs[:stop], refs[stop:], place()
        slots = (mine[0].shape[0] - FOOT) // bs
        feet[k] = mine[0][slots * bs :, :].astype(jnp.float32).astype(jnp.int32)
        parts += [(mine[p], k, 2 * p) for p in range(start, stop)]
        panels += [a_ref[place, p] for p in range(start, stop)]
    copy = pltpu.make_async_copy(feet, where, sem)
    copy.start()
    copy.wait()
    low = lax.broadcasted_iota(jnp.int32, (bs, 2 * bs), 1) < bs
    left_side = jnp.concatenate(panels, axis=-1)

    def block(part, slot):
        at = pl.multiple_of(jnp.minimum(slot, slots - 1) * bs, bs)
        return jnp.where(slot < slots, part[pl.ds(at, bs), :], jnp.zeros((bs, 2 * bs), part.dtype))

    def body(g, carry):
        rows = []
        for part, k, r in parts:
            for h in range(2):
                tiles = []
                for q in (2 * g, 2 * g + 1):
                    left = block(part, where[k, r + h, 2 * q])
                    right = block(part, where[k, r + h, 2 * q + 1])
                    if h == 0:
                        right = pltpu.roll(right, bs, 1)
                    else:
                        left = pltpu.roll(left, bs, 1)
                    tiles.append(jnp.where(low, left, right))
                rows.append(jnp.concatenate(tiles, axis=-1))
        sums = jnp.dot(left_side, jnp.concatenate(rows, axis=0), preferred_element_type=jnp.float32)
        for t in range(2):
            piece = sums[:, t * 2 * bs : (t + 1) * 2 * bs]
            if first:
                total[g, t] = piece
            else:
                total[g, t] += piece
        return carry

    lax.fori_loop(0, groups, body, 0, unroll=min(groups, 4))


def first_kernel(sources, a_ref, *refs):
    *parts, total, feet, where, sem = refs
    add_products(a_ref, sources, parts, total, True, feet, where, sem)


def middle_kernel(sources, a_ref, before, *refs):
    *parts, total, feet, where, sem = refs
    add_products(a_ref, sources, parts, total, False, feet, where, sem)


def last_kernel(sources, a_ref, total, cols_hbm, *refs):
    *parts, o_hbm, feet, where, sem, cols_ref, o_ref, cols_sem, sems = refs
    fetch = pltpu.make_async_copy(cols_hbm, cols_ref, cols_sem)
    fetch.start()
    add_products(a_ref, sources, parts, total, False, feet, where, sem)
    fetch.wait()
    rows, slots, bs, _ = o_ref.shape
    half = total.shape[0] * 4
    copies = []
    for i in range(rows):
        for k in range(slots):
            l = within(cols_ref[i, k], half)
            tile = total[l >> 2, (l >> 1) & 1, i * bs : (i + 1) * bs, :].astype(o_ref.dtype)
            tile = jnp.where(l & 1 == 0, tile, pltpu.roll(tile, bs, 1))
            o_ref[i, k] = tile[:, :bs]
            if k % STRIDE == STRIDE - 1 or k == slots - 1:
                some = pl.ds(k // STRIDE * STRIDE, k % STRIDE + 1)
                copies.append(pltpu.make_async_copy(o_ref.at[i, some], o_hbm.at[i, some], sems.at[i, k // STRIDE]))
                copies[-1].start()
    for copy in copies:
        copy.wait()


def product(order, arrived, a, total, out, cols=None):
    hbm, vmem = pl.BlockSpec(memory_space=pl.ANY), pl.BlockSpec(memory_space=VMEM)
    kernel = first_kernel if total is None else middle_kernel if cols is None else last_kernel
    sources = [
        (functools.partial(arrived_from, order, way, steps), start, len(refs)) for way, steps, refs, start in arrived
    ]
    parts = [ref for _, _, refs, _ in arrived for ref in refs]
    feet = (len(arrived), FOOT, parts[0].shape[1])
    scratch = [VMEM(feet, jnp.int32), SMEM(feet, jnp.int32), pltpu.SemaphoreType.DMA]
    arrays, specs = [a], [vmem]
    if total is not None:
        arrays, specs = arrays + [total], specs + [vmem]
    if cols is not None:
        arrays, specs = arrays + [cols], specs + [hbm]
        scratch += [
            SMEM(cols.shape, cols.dtype),
            VMEM(out.shape, out.dtype),
            pltpu.SemaphoreType.DMA,
            pltpu.SemaphoreType.DMA((out.shape[0], -(-out.shape[1] // STRIDE))),
        ]
    return pl.pallas_call(
        functools.partial(kernel, sources),
        out_shape=out,
        in_specs=specs + [vmem] * len(parts),
        out_specs=vmem if cols is None else hbm,
        scratch_shapes=scratch,
        input_output_aliases={1: 0} if total is not None and cols is None else {},
        compiler_params=params(),
        cost_estimate=cost(2 * len(arrived) * a.shape[2] * math.prod(out.shape), 0),
    )(*arrays, *parts)


def local(order, a_vals, b_vals, cols):
    sources = len(order)
    rows, slots, bs, _ = a_vals.shape
    half = sources * rows // 2
    hops = {1: sources // 2, -1: (sources - 1) // 2}

    def ring(way):
        return [
            (order[r] * 2 + c, order[(r + (way if c == 0 else -way)) % sources] * 2 + c)
            for r in range(sources)
            for c in range(2)
        ]

    parts = pack(half, cols, b_vals)
    _, *mine = lax.optimization_barrier((parts[0], a_vals, cols))
    swap = [(0, 1), (1, 0)]
    a_other, others = (lax.ppermute(x, "col", swap) for x in mine)
    a = dense_rows(sources, cols, others, a_vals, a_other)
    total_shape = jax.ShapeDtypeStruct((half // 4, 2, rows * bs, 2 * bs), jnp.float32)
    total = None
    held = {way: parts for way in hops}
    rounds = [[(1, 0, parts, 0)]]
    for step in range(1, hops[1] + 1):
        ways = [way for way in hops if step <= hops[way]]
        for way in ways:
            sent = list(held[way])
            if (step, way) == (1, -1):
                sent = [lax.optimization_barrier((part, others))[0] for part in sent]
            if (step, way) == (2, -1):
                sent[0], _ = lax.optimization_barrier((sent[0], a))
            if step > 2 and way == -1:
                total = product(order, rounds.pop(0), a, total, total_shape)
                sent[0], total = lax.optimization_barrier((sent[0], total))
            held[way] = [lax.ppermute(part, ("row", "col"), ring(way)) for part in sent]
        rounds.append([(way, step, held[way], 0) for way in ways])
    *_, late, last = rounds
    total = product(order, sum(rounds[:-2], late[:1]), a, total, total_shape)
    late = late[1:] + last
    total = product(order, [(*what, refs[:1], 0) for *what, refs, _ in late], a, total, total_shape)
    out = jax.ShapeDtypeStruct(a_vals.shape, a_vals.dtype)
    return product(order, [(*what, refs, 1) for *what, refs, _ in late], a, total, out, cols)


def ring_order(mesh):
    count = mesh.shape["row"]
    coords = [getattr(d, "coords", None) for d in mesh.devices[0, :, 0]]
    loop = [*range(0, count, 2), *range(count - 1 - count % 2, 0, -2)]
    if None not in coords:
        steps = [
            sum(abs(x - y) for x, y in zip(coords[loop[k - 1]], coords[loop[k]]))
            for k in range(count)
        ]
        if max(steps) <= 1:
            return loop
    return list(range(count))


def solution(mesh):
    return jax.shard_map(
        functools.partial(local, ring_order(mesh)),
        mesh=mesh,
        in_specs=(
            P(("groups", "row"), "col", None, None),
            P(("groups", "row"), "col", None, None),
            P(("groups", "row"), "col"),
        ),
        out_specs=P(("groups", "row"), "col", None, None),
        check_vma=False,
    )
```

```python
import functools
import math

import jax
import jax.numpy as jnp
import numpy as np
from jax import lax
from jax.experimental import pallas as pl
from jax.experimental.pallas import tpu as pltpu
from jax.sharding import PartitionSpec as P

VMEM = pltpu.VMEM
SMEM = pltpu.SMEM
LIMIT = 48 * 1024 * 1024
STRIDE = 2
FOOT = 16


def params():
    return pltpu.CompilerParams(vmem_limit_bytes=LIMIT)


def within(col, half):
    return jnp.where(col >= half, col - half, col)


def cost(flops, size):
    return pl.CostEstimate(flops=flops, bytes_accessed=size, transcendentals=0)


def pack_kernel(half, cols_hbm, b_hbm, *refs):
    *o_refs, cols_ref, b_ref, sem, sems = refs
    rows, slots, bs, _ = b_ref.shape
    fetch = pltpu.make_async_copy(cols_hbm, cols_ref, sem)
    fetch.start()
    copies = {}
    for r in range(rows):
        for k in range(0, slots, STRIDE):
            some = pl.ds(k, min(STRIDE, slots - k))
            copies[r, k] = pltpu.make_async_copy(b_hbm.at[r, some], b_ref.at[r, some], sems.at[r, k // STRIDE])
            copies[r, k].start()
    row = lax.broadcasted_iota(jnp.int32, (FOOT, 2 * bs), 0)
    lane = lax.broadcasted_iota(jnp.int32, (FOOT, 2 * bs), 1)
    fetch.wait()
    foot = jnp.full((FOOT, 2 * bs), slots, jnp.int32)
    for r in range(rows):
        for n in range(slots):
            here = (row == r) & (lane == within(cols_ref[r, n], half))
            foot = jnp.where(here, n, foot)
    o_refs[0][slots * bs :, :] = foot.astype(jnp.float32).astype(b_ref.dtype)
    for p, o_ref in enumerate(o_refs):
        for n in range(slots):
            if n % STRIDE == 0:
                copies[2 * p, n].wait()
                copies[2 * p + 1, n].wait()
            o_ref[n * bs : (n + 1) * bs, :] = jnp.concatenate([b_ref[2 * p, n], b_ref[2 * p + 1, n]], axis=-1)


def pack(half, cols, b_vals):
    rows, slots, bs, _ = b_vals.shape
    shapes = [(slots * bs + (FOOT if p == 0 else 0), 2 * bs) for p in range(rows // 2)]
    cols, b_vals = (pltpu.with_memory_space_constraint(x, pltpu.HBM) for x in (cols, b_vals))
    return pl.pallas_call(
        functools.partial(pack_kernel, half),
        out_shape=[jax.ShapeDtypeStruct(shape, b_vals.dtype) for shape in shapes],
        in_specs=[pl.BlockSpec(memory_space=pl.ANY)] * 2,
        out_specs=[pl.BlockSpec(memory_space=VMEM)] * len(shapes),
        scratch_shapes=[
            SMEM(cols.shape, cols.dtype),
            VMEM(b_vals.shape, b_vals.dtype),
            pltpu.SemaphoreType.DMA,
            pltpu.SemaphoreType.DMA((rows, -(-slots // STRIDE))),
        ],
        compiler_params=params(),
        cost_estimate=cost(0, 2 * b_vals.size * 2),
    )(cols, b_vals)


def dense_kernel(cols_ref, others_ref, own_ref, other_ref, o_ref, blocks, where):
    rows, slots, bs, _ = own_ref.shape
    sources, pairs = o_ref.shape[:2]
    blocks[:, :slots] = own_ref[...]
    blocks[:, slots : 2 * slots] = other_ref[...]
    blocks[:, 2 * slots] = jnp.zeros_like(blocks[:, 2 * slots])
    for i in range(rows):
        def clear(j, carry):
            where[i, j] = 2 * slots
            return carry

        lax.fori_loop(0, 2 * sources * pairs, clear, 0, unroll=8)
        for m in range(slots):
            where[i, cols_ref[i, m]] = m
            where[i, others_ref[i, m]] = slots + m

    def body(s, carry):
        for p in range(pairs):
            j = (s * pairs + p) * 2
            for i in range(rows):
                left = blocks[i, where[i, j]]
                right = blocks[i, where[i, j + 1]]
                o_ref[s, p, i * bs : (i + 1) * bs, :] = jnp.concatenate([left, right], axis=-1)
        return carry

    lax.fori_loop(0, sources, body, 0, unroll=2)


def dense_rows(sources, cols, others, own, other):
    rows, slots, bs, _ = own.shape
    return pl.pallas_call(
        dense_kernel,
        out_shape=jax.ShapeDtypeStruct((sources, rows // 2, rows * bs, 2 * bs), own.dtype),
        grid_spec=pltpu.PrefetchScalarGridSpec(
            num_scalar_prefetch=2,
            grid=(),
            in_specs=[pl.BlockSpec(memory_space=VMEM)] * 2,
            out_specs=pl.BlockSpec(memory_space=VMEM),
            scratch_shapes=[
                VMEM((rows, 2 * slots + 1, bs, bs), own.dtype),
                SMEM((rows, sources * rows), jnp.int32),
            ],
        ),
        compiler_params=params(),
        cost_estimate=cost(0, 8 * own.size),
    )(cols, others, own, other)


def look_up(table, k):
    value = jnp.int32(table[0])
    for n, entry in enumerate(table[1:], 1):
        value = jnp.where(k == n, entry, value)
    return value


def arrived_from(order, way, steps):
    spots = [order.index(r) for r in range(len(order))]
    ahead = jnp.where(lax.axis_index("col") == 0, way, -way) * steps
    return look_up(order, lax.rem(look_up(spots, lax.axis_index("row")) - ahead + len(order), len(order)))


def add_products(a_ref, sources, refs, total, first, feet, where, sem):
    groups, bs = total.shape[0], total.shape[3] // 2
    parts, panels, refs = [], [], list(refs)
    for k, (place, start, stop) in enumerate(sources):
        mine, refs, place = refs[:stop], refs[stop:], place()
        slots = (mine[0].shape[0] - FOOT) // bs
        feet[k] = mine[0][slots * bs :, :].astype(jnp.float32).astype(jnp.int32)
        parts += [(mine[p], k, 2 * p) for p in range(start, stop)]
        panels += [a_ref[place, p] for p in range(start, stop)]
    copy = pltpu.make_async_copy(feet, where, sem)
    copy.start()
    copy.wait()
    low = lax.broadcasted_iota(jnp.int32, (bs, 2 * bs), 1) < bs
    left_side = jnp.concatenate(panels, axis=-1)

    def block(part, slot):
        at = pl.multiple_of(jnp.minimum(slot, slots - 1) * bs, bs)
        return jnp.where(slot < slots, part[pl.ds(at, bs), :], jnp.zeros((bs, 2 * bs), part.dtype))

    def body(g, carry):
        rows = []
        for part, k, r in parts:
            for h in range(2):
                tiles = []
                for q in (2 * g, 2 * g + 1):
                    left = block(part, where[k, r + h, 2 * q])
                    right = block(part, where[k, r + h, 2 * q + 1])
                    if h == 0:
                        right = pltpu.roll(right, bs, 1)
                    else:
                        left = pltpu.roll(left, bs, 1)
                    tiles.append(jnp.where(low, left, right))
                rows.append(jnp.concatenate(tiles, axis=-1))
        sums = jnp.dot(left_side, jnp.concatenate(rows, axis=0), preferred_element_type=jnp.float32)
        for t in range(2):
            piece = sums[:, t * 2 * bs : (t + 1) * 2 * bs]
            if first:
                total[g, t] = piece
            else:
                total[g, t] += piece
        return carry

    lax.fori_loop(0, groups, body, 0, unroll=min(groups, 4))


def first_kernel(sources, a_ref, *refs):
    *parts, total, feet, where, sem = refs
    add_products(a_ref, sources, parts, total, True, feet, where, sem)


def middle_kernel(sources, a_ref, before, *refs):
    *parts, total, feet, where, sem = refs
    add_products(a_ref, sources, parts, total, False, feet, where, sem)


def last_kernel(sources, a_ref, total, cols_hbm, *refs):
    *parts, o_hbm, feet, where, sem, cols_ref, o_ref, cols_sem, sems = refs
    fetch = pltpu.make_async_copy(cols_hbm, cols_ref, cols_sem)
    fetch.start()
    add_products(a_ref, sources, parts, total, False, feet, where, sem)
    fetch.wait()
    rows, slots, bs, _ = o_ref.shape
    half = total.shape[0] * 4
    copies = []
    for i in range(rows):
        for k in range(slots):
            l = within(cols_ref[i, k], half)
            tile = total[l >> 2, (l >> 1) & 1, i * bs : (i + 1) * bs, :].astype(o_ref.dtype)
            tile = jnp.where(l & 1 == 0, tile, pltpu.roll(tile, bs, 1))
            o_ref[i, k] = tile[:, :bs]
            if k % STRIDE == STRIDE - 1 or k == slots - 1:
                some = pl.ds(k // STRIDE * STRIDE, k % STRIDE + 1)
                copies.append(pltpu.make_async_copy(o_ref.at[i, some], o_hbm.at[i, some], sems.at[i, k // STRIDE]))
                copies[-1].start()
    for copy in copies:
        copy.wait()


def product(order, arrived, a, total, out, cols=None):
    hbm, vmem = pl.BlockSpec(memory_space=pl.ANY), pl.BlockSpec(memory_space=VMEM)
    kernel = first_kernel if total is None else middle_kernel if cols is None else last_kernel
    sources = [
        (functools.partial(arrived_from, order, way, steps), start, len(refs)) for way, steps, refs, start in arrived
    ]
    parts = [ref for _, _, refs, _ in arrived for ref in refs]
    feet = (len(arrived), FOOT, parts[0].shape[1])
    scratch = [VMEM(feet, jnp.int32), SMEM(feet, jnp.int32), pltpu.SemaphoreType.DMA]
    arrays, specs = [a], [vmem]
    if total is not None:
        arrays, specs = arrays + [total], specs + [vmem]
    if cols is not None:
        arrays, specs = arrays + [cols], specs + [hbm]
        scratch += [
            SMEM(cols.shape, cols.dtype),
            VMEM(out.shape, out.dtype),
            pltpu.SemaphoreType.DMA,
            pltpu.SemaphoreType.DMA((out.shape[0], -(-out.shape[1] // STRIDE))),
        ]
    return pl.pallas_call(
        functools.partial(kernel, sources),
        out_shape=out,
        in_specs=specs + [vmem] * len(parts),
        out_specs=vmem if cols is None else hbm,
        scratch_shapes=scratch,
        input_output_aliases={1: 0} if total is not None and cols is None else {},
        compiler_params=params(),
        cost_estimate=cost(2 * len(arrived) * a.shape[2] * math.prod(out.shape), 0),
    )(*arrays, *parts)


def local(order, a_vals, b_vals, cols):
    sources = len(order)
    rows, slots, bs, _ = a_vals.shape
    half = sources * rows // 2
    hops = {1: sources // 2, -1: (sources - 1) // 2}

    def ring(way):
        return [
            (order[r] * 2 + c, order[(r + (way if c == 0 else -way)) % sources] * 2 + c)
            for r in range(sources)
            for c in range(2)
        ]

    parts = pack(half, cols, b_vals)
    _, *mine = lax.optimization_barrier((parts[0], a_vals, cols))
    swap = [(0, 1), (1, 0)]
    a_other, others = (lax.ppermute(x, "col", swap) for x in mine)
    a = dense_rows(sources, cols, others, a_vals, a_other)
    total_shape = jax.ShapeDtypeStruct((half // 4, 2, rows * bs, 2 * bs), jnp.float32)
    total = None
    held = {way: parts for way in hops}
    rounds = [[(1, 0, parts, 0)]]
    for step in range(1, hops[1] + 1):
        ways = [way for way in hops if step <= hops[way]]
        for way in ways:
            sent = list(held[way])
            if (step, way) == (1, -1):
                sent = [lax.optimization_barrier((part, others))[0] for part in sent]
            if (step, way) == (2, -1):
                sent[0], _ = lax.optimization_barrier((sent[0], a))
            if step > 2 and way == -1:
                total = product(order, rounds.pop(0), a, total, total_shape)
                sent[0], total = lax.optimization_barrier((sent[0], total))
            held[way] = [lax.ppermute(part, ("row", "col"), ring(way)) for part in sent]
        rounds.append([(way, step, held[way], 0) for way in ways])
    *_, late, last = rounds
    total = product(order, sum(rounds[:-2], late[:1]), a, total, total_shape)
    late = late[1:] + last
    total = product(order, [(*what, refs[:1], 0) for *what, refs, _ in late], a, total, total_shape)
    out = jax.ShapeDtypeStruct(a_vals.shape, a_vals.dtype)
    return product(order, [(*what, refs, 1) for *what, refs, _ in late], a, total, out, cols)


def ring_order(mesh):
    count = mesh.shape["row"]
    coords = [getattr(d, "coords", None) for d in mesh.devices[0, :, 0]]
    loop = [*range(0, count, 2), *range(count - 1 - count % 2, 0, -2)]
    if None not in coords:
        steps = [
            sum(abs(x - y) for x, y in zip(coords[loop[k - 1]], coords[loop[k]]))
            for k in range(count)
        ]
        if max(steps) <= 1:
            return loop
    return list(range(count))


def solution(mesh):
    return jax.shard_map(
        functools.partial(local, ring_order(mesh)),
        mesh=mesh,
        in_specs=(
            P(("groups", "row"), "col", None, None),
            P(("groups", "row"), "col", None, None),
            P(("groups", "row"), "col"),
        ),
        out_specs=P(("groups", "row"), "col", None, None),
        check_vma=False,
    )
```

```python
import functools
import math

import jax
import jax.numpy as jnp
from jax import lax
from jax.experimental import pallas as pl
from jax.experimental.pallas import tpu as pltpu
from jax.sharding import PartitionSpec as P

VMEM = pltpu.VMEM
SMEM = pltpu.SMEM
LIMIT = 48 * 1024 * 1024
STRIDE = 5
FOOT = 16


def params():
    return pltpu.CompilerParams(vmem_limit_bytes=LIMIT)


def within(col, half):
    return jnp.where(col >= half, col - half, col)


def cost(flops, size):
    return pl.CostEstimate(flops=flops, bytes_accessed=size, transcendentals=0)


def pack_kernel(half, cols_hbm, b_hbm, *refs):
    *o_refs, cols_ref, b_ref, sem, sems = refs
    rows, slots, bs, _ = b_ref.shape
    pairs = [pl.ds(2 * p, 2) for p in range(rows // 2)]
    copies = [pltpu.make_async_copy(b_hbm.at[pair], b_ref.at[pair], sems.at[p]) for p, pair in enumerate(pairs)]
    fetch = pltpu.make_async_copy(cols_hbm, cols_ref, sem)
    fetch.start()
    for copy in copies:
        copy.start()
    row = lax.broadcasted_iota(jnp.int32, (FOOT, 2 * bs), 0)
    lane = lax.broadcasted_iota(jnp.int32, (FOOT, 2 * bs), 1)
    fetch.wait()
    foot = jnp.full((FOOT, 2 * bs), slots, jnp.int32)
    for r in range(rows):
        for n in range(slots):
            here = (row == r) & (lane == within(cols_ref[r, n], half))
            foot = jnp.where(here, n, foot)
    o_refs[0][slots * bs :, :] = foot.astype(jnp.float32).astype(b_ref.dtype)
    for p, o_ref in enumerate(o_refs):
        copies[p].wait()
        for n in range(slots):
            o_ref[n * bs : (n + 1) * bs, :] = jnp.concatenate([b_ref[2 * p, n], b_ref[2 * p + 1, n]], axis=-1)


def pack(half, cols, b_vals):
    rows, slots, bs, _ = b_vals.shape
    shapes = [(slots * bs + (FOOT if p == 0 else 0), 2 * bs) for p in range(rows // 2)]
    cols, b_vals = (pltpu.with_memory_space_constraint(x, pltpu.HBM) for x in (cols, b_vals))
    return pl.pallas_call(
        functools.partial(pack_kernel, half),
        out_shape=[jax.ShapeDtypeStruct(shape, b_vals.dtype) for shape in shapes],
        in_specs=[pl.BlockSpec(memory_space=pl.ANY)] * 2,
        out_specs=[pl.BlockSpec(memory_space=VMEM)] * len(shapes),
        scratch_shapes=[
            SMEM(cols.shape, cols.dtype),
            VMEM(b_vals.shape, b_vals.dtype),
            pltpu.SemaphoreType.DMA,
            pltpu.SemaphoreType.DMA((rows // 2,)),
        ],
        compiler_params=params(),
        cost_estimate=cost(0, 2 * b_vals.size * 2),
    )(cols, b_vals)


def dense_kernel(cols_ref, others_ref, own_ref, other_ref, o_ref, blocks, where):
    rows, slots, bs, _ = own_ref.shape
    sources, pairs = o_ref.shape[:2]
    blocks[:, :slots] = own_ref[...]
    blocks[:, slots : 2 * slots] = other_ref[...]
    blocks[:, 2 * slots] = jnp.zeros_like(blocks[:, 2 * slots])
    for i in range(rows):
        def clear(j, carry):
            where[i, j] = 2 * slots
            return carry

        lax.fori_loop(0, 2 * sources * pairs, clear, 0, unroll=8)
        for m in range(slots):
            where[i, cols_ref[i, m]] = m
            where[i, others_ref[i, m]] = slots + m

    def body(s, carry):
        for p in range(pairs):
            j = (s * pairs + p) * 2
            for i in range(rows):
                left = blocks[i, where[i, j]]
                right = blocks[i, where[i, j + 1]]
                o_ref[s, p, i * bs : (i + 1) * bs, :] = jnp.concatenate([left, right], axis=-1)
        return carry

    lax.fori_loop(0, sources, body, 0, unroll=2)


def dense_rows(sources, cols, others, own, other):
    rows, slots, bs, _ = own.shape
    return pl.pallas_call(
        dense_kernel,
        out_shape=jax.ShapeDtypeStruct((sources, rows // 2, rows * bs, 2 * bs), own.dtype),
        grid_spec=pltpu.PrefetchScalarGridSpec(
            num_scalar_prefetch=2,
            grid=(),
            in_specs=[pl.BlockSpec(memory_space=VMEM)] * 2,
            out_specs=pl.BlockSpec(memory_space=VMEM),
            scratch_shapes=[
                VMEM((rows, 2 * slots + 1, bs, bs), own.dtype),
                SMEM((rows, sources * rows), jnp.int32),
            ],
        ),
        compiler_params=params(),
        cost_estimate=cost(0, 8 * own.size),
    )(cols, others, own, other)


def look_up(table, k):
    value = jnp.int32(table[0])
    for n, entry in enumerate(table[1:], 1):
        value = jnp.where(k == n, entry, value)
    return value


def arrived_from(order, way, steps):
    spots = [order.index(r) for r in range(len(order))]
    ahead = jnp.where(lax.axis_index("col") == 1, way, -way) * steps
    return look_up(order, lax.rem(look_up(spots, lax.axis_index("row")) - ahead + len(order), len(order)))


def add_products(a_ref, sources, refs, total, first, feet, where, sem):
    groups, bs = total.shape[0], total.shape[3] // 2
    parts, panels, refs = [], [], list(refs)
    for k, (place, start, stop) in enumerate(sources):
        mine, refs, place = refs[:stop], refs[stop:], place()
        slots = (mine[0].shape[0] - FOOT) // bs
        feet[k] = mine[0][slots * bs :, :].astype(jnp.float32).astype(jnp.int32)
        parts += [(mine[p], k, 2 * p) for p in range(start, stop)]
        panels += [a_ref[place, p] for p in range(start, stop)]
    copy = pltpu.make_async_copy(feet, where, sem)
    copy.start()
    copy.wait()
    low = lax.broadcasted_iota(jnp.int32, (bs, 2 * bs), 1) < bs
    left_side = jnp.concatenate(panels, axis=-1)

    def block(part, slot):
        at = pl.multiple_of(jnp.minimum(slot, slots - 1) * bs, bs)
        return jnp.where(slot < slots, part[pl.ds(at, bs), :], jnp.zeros((bs, 2 * bs), part.dtype))

    def body(g, carry):
        rows = []
        for part, k, r in parts:
            for h in range(2):
                tiles = []
                for q in (2 * g, 2 * g + 1):
                    left = block(part, where[k, r + h, 2 * q])
                    right = block(part, where[k, r + h, 2 * q + 1])
                    if h == 0:
                        right = pltpu.roll(right, bs, 1)
                    else:
                        left = pltpu.roll(left, bs, 1)
                    tiles.append(jnp.where(low, left, right))
                rows.append(jnp.concatenate(tiles, axis=-1))
        sums = jnp.dot(left_side, jnp.concatenate(rows, axis=0), preferred_element_type=jnp.float32)
        for t in range(2):
            piece = sums[:, t * 2 * bs : (t + 1) * 2 * bs]
            if first:
                total[g, t] = piece
            else:
                total[g, t] += piece
        return carry

    lax.fori_loop(0, groups, body, 0, unroll=min(groups, 4))


def first_kernel(sources, a_ref, *refs):
    *parts, total, feet, where, sem = refs
    add_products(a_ref, sources, parts, total, True, feet, where, sem)


def middle_kernel(sources, a_ref, before, *refs):
    *parts, total, feet, where, sem = refs
    add_products(a_ref, sources, parts, total, False, feet, where, sem)


def last_kernel(sources, a_ref, total, cols_hbm, *refs):
    *parts, o_hbm, feet, where, sem, cols_ref, o_ref, cols_sem, sems = refs
    fetch = pltpu.make_async_copy(cols_hbm, cols_ref, cols_sem)
    fetch.start()
    add_products(a_ref, sources, parts, total, False, feet, where, sem)
    fetch.wait()
    rows, slots, bs, _ = o_ref.shape
    half = total.shape[0] * 4
    copies = []
    for i in range(rows):
        for k in range(slots):
            l = within(cols_ref[i, k], half)
            tile = total[l >> 2, (l >> 1) & 1, i * bs : (i + 1) * bs, :].astype(o_ref.dtype)
            tile = jnp.where(l & 1 == 0, tile, pltpu.roll(tile, bs, 1))
            o_ref[i, k] = tile[:, :bs]
            if k % STRIDE == STRIDE - 1 or k == slots - 1:
                some = pl.ds(k // STRIDE * STRIDE, k % STRIDE + 1)
                copies.append(pltpu.make_async_copy(o_ref.at[i, some], o_hbm.at[i, some], sems.at[i, k // STRIDE]))
                copies[-1].start()
    for copy in copies:
        copy.wait()


def product(order, arrived, a, total, out, cols=None):
    hbm, vmem = pl.BlockSpec(memory_space=pl.ANY), pl.BlockSpec(memory_space=VMEM)
    kernel = first_kernel if total is None else middle_kernel if cols is None else last_kernel
    sources = [
        (functools.partial(arrived_from, order, way, steps), start, len(refs)) for way, steps, refs, start in arrived
    ]
    parts = [ref for _, _, refs, _ in arrived for ref in refs]
    feet = (len(arrived), FOOT, parts[0].shape[1])
    scratch = [VMEM(feet, jnp.int32), SMEM(feet, jnp.int32), pltpu.SemaphoreType.DMA]
    arrays, specs = [a], [vmem]
    if total is not None:
        arrays, specs = arrays + [total], specs + [vmem]
    if cols is not None:
        arrays, specs = arrays + [cols], specs + [hbm]
        scratch += [
            SMEM(cols.shape, cols.dtype),
            VMEM(out.shape, out.dtype),
            pltpu.SemaphoreType.DMA,
            pltpu.SemaphoreType.DMA((out.shape[0], -(-out.shape[1] // STRIDE))),
        ]
    return pl.pallas_call(
        functools.partial(kernel, sources),
        out_shape=out,
        in_specs=specs + [vmem] * len(parts),
        out_specs=vmem if cols is None else hbm,
        scratch_shapes=scratch,
        input_output_aliases={1: 0} if total is not None and cols is None else {},
        compiler_params=params(),
        cost_estimate=cost(2 * len(arrived) * a.shape[2] * math.prod(out.shape), 0),
    )(*arrays, *parts)


def local(order, a_vals, b_vals, cols):
    sources = len(order)
    rows, slots, bs, _ = a_vals.shape
    half = sources * rows // 2
    hops = {1: sources // 2, -1: (sources - 1) // 2}

    def ring(way):
        return [
            (order[r] * 2 + c, order[(r + (way if c == 1 else -way)) % sources] * 2 + c)
            for r in range(sources)
            for c in range(2)
        ]

    parts = pack(half, cols, b_vals)
    _, *mine = lax.optimization_barrier((parts[0], a_vals, cols))
    swap = [(0, 1), (1, 0)]
    a_other, others = (lax.ppermute(x, "col", swap) for x in mine)
    a = dense_rows(sources, cols, others, a_vals, a_other)
    total_shape = jax.ShapeDtypeStruct((half // 4, 2, rows * bs, 2 * bs), jnp.float32)
    total = None
    held = {way: parts for way in hops}
    rounds = [[(1, 0, parts, 0)]]
    for step in range(1, hops[1] + 1):
        ways = [way for way in hops if step <= hops[way]]
        for way in ways:
            sent = list(held[way])
            if (step, way) == (1, -1):
                sent = [lax.optimization_barrier((part, others))[0] for part in sent]
            if (step, way) == (2, -1):
                sent[0], _ = lax.optimization_barrier((sent[0], a))
            if step > 2 and way == -1:
                total = product(order, rounds.pop(0), a, total, total_shape)
                sent[0], total = lax.optimization_barrier((sent[0], total))
            held[way] = [lax.ppermute(part, ("row", "col"), ring(way)) for part in sent]
        rounds.append([(way, step, held[way], 0) for way in ways])
    *_, late, last = rounds
    total = product(order, sum(rounds[:-2], late[:1]), a, total, total_shape)
    late = late[1:] + last
    total = product(order, [(*what, refs[:1], 0) for *what, refs, _ in late], a, total, total_shape)
    out = jax.ShapeDtypeStruct(a_vals.shape, a_vals.dtype)
    return product(order, [(*what, refs, 1) for *what, refs, _ in late], a, total, out, cols)


def ring_order(mesh):
    count = mesh.shape["row"]
    coords = [getattr(d, "coords", None) for d in mesh.devices[0, :, 0]]
    loop = [*range(0, count, 2), *range(count - 1 - count % 2, 0, -2)]
    if None not in coords:
        steps = [
            sum(abs(x - y) for x, y in zip(coords[loop[k - 1]], coords[loop[k]]))
            for k in range(count)
        ]
        if max(steps) <= 1:
            return loop
    return list(range(count))


def solution(mesh):
    return jax.shard_map(
        functools.partial(local, ring_order(mesh)),
        mesh=mesh,
        in_specs=(
            P(("groups", "row"), "col", None, None),
            P(("groups", "row"), "col", None, None),
            P(("groups", "row"), "col"),
        ),
        out_specs=P(("groups", "row"), "col", None, None),
        check_vma=False,
    )
```

```python
import functools
import math

import jax
import jax.numpy as jnp
from jax import lax
from jax.experimental import pallas as pl
from jax.experimental.pallas import tpu as pltpu
from jax.sharding import PartitionSpec as P

VMEM = pltpu.VMEM
SMEM = pltpu.SMEM
LIMIT = 48 * 1024 * 1024
STRIDE = 5
FOOT = 16


def params():
    return pltpu.CompilerParams(vmem_limit_bytes=LIMIT)


def within(col, half):
    return jnp.where(col >= half, col - half, col)


def cost(flops, size):
    return pl.CostEstimate(flops=flops, bytes_accessed=size, transcendentals=0)


def pack_kernel(half, cols_hbm, b_hbm, *refs):
    *o_refs, cols_ref, b_ref, sem, sems = refs
    rows, slots, bs, _ = b_ref.shape
    pairs = [pl.ds(2 * p, 2) for p in range(rows // 2)]
    copies = [pltpu.make_async_copy(b_hbm.at[pair], b_ref.at[pair], sems.at[p]) for p, pair in enumerate(pairs)]
    fetch = pltpu.make_async_copy(cols_hbm, cols_ref, sem)
    fetch.start()
    for copy in copies:
        copy.start()
    row = lax.broadcasted_iota(jnp.int32, (FOOT, 2 * bs), 0)
    lane = lax.broadcasted_iota(jnp.int32, (FOOT, 2 * bs), 1)
    fetch.wait()
    foot = jnp.full((FOOT, 2 * bs), slots, jnp.int32)
    for r in range(rows):
        for n in range(slots):
            here = (row == r) & (lane == within(cols_ref[r, n], half))
            foot = jnp.where(here, n, foot)
    o_refs[0][slots * bs :, :] = foot.astype(jnp.float32).astype(b_ref.dtype)
    for p, o_ref in enumerate(o_refs):
        copies[p].wait()
        for n in range(slots):
            o_ref[n * bs : (n + 1) * bs, :] = jnp.concatenate([b_ref[2 * p, n], b_ref[2 * p + 1, n]], axis=-1)


def pack(half, cols, b_vals):
    rows, slots, bs, _ = b_vals.shape
    shapes = [(slots * bs + (FOOT if p == 0 else 0), 2 * bs) for p in range(rows // 2)]
    cols, b_vals = (pltpu.with_memory_space_constraint(x, pltpu.HBM) for x in (cols, b_vals))
    return pl.pallas_call(
        functools.partial(pack_kernel, half),
        out_shape=[jax.ShapeDtypeStruct(shape, b_vals.dtype) for shape in shapes],
        in_specs=[pl.BlockSpec(memory_space=pl.ANY)] * 2,
        out_specs=[pl.BlockSpec(memory_space=VMEM)] * len(shapes),
        scratch_shapes=[
            SMEM(cols.shape, cols.dtype),
            VMEM(b_vals.shape, b_vals.dtype),
            pltpu.SemaphoreType.DMA,
            pltpu.SemaphoreType.DMA((rows // 2,)),
        ],
        compiler_params=params(),
        cost_estimate=cost(0, 2 * b_vals.size * 2),
    )(cols, b_vals)


def dense_kernel(cols_ref, others_ref, own_ref, other_ref, o_ref, blocks, where):
    rows, slots, bs, _ = own_ref.shape
    sources, pairs = o_ref.shape[:2]
    blocks[:, :slots] = own_ref[...]
    blocks[:, slots : 2 * slots] = other_ref[...]
    blocks[:, 2 * slots] = jnp.zeros_like(blocks[:, 2 * slots])
    for i in range(rows):
        def clear(j, carry):
            where[i, j] = 2 * slots
            return carry

        lax.fori_loop(0, 2 * sources * pairs, clear, 0, unroll=8)
        for m in range(slots):
            where[i, cols_ref[i, m]] = m
            where[i, others_ref[i, m]] = slots + m

    def body(s, carry):
        for p in range(pairs):
            j = (s * pairs + p) * 2
            for i in range(rows):
                left = blocks[i, where[i, j]]
                right = blocks[i, where[i, j + 1]]
                o_ref[s, p, i * bs : (i + 1) * bs, :] = jnp.concatenate([left, right], axis=-1)
        return carry

    lax.fori_loop(0, sources, body, 0, unroll=2)


def dense_rows(sources, cols, others, own, other):
    rows, slots, bs, _ = own.shape
    return pl.pallas_call(
        dense_kernel,
        out_shape=jax.ShapeDtypeStruct((sources, rows // 2, rows * bs, 2 * bs), own.dtype),
        grid_spec=pltpu.PrefetchScalarGridSpec(
            num_scalar_prefetch=2,
            grid=(),
            in_specs=[pl.BlockSpec(memory_space=VMEM)] * 2,
            out_specs=pl.BlockSpec(memory_space=VMEM),
            scratch_shapes=[
                VMEM((rows, 2 * slots + 1, bs, bs), own.dtype),
                SMEM((rows, sources * rows), jnp.int32),
            ],
        ),
        compiler_params=params(),
        cost_estimate=cost(0, 8 * own.size),
    )(cols, others, own, other)


def look_up(table, k):
    value = jnp.int32(table[0])
    for n, entry in enumerate(table[1:], 1):
        value = jnp.where(k == n, entry, value)
    return value


def arrived_from(order, way, steps):
    spots = [order.index(r) for r in range(len(order))]
    ahead = jnp.where(lax.axis_index("col") == 1, way, -way) * steps
    return look_up(order, lax.rem(look_up(spots, lax.axis_index("row")) - ahead + len(order), len(order)))


def add_products(a_ref, sources, refs, total, first, feet, where, sem):
    groups, bs = total.shape[0], total.shape[3] // 2
    parts, panels, refs = [], [], list(refs)
    for k, (place, start, stop) in enumerate(sources):
        mine, refs, place = refs[:stop], refs[stop:], place()
        slots = (mine[0].shape[0] - FOOT) // bs
        feet[k] = mine[0][slots * bs :, :].astype(jnp.float32).astype(jnp.int32)
        parts += [(mine[p], k, 2 * p) for p in range(start, stop)]
        panels += [a_ref[place, p] for p in range(start, stop)]
    copy = pltpu.make_async_copy(feet, where, sem)
    copy.start()
    copy.wait()
    low = lax.broadcasted_iota(jnp.int32, (bs, 2 * bs), 1) < bs
    left_side = jnp.concatenate(panels, axis=-1)

    def block(part, slot):
        at = pl.multiple_of(jnp.minimum(slot, slots - 1) * bs, bs)
        return jnp.where(slot < slots, part[pl.ds(at, bs), :], jnp.zeros((bs, 2 * bs), part.dtype))

    def body(g, carry):
        rows = []
        for part, k, r in parts:
            for h in range(2):
                tiles = []
                for q in (2 * g, 2 * g + 1):
                    left = block(part, where[k, r + h, 2 * q])
                    right = block(part, where[k, r + h, 2 * q + 1])
                    if h == 0:
                        right = pltpu.roll(right, bs, 1)
                    else:
                        left = pltpu.roll(left, bs, 1)
                    tiles.append(jnp.where(low, left, right))
                rows.append(jnp.concatenate(tiles, axis=-1))
        sums = jnp.dot(left_side, jnp.concatenate(rows, axis=0), preferred_element_type=jnp.float32)
        for t in range(2):
            piece = sums[:, t * 2 * bs : (t + 1) * 2 * bs]
            if first:
                total[g, t] = piece
            else:
                total[g, t] += piece
        return carry

    lax.fori_loop(0, groups, body, 0, unroll=min(groups, 4))


def first_kernel(sources, a_ref, *refs):
    *parts, total, feet, where, sem = refs
    add_products(a_ref, sources, parts, total, True, feet, where, sem)


def middle_kernel(sources, a_ref, before, *refs):
    *parts, total, feet, where, sem = refs
    add_products(a_ref, sources, parts, total, False, feet, where, sem)


def last_kernel(sources, a_ref, total, cols_hbm, *refs):
    *parts, o_hbm, feet, where, sem, cols_ref, o_ref, cols_sem, sems = refs
    fetch = pltpu.make_async_copy(cols_hbm, cols_ref, cols_sem)
    fetch.start()
    add_products(a_ref, sources, parts, total, False, feet, where, sem)
    fetch.wait()
    rows, slots, bs, _ = o_ref.shape
    half = total.shape[0] * 4
    copies = []
    for i in range(rows):
        for k in range(slots):
            l = within(cols_ref[i, k], half)
            tile = total[l >> 2, (l >> 1) & 1, i * bs : (i + 1) * bs, :].astype(o_ref.dtype)
            tile = jnp.where(l & 1 == 0, tile, pltpu.roll(tile, bs, 1))
            o_ref[i, k] = tile[:, :bs]
            if k % STRIDE == STRIDE - 1 or k == slots - 1:
                some = pl.ds(k // STRIDE * STRIDE, k % STRIDE + 1)
                copies.append(pltpu.make_async_copy(o_ref.at[i, some], o_hbm.at[i, some], sems.at[i, k // STRIDE]))
                copies[-1].start()
    for copy in copies:
        copy.wait()


def product(order, arrived, a, total, out, cols=None):
    hbm, vmem = pl.BlockSpec(memory_space=pl.ANY), pl.BlockSpec(memory_space=VMEM)
    kernel = first_kernel if total is None else middle_kernel if cols is None else last_kernel
    sources = [
        (functools.partial(arrived_from, order, way, steps), start, len(refs)) for way, steps, refs, start in arrived
    ]
    parts = [ref for _, _, refs, _ in arrived for ref in refs]
    feet = (len(arrived), FOOT, parts[0].shape[1])
    scratch = [VMEM(feet, jnp.int32), SMEM(feet, jnp.int32), pltpu.SemaphoreType.DMA]
    arrays, specs = [a], [vmem]
    if total is not None:
        arrays, specs = arrays + [total], specs + [vmem]
    if cols is not None:
        arrays, specs = arrays + [cols], specs + [hbm]
        scratch += [
            SMEM(cols.shape, cols.dtype),
            VMEM(out.shape, out.dtype),
            pltpu.SemaphoreType.DMA,
            pltpu.SemaphoreType.DMA((out.shape[0], -(-out.shape[1] // STRIDE))),
        ]
    return pl.pallas_call(
        functools.partial(kernel, sources),
        out_shape=out,
        in_specs=specs + [vmem] * len(parts),
        out_specs=vmem if cols is None else hbm,
        scratch_shapes=scratch,
        input_output_aliases={1: 0} if total is not None and cols is None else {},
        compiler_params=params(),
        cost_estimate=cost(2 * len(arrived) * a.shape[2] * math.prod(out.shape), 0),
    )(*arrays, *parts)


def local(order, a_vals, b_vals, cols):
    sources = len(order)
    rows, slots, bs, _ = a_vals.shape
    half = sources * rows // 2
    hops = {1: sources // 2, -1: (sources - 1) // 2}

    def ring(way):
        return [
            (order[r] * 2 + c, order[(r + (way if c == 1 else -way)) % sources] * 2 + c)
            for r in range(sources)
            for c in range(2)
        ]

    parts = pack(half, cols, b_vals)
    _, *mine = lax.optimization_barrier((parts[0], a_vals, cols))
    swap = [(0, 1), (1, 0)]
    a_other, others = (lax.ppermute(x, "col", swap) for x in mine)
    a = dense_rows(sources, cols, others, a_vals, a_other)
    total_shape = jax.ShapeDtypeStruct((half // 4, 2, rows * bs, 2 * bs), jnp.float32)
    total = None
    held = {way: parts for way in hops}
    rounds = [[(1, 0, parts, 0)]]
    for step in range(1, hops[1] + 1):
        ways = [way for way in hops if step <= hops[way]]
        for way in ways:
            sent = list(held[way])
            if (step, way) == (1, -1):
                sent = [lax.optimization_barrier((part, others))[0] for part in sent]
            if (step, way) == (2, -1):
                sent[0], _ = lax.optimization_barrier((sent[0], a))
            if step > 3 and way == -1:
                total = product(order, rounds.pop(0), a, total, total_shape)
                sent[0], total = lax.optimization_barrier((sent[0], total))
            held[way] = [lax.ppermute(part, ("row", "col"), ring(way)) for part in sent]
        rounds.append([(way, step, held[way], 0) for way in ways])
    *_, late, last = rounds
    total = product(order, sum(rounds[:-2], late[:1]), a, total, total_shape)
    late = late[1:] + last
    total = product(order, [(*what, refs[:1], 0) for *what, refs, _ in late], a, total, total_shape)
    out = jax.ShapeDtypeStruct(a_vals.shape, a_vals.dtype)
    return product(order, [(*what, refs, 1) for *what, refs, _ in late], a, total, out, cols)


def ring_order(mesh):
    count = mesh.shape["row"]
    coords = [getattr(d, "coords", None) for d in mesh.devices[0, :, 0]]
    loop = [*range(0, count, 2), *range(count - 1 - count % 2, 0, -2)]
    if None not in coords:
        steps = [
            sum(abs(x - y) for x, y in zip(coords[loop[k - 1]], coords[loop[k]]))
            for k in range(count)
        ]
        if max(steps) <= 1:
            return loop
    return list(range(count))


def solution(mesh):
    return jax.shard_map(
        functools.partial(local, ring_order(mesh)),
        mesh=mesh,
        in_specs=(
            P(("groups", "row"), "col", None, None),
            P(("groups", "row"), "col", None, None),
            P(("groups", "row"), "col"),
        ),
        out_specs=P(("groups", "row"), "col", None, None),
        check_vma=False,
    )
```

```python
import functools
import math

import jax
import jax.numpy as jnp
from jax import lax
from jax.experimental import pallas as pl
from jax.experimental.pallas import tpu as pltpu
from jax.sharding import PartitionSpec as P

VMEM = pltpu.VMEM
SMEM = pltpu.SMEM
LIMIT = 48 * 1024 * 1024
STRIDE = 5
FOOT = 16


def params():
    return pltpu.CompilerParams(vmem_limit_bytes=LIMIT)


def within(col, half):
    return jnp.where(col >= half, col - half, col)


def cost(flops, size):
    return pl.CostEstimate(flops=flops, bytes_accessed=size, transcendentals=0)


def pack_kernel(half, cols_hbm, b_hbm, *refs):
    *o_refs, cols_ref, b_ref, sem, sems = refs
    rows, slots, bs, _ = b_ref.shape
    pairs = [pl.ds(2 * p, 2) for p in range(rows // 2)]
    copies = [pltpu.make_async_copy(b_hbm.at[pair], b_ref.at[pair], sems.at[p]) for p, pair in enumerate(pairs)]
    fetch = pltpu.make_async_copy(cols_hbm, cols_ref, sem)
    fetch.start()
    for copy in copies:
        copy.start()
    row = lax.broadcasted_iota(jnp.int32, (FOOT, 2 * bs), 0)
    lane = lax.broadcasted_iota(jnp.int32, (FOOT, 2 * bs), 1)
    fetch.wait()
    foot = jnp.full((FOOT, 2 * bs), slots, jnp.int32)
    for r in range(rows):
        for n in range(slots):
            here = (row == r) & (lane == within(cols_ref[r, n], half))
            foot = jnp.where(here, n, foot)
    o_refs[0][slots * bs :, :] = foot.astype(jnp.float32).astype(b_ref.dtype)
    for p, o_ref in enumerate(o_refs):
        copies[p].wait()
        for n in range(slots):
            o_ref[n * bs : (n + 1) * bs, :] = jnp.concatenate([b_ref[2 * p, n], b_ref[2 * p + 1, n]], axis=-1)


def pack(half, cols, b_vals):
    rows, slots, bs, _ = b_vals.shape
    shapes = [(slots * bs + (FOOT if p == 0 else 0), 2 * bs) for p in range(rows // 2)]
    cols, b_vals = (pltpu.with_memory_space_constraint(x, pltpu.HBM) for x in (cols, b_vals))
    return pl.pallas_call(
        functools.partial(pack_kernel, half),
        out_shape=[jax.ShapeDtypeStruct(shape, b_vals.dtype) for shape in shapes],
        in_specs=[pl.BlockSpec(memory_space=pl.ANY)] * 2,
        out_specs=[pl.BlockSpec(memory_space=VMEM)] * len(shapes),
        scratch_shapes=[
            SMEM(cols.shape, cols.dtype),
            VMEM(b_vals.shape, b_vals.dtype),
            pltpu.SemaphoreType.DMA,
            pltpu.SemaphoreType.DMA((rows // 2,)),
        ],
        compiler_params=params(),
        cost_estimate=cost(0, 2 * b_vals.size * 2),
    )(cols, b_vals)


def dense_kernel(cols_ref, others_ref, own_ref, other_ref, o_ref, blocks, where):
    rows, slots, bs, _ = own_ref.shape
    sources, pairs = o_ref.shape[:2]
    blocks[:, :slots] = own_ref[...]
    blocks[:, slots : 2 * slots] = other_ref[...]
    blocks[:, 2 * slots] = jnp.zeros_like(blocks[:, 2 * slots])
    for i in range(rows):
        def clear(j, carry):
            where[i, j] = 2 * slots
            return carry

        lax.fori_loop(0, 2 * sources * pairs, clear, 0, unroll=8)
        for m in range(slots):
            where[i, cols_ref[i, m]] = m
            where[i, others_ref[i, m]] = slots + m

    def body(s, carry):
        for p in range(pairs):
            j = (s * pairs + p) * 2
            for i in range(rows):
                left = blocks[i, where[i, j]]
                right = blocks[i, where[i, j + 1]]
                o_ref[s, p, i * bs : (i + 1) * bs, :] = jnp.concatenate([left, right], axis=-1)
        return carry

    lax.fori_loop(0, sources, body, 0, unroll=2)


def dense_rows(sources, cols, others, own, other):
    rows, slots, bs, _ = own.shape
    return pl.pallas_call(
        dense_kernel,
        out_shape=jax.ShapeDtypeStruct((sources, rows // 2, rows * bs, 2 * bs), own.dtype),
        grid_spec=pltpu.PrefetchScalarGridSpec(
            num_scalar_prefetch=2,
            grid=(),
            in_specs=[pl.BlockSpec(memory_space=VMEM)] * 2,
            out_specs=pl.BlockSpec(memory_space=VMEM),
            scratch_shapes=[
                VMEM((rows, 2 * slots + 1, bs, bs), own.dtype),
                SMEM((rows, sources * rows), jnp.int32),
            ],
        ),
        compiler_params=params(),
        cost_estimate=cost(0, 8 * own.size),
    )(cols, others, own, other)


def look_up(table, k):
    value = jnp.int32(table[0])
    for n, entry in enumerate(table[1:], 1):
        value = jnp.where(k == n, entry, value)
    return value


def arrived_from(order, way, steps):
    spots = [order.index(r) for r in range(len(order))]
    ahead = jnp.where(lax.axis_index("col") == 1, way, -way) * steps
    return look_up(order, lax.rem(look_up(spots, lax.axis_index("row")) - ahead + len(order), len(order)))


def add_products(a_ref, sources, refs, total, first, feet, where, sem):
    groups, bs = total.shape[0], total.shape[3] // 2
    parts, panels, refs = [], [], list(refs)
    for k, (place, start, stop) in enumerate(sources):
        mine, refs, place = refs[:stop], refs[stop:], place()
        slots = (mine[0].shape[0] - FOOT) // bs
        feet[k] = mine[0][slots * bs :, :].astype(jnp.float32).astype(jnp.int32)
        parts += [(mine[p], k, 2 * p) for p in range(start, stop)]
        panels += [a_ref[place, p] for p in range(start, stop)]
    copy = pltpu.make_async_copy(feet, where, sem)
    copy.start()
    copy.wait()
    low = lax.broadcasted_iota(jnp.int32, (bs, 2 * bs), 1) < bs
    left_side = jnp.concatenate(panels, axis=-1)

    def block(part, slot):
        at = pl.multiple_of(jnp.minimum(slot, slots - 1) * bs, bs)
        return jnp.where(slot < slots, part[pl.ds(at, bs), :], jnp.zeros((bs, 2 * bs), part.dtype))

    def body(g, carry):
        rows = []
        for part, k, r in parts:
            for h in range(2):
                tiles = []
                for q in (2 * g, 2 * g + 1):
                    left = block(part, where[k, r + h, 2 * q])
                    right = block(part, where[k, r + h, 2 * q + 1])
                    if h == 0:
                        right = pltpu.roll(right, bs, 1)
                    else:
                        left = pltpu.roll(left, bs, 1)
                    tiles.append(jnp.where(low, left, right))
                rows.append(jnp.concatenate(tiles, axis=-1))
        sums = jnp.dot(left_side, jnp.concatenate(rows, axis=0), preferred_element_type=jnp.float32)
        for t in range(2):
            piece = sums[:, t * 2 * bs : (t + 1) * 2 * bs]
            if first:
                total[g, t] = piece
            else:
                total[g, t] += piece
        return carry

    lax.fori_loop(0, groups, body, 0, unroll=min(groups, 4))


def first_kernel(sources, a_ref, *refs):
    *parts, total, feet, where, sem = refs
    add_products(a_ref, sources, parts, total, True, feet, where, sem)


def middle_kernel(sources, a_ref, before, *refs):
    *parts, total, feet, where, sem = refs
    add_products(a_ref, sources, parts, total, False, feet, where, sem)


def last_kernel(sources, a_ref, total, cols_hbm, *refs):
    *parts, o_hbm, feet, where, sem, cols_ref, o_ref, cols_sem, sems = refs
    fetch = pltpu.make_async_copy(cols_hbm, cols_ref, cols_sem)
    fetch.start()
    add_products(a_ref, sources, parts, total, False, feet, where, sem)
    fetch.wait()
    rows, slots, bs, _ = o_ref.shape
    half = total.shape[0] * 4
    copies = []
    for i in range(rows):
        for k in range(slots):
            l = within(cols_ref[i, k], half)
            tile = total[l >> 2, (l >> 1) & 1, i * bs : (i + 1) * bs, :].astype(o_ref.dtype)
            tile = jnp.where(l & 1 == 0, tile, pltpu.roll(tile, bs, 1))
            o_ref[i, k] = tile[:, :bs]
            if k % STRIDE == STRIDE - 1 or k == slots - 1:
                some = pl.ds(k // STRIDE * STRIDE, k % STRIDE + 1)
                copies.append(pltpu.make_async_copy(o_ref.at[i, some], o_hbm.at[i, some], sems.at[i, k // STRIDE]))
                copies[-1].start()
    for copy in copies:
        copy.wait()


def product(order, arrived, a, total, out, cols=None):
    hbm, vmem = pl.BlockSpec(memory_space=pl.ANY), pl.BlockSpec(memory_space=VMEM)
    kernel = first_kernel if total is None else middle_kernel if cols is None else last_kernel
    sources = [
        (functools.partial(arrived_from, order, way, steps), start, len(refs)) for way, steps, refs, start in arrived
    ]
    parts = [ref for _, _, refs, _ in arrived for ref in refs]
    feet = (len(arrived), FOOT, parts[0].shape[1])
    scratch = [VMEM(feet, jnp.int32), SMEM(feet, jnp.int32), pltpu.SemaphoreType.DMA]
    arrays, specs = [a], [vmem]
    if total is not None:
        arrays, specs = arrays + [total], specs + [vmem]
    if cols is not None:
        arrays, specs = arrays + [cols], specs + [hbm]
        scratch += [
            SMEM(cols.shape, cols.dtype),
            VMEM(out.shape, out.dtype),
            pltpu.SemaphoreType.DMA,
            pltpu.SemaphoreType.DMA((out.shape[0], -(-out.shape[1] // STRIDE))),
        ]
    return pl.pallas_call(
        functools.partial(kernel, sources),
        out_shape=out,
        in_specs=specs + [vmem] * len(parts),
        out_specs=vmem if cols is None else hbm,
        scratch_shapes=scratch,
        input_output_aliases={1: 0} if total is not None and cols is None else {},
        compiler_params=params(),
        cost_estimate=cost(2 * len(arrived) * a.shape[2] * math.prod(out.shape), 0),
    )(*arrays, *parts)


def local(order, a_vals, b_vals, cols):
    sources = len(order)
    rows, slots, bs, _ = a_vals.shape
    half = sources * rows // 2
    hops = {1: sources // 2, -1: (sources - 1) // 2}

    def ring(way):
        return [
            (order[r] * 2 + c, order[(r + (way if c == 1 else -way)) % sources] * 2 + c)
            for r in range(sources)
            for c in range(2)
        ]

    parts = pack(half, cols, b_vals)
    _, *mine = lax.optimization_barrier((parts[0], a_vals, cols))
    swap = [(0, 1), (1, 0)]
    a_other, others = (lax.ppermute(x, "col", swap) for x in mine)
    a = dense_rows(sources, cols, others, a_vals, a_other)
    total_shape = jax.ShapeDtypeStruct((half // 4, 2, rows * bs, 2 * bs), jnp.float32)
    total = None
    held = {way: parts for way in hops}
    rounds = [[(1, 0, parts, 0)]]
    for step in range(1, hops[1] + 1):
        ways = [way for way in hops if step <= hops[way]]
        for way in ways:
            sent = list(held[way])
            if (step, way) == (1, -1):
                sent = [lax.optimization_barrier((part, others))[0] for part in sent]
            if (step, way) == (2, -1):
                sent[0], _ = lax.optimization_barrier((sent[0], a))
            if step > 3 and way == -1:
                total = product(order, rounds.pop(0), a, total, total_shape)
                sent[0], total = lax.optimization_barrier((sent[0], total))
            held[way] = [lax.ppermute(part, ("row", "col"), ring(way)) for part in sent]
        rounds.append([(way, step, held[way], 0) for way in ways])
    *_, late, last = rounds
    total = product(order, sum(rounds[:-2], late[:1]), a, total, total_shape)
    out = jax.ShapeDtypeStruct(a_vals.shape, a_vals.dtype)
    return product(order, late[1:] + last, a, total, out, cols)


def ring_order(mesh):
    count = mesh.shape["row"]
    coords = [getattr(d, "coords", None) for d in mesh.devices[0, :, 0]]
    loop = [*range(0, count, 2), *range(count - 1 - count % 2, 0, -2)]
    if None not in coords:
        steps = [
            sum(abs(x - y) for x, y in zip(coords[loop[k - 1]], coords[loop[k]]))
            for k in range(count)
        ]
        if max(steps) <= 1:
            return loop
    return list(range(count))


def solution(mesh):
    return jax.shard_map(
        functools.partial(local, ring_order(mesh)),
        mesh=mesh,
        in_specs=(
            P(("groups", "row"), "col", None, None),
            P(("groups", "row"), "col", None, None),
            P(("groups", "row"), "col"),
        ),
        out_specs=P(("groups", "row"), "col", None, None),
        check_vma=False,
    )
```

```python
import functools
import math

import jax
import jax.numpy as jnp
from jax import lax
from jax.experimental import pallas as pl
from jax.experimental.pallas import tpu as pltpu
from jax.sharding import PartitionSpec as P

VMEM = pltpu.VMEM
SMEM = pltpu.SMEM
LIMIT = 48 * 1024 * 1024
STRIDE = 5
FOOT = 16


def params():
    return pltpu.CompilerParams(vmem_limit_bytes=LIMIT)


def within(col, half):
    return jnp.where(col >= half, col - half, col)


def cost(flops, size):
    return pl.CostEstimate(flops=flops, bytes_accessed=size, transcendentals=0)


def pack_kernel(half, cols_hbm, b_hbm, *refs):
    *o_refs, cols_ref, b_ref, sem, sems = refs
    rows, slots, bs, _ = b_ref.shape
    pairs = [pl.ds(2 * p, 2) for p in range(rows // 2)]
    copies = [pltpu.make_async_copy(b_hbm.at[pair], b_ref.at[pair], sems.at[p]) for p, pair in enumerate(pairs)]
    fetch = pltpu.make_async_copy(cols_hbm, cols_ref, sem)
    fetch.start()
    for copy in copies:
        copy.start()
    row = lax.broadcasted_iota(jnp.int32, (FOOT, 2 * bs), 0)
    lane = lax.broadcasted_iota(jnp.int32, (FOOT, 2 * bs), 1)
    fetch.wait()
    foot = jnp.full((FOOT, 2 * bs), slots, jnp.int32)
    for r in range(rows):
        for n in range(slots):
            here = (row == r) & (lane == within(cols_ref[r, n], half))
            foot = jnp.where(here, n, foot)
    o_refs[0][slots * bs :, :] = foot.astype(jnp.float32).astype(b_ref.dtype)
    for p, o_ref in enumerate(o_refs):
        copies[p].wait()
        for n in range(slots):
            o_ref[n * bs : (n + 1) * bs, :] = jnp.concatenate([b_ref[2 * p, n], b_ref[2 * p + 1, n]], axis=-1)


def pack(half, cols, b_vals):
    rows, slots, bs, _ = b_vals.shape
    shapes = [(slots * bs + (FOOT if p == 0 else 0), 2 * bs) for p in range(rows // 2)]
    cols, b_vals = (pltpu.with_memory_space_constraint(x, pltpu.HBM) for x in (cols, b_vals))
    return pl.pallas_call(
        functools.partial(pack_kernel, half),
        out_shape=[jax.ShapeDtypeStruct(shape, b_vals.dtype) for shape in shapes],
        in_specs=[pl.BlockSpec(memory_space=pl.ANY)] * 2,
        out_specs=[pl.BlockSpec(memory_space=VMEM)] * len(shapes),
        scratch_shapes=[
            SMEM(cols.shape, cols.dtype),
            VMEM(b_vals.shape, b_vals.dtype),
            pltpu.SemaphoreType.DMA,
            pltpu.SemaphoreType.DMA((rows // 2,)),
        ],
        compiler_params=params(),
        cost_estimate=cost(0, 2 * b_vals.size * 2),
    )(cols, b_vals)


def dense_kernel(cols_ref, others_ref, own_ref, other_ref, o_ref, blocks, where):
    rows, slots, bs, _ = own_ref.shape
    sources, pairs = o_ref.shape[:2]
    blocks[:, :slots] = own_ref[...]
    blocks[:, slots : 2 * slots] = other_ref[...]
    blocks[:, 2 * slots] = jnp.zeros_like(blocks[:, 2 * slots])
    for i in range(rows):
        def clear(j, carry):
            where[i, j] = 2 * slots
            return carry

        lax.fori_loop(0, 2 * sources * pairs, clear, 0, unroll=8)
        for m in range(slots):
            where[i, cols_ref[i, m]] = m
            where[i, others_ref[i, m]] = slots + m

    def body(s, carry):
        for p in range(pairs):
            j = (s * pairs + p) * 2
            for i in range(rows):
                left = blocks[i, where[i, j]]
                right = blocks[i, where[i, j + 1]]
                o_ref[s, p, i * bs : (i + 1) * bs, :] = jnp.concatenate([left, right], axis=-1)
        return carry

    lax.fori_loop(0, sources, body, 0, unroll=2)


def dense_rows(sources, cols, others, own, other):
    rows, slots, bs, _ = own.shape
    return pl.pallas_call(
        dense_kernel,
        out_shape=jax.ShapeDtypeStruct((sources, rows // 2, rows * bs, 2 * bs), own.dtype),
        grid_spec=pltpu.PrefetchScalarGridSpec(
            num_scalar_prefetch=2,
            grid=(),
            in_specs=[pl.BlockSpec(memory_space=VMEM)] * 2,
            out_specs=pl.BlockSpec(memory_space=VMEM),
            scratch_shapes=[
                VMEM((rows, 2 * slots + 1, bs, bs), own.dtype),
                SMEM((rows, sources * rows), jnp.int32),
            ],
        ),
        compiler_params=params(),
        cost_estimate=cost(0, 8 * own.size),
    )(cols, others, own, other)


def look_up(table, k):
    value = jnp.int32(table[0])
    for n, entry in enumerate(table[1:], 1):
        value = jnp.where(k == n, entry, value)
    return value


def arrived_from(order, way, steps):
    spots = [order.index(r) for r in range(len(order))]
    ahead = jnp.where(lax.axis_index("col") == 1, way, -way) * steps
    return look_up(order, lax.rem(look_up(spots, lax.axis_index("row")) - ahead + len(order), len(order)))


def add_products(a_ref, sources, refs, total, first, feet, where, sem):
    groups, bs = total.shape[0], total.shape[3] // 2
    parts, panels, refs = [], [], list(refs)
    for k, (place, start, stop) in enumerate(sources):
        mine, refs, place = refs[:stop], refs[stop:], place()
        slots = (mine[0].shape[0] - FOOT) // bs
        feet[k] = mine[0][slots * bs :, :].astype(jnp.float32).astype(jnp.int32)
        parts += [(mine[p], k, 2 * p) for p in range(start, stop)]
        panels += [a_ref[place, p] for p in range(start, stop)]
    copy = pltpu.make_async_copy(feet, where, sem)
    copy.start()
    copy.wait()
    low = lax.broadcasted_iota(jnp.int32, (bs, 2 * bs), 1) < bs
    left_side = jnp.concatenate(panels, axis=-1)

    def block(part, slot):
        at = pl.multiple_of(jnp.minimum(slot, slots - 1) * bs, bs)
        return jnp.where(slot < slots, part[pl.ds(at, bs), :], jnp.zeros((bs, 2 * bs), part.dtype))

    def body(g, carry):
        rows = []
        for part, k, r in parts:
            for h in range(2):
                tiles = []
                for q in (2 * g, 2 * g + 1):
                    left = block(part, where[k, r + h, 2 * q])
                    right = block(part, where[k, r + h, 2 * q + 1])
                    if h == 0:
                        right = pltpu.roll(right, bs, 1)
                    else:
                        left = pltpu.roll(left, bs, 1)
                    tiles.append(jnp.where(low, left, right))
                rows.append(jnp.concatenate(tiles, axis=-1))
        sums = jnp.dot(left_side, jnp.concatenate(rows, axis=0), preferred_element_type=jnp.float32)
        for t in range(2):
            piece = sums[:, t * 2 * bs : (t + 1) * 2 * bs]
            if first:
                total[g, t] = piece
            else:
                total[g, t] += piece
        return carry

    lax.fori_loop(0, groups, body, 0, unroll=min(groups, 4))


def first_kernel(sources, a_ref, *refs):
    *parts, total, feet, where, sem = refs
    add_products(a_ref, sources, parts, total, True, feet, where, sem)


def middle_kernel(sources, a_ref, before, *refs):
    *parts, total, feet, where, sem = refs
    add_products(a_ref, sources, parts, total, False, feet, where, sem)


def last_kernel(sources, a_ref, total, cols_hbm, *refs):
    *parts, o_hbm, feet, where, sem, cols_ref, o_ref, cols_sem, sems = refs
    fetch = pltpu.make_async_copy(cols_hbm, cols_ref, cols_sem)
    fetch.start()
    add_products(a_ref, sources, parts, total, False, feet, where, sem)
    fetch.wait()
    rows, slots, bs, _ = o_ref.shape
    half = total.shape[0] * 4
    copies = []
    for i in range(rows):
        for k in range(slots):
            l = within(cols_ref[i, k], half)
            tile = total[l >> 2, (l >> 1) & 1, i * bs : (i + 1) * bs, :].astype(o_ref.dtype)
            tile = jnp.where(l & 1 == 0, tile, pltpu.roll(tile, bs, 1))
            o_ref[i, k] = tile[:, :bs]
            if k % STRIDE == STRIDE - 1 or k == slots - 1:
                some = pl.ds(k // STRIDE * STRIDE, k % STRIDE + 1)
                copies.append(pltpu.make_async_copy(o_ref.at[i, some], o_hbm.at[i, some], sems.at[i, k // STRIDE]))
                copies[-1].start()
    for copy in copies:
        copy.wait()


def product(order, arrived, a, total, out, cols=None):
    hbm, vmem = pl.BlockSpec(memory_space=pl.ANY), pl.BlockSpec(memory_space=VMEM)
    kernel = first_kernel if total is None else middle_kernel if cols is None else last_kernel
    sources = [
        (functools.partial(arrived_from, order, way, steps), start, len(refs)) for way, steps, refs, start in arrived
    ]
    parts = [ref for _, _, refs, _ in arrived for ref in refs]
    feet = (len(arrived), FOOT, parts[0].shape[1])
    scratch = [VMEM(feet, jnp.int32), SMEM(feet, jnp.int32), pltpu.SemaphoreType.DMA]
    arrays, specs = [a], [vmem]
    if total is not None:
        arrays, specs = arrays + [total], specs + [vmem]
    if cols is not None:
        arrays, specs = arrays + [cols], specs + [hbm]
        scratch += [
            SMEM(cols.shape, cols.dtype),
            VMEM(out.shape, out.dtype),
            pltpu.SemaphoreType.DMA,
            pltpu.SemaphoreType.DMA((out.shape[0], -(-out.shape[1] // STRIDE))),
        ]
    return pl.pallas_call(
        functools.partial(kernel, sources),
        out_shape=out,
        in_specs=specs + [vmem] * len(parts),
        out_specs=vmem if cols is None else hbm,
        scratch_shapes=scratch,
        input_output_aliases={1: 0} if total is not None and cols is None else {},
        compiler_params=params(),
        cost_estimate=cost(2 * len(arrived) * a.shape[2] * math.prod(out.shape), 0),
    )(*arrays, *parts)


def local(order, a_vals, b_vals, cols):
    sources = len(order)
    rows, slots, bs, _ = a_vals.shape
    half = sources * rows // 2
    hops = {1: sources // 2, -1: (sources - 1) // 2}

    def ring(way):
        return [
            (order[r] * 2 + c, order[(r + (way if c == 1 else -way)) % sources] * 2 + c)
            for r in range(sources)
            for c in range(2)
        ]

    parts = pack(half, cols, b_vals)
    _, *mine = lax.optimization_barrier((parts[0], a_vals, cols))
    swap = [(0, 1), (1, 0)]
    a_other, others = (lax.ppermute(x, "col", swap) for x in mine)
    a = dense_rows(sources, cols, others, a_vals, a_other)
    total_shape = jax.ShapeDtypeStruct((half // 4, 2, rows * bs, 2 * bs), jnp.float32)
    total = None
    held = {way: parts for way in hops}
    rounds = [[(1, 0, parts, 0)]]
    for step in range(1, hops[1] + 1):
        ways = [way for way in hops if step <= hops[way]]
        for way in ways:
            sent = list(held[way])
            if (step, way) == (1, -1):
                sent = [lax.optimization_barrier((part, others))[0] for part in sent]
            if (step, way) == (2, -1):
                sent[0], _ = lax.optimization_barrier((sent[0], a))
            if step > 3 and way == -1:
                total = product(order, rounds.pop(0), a, total, total_shape)
                sent[0], total = lax.optimization_barrier((sent[0], total))
            held[way] = [lax.ppermute(part, ("row", "col"), ring(way)) for part in sent]
        rounds.append([(way, step, held[way], 0) for way in ways])
    *_, late, last = rounds
    total = product(order, rounds[0] + rounds[1], a, total, total_shape)
    early, late = sum(rounds[2:-2], late[:1]), late[1:] + last
    early += [(*what, refs[:1], 0) for *what, refs, _ in late]
    total = product(order, early, a, total, total_shape)
    out = jax.ShapeDtypeStruct(a_vals.shape, a_vals.dtype)
    return product(order, [(*what, refs, 1) for *what, refs, _ in late], a, total, out, cols)


def ring_order(mesh):
    count = mesh.shape["row"]
    coords = [getattr(d, "coords", None) for d in mesh.devices[0, :, 0]]
    loop = [*range(0, count, 2), *range(count - 1 - count % 2, 0, -2)]
    if None not in coords:
        steps = [
            sum(abs(x - y) for x, y in zip(coords[loop[k - 1]], coords[loop[k]]))
            for k in range(count)
        ]
        if max(steps) <= 1:
            return loop
    return list(range(count))


def solution(mesh):
    return jax.shard_map(
        functools.partial(local, ring_order(mesh)),
        mesh=mesh,
        in_specs=(
            P(("groups", "row"), "col", None, None),
            P(("groups", "row"), "col", None, None),
            P(("groups", "row"), "col"),
        ),
        out_specs=P(("groups", "row"), "col", None, None),
        check_vma=False,
    )
```

```python
import functools
import math

import jax
import jax.numpy as jnp
from jax import lax
from jax.experimental import pallas as pl
from jax.experimental.pallas import tpu as pltpu
from jax.sharding import PartitionSpec as P

VMEM = pltpu.VMEM
SMEM = pltpu.SMEM
LIMIT = 48 * 1024 * 1024
STRIDE = 10
FOOT = 16


def params():
    return pltpu.CompilerParams(vmem_limit_bytes=LIMIT)


def within(col, half):
    return jnp.where(col >= half, col - half, col)


def cost(flops, size):
    return pl.CostEstimate(flops=flops, bytes_accessed=size, transcendentals=0)


def pack_kernel(half, cols_hbm, b_hbm, *refs):
    *o_refs, cols_ref, b_ref, sem, sems = refs
    rows, slots, bs, _ = b_ref.shape
    pairs = [pl.ds(2 * p, 2) for p in range(rows // 2)]
    copies = [pltpu.make_async_copy(b_hbm.at[pair], b_ref.at[pair], sems.at[p]) for p, pair in enumerate(pairs)]
    fetch = pltpu.make_async_copy(cols_hbm, cols_ref, sem)
    fetch.start()
    for copy in copies:
        copy.start()
    row = lax.broadcasted_iota(jnp.int32, (FOOT, 2 * bs), 0)
    lane = lax.broadcasted_iota(jnp.int32, (FOOT, 2 * bs), 1)
    fetch.wait()
    foot = jnp.full((FOOT, 2 * bs), slots, jnp.int32)
    for r in range(rows):
        for n in range(slots):
            here = (row == r) & (lane == within(cols_ref[r, n], half))
            foot = jnp.where(here, n, foot)
    o_refs[0][slots * bs :, :] = foot.astype(jnp.float32).astype(b_ref.dtype)
    for p, o_ref in enumerate(o_refs):
        copies[p].wait()
        for n in range(slots):
            o_ref[n * bs : (n + 1) * bs, :] = jnp.concatenate([b_ref[2 * p, n], b_ref[2 * p + 1, n]], axis=-1)


def pack(half, cols, b_vals):
    rows, slots, bs, _ = b_vals.shape
    shapes = [(slots * bs + (FOOT if p == 0 else 0), 2 * bs) for p in range(rows // 2)]
    cols, b_vals = (pltpu.with_memory_space_constraint(x, pltpu.HBM) for x in (cols, b_vals))
    return pl.pallas_call(
        functools.partial(pack_kernel, half),
        out_shape=[jax.ShapeDtypeStruct(shape, b_vals.dtype) for shape in shapes],
        in_specs=[pl.BlockSpec(memory_space=pl.ANY)] * 2,
        out_specs=[pl.BlockSpec(memory_space=VMEM)] * len(shapes),
        scratch_shapes=[
            SMEM(cols.shape, cols.dtype),
            VMEM(b_vals.shape, b_vals.dtype),
            pltpu.SemaphoreType.DMA,
            pltpu.SemaphoreType.DMA((rows // 2,)),
        ],
        compiler_params=params(),
        cost_estimate=cost(0, 2 * b_vals.size * 2),
    )(cols, b_vals)


def dense_kernel(cols_ref, others_ref, own_ref, other_ref, o_ref, blocks, where):
    rows, slots, bs, _ = own_ref.shape
    sources, pairs = o_ref.shape[:2]
    blocks[:, :slots] = own_ref[...]
    blocks[:, slots : 2 * slots] = other_ref[...]
    blocks[:, 2 * slots] = jnp.zeros_like(blocks[:, 2 * slots])
    for i in range(rows):
        def clear(j, carry):
            where[i, j] = 2 * slots
            return carry

        lax.fori_loop(0, 2 * sources * pairs, clear, 0, unroll=8)
        for m in range(slots):
            where[i, cols_ref[i, m]] = m
            where[i, others_ref[i, m]] = slots + m

    def body(s, carry):
        for p in range(pairs):
            j = (s * pairs + p) * 2
            for i in range(rows):
                left = blocks[i, where[i, j]]
                right = blocks[i, where[i, j + 1]]
                o_ref[s, p, i * bs : (i + 1) * bs, :] = jnp.concatenate([left, right], axis=-1)
        return carry

    lax.fori_loop(0, sources, body, 0, unroll=2)


def dense_rows(sources, cols, others, own, other):
    rows, slots, bs, _ = own.shape
    return pl.pallas_call(
        dense_kernel,
        out_shape=jax.ShapeDtypeStruct((sources, rows // 2, rows * bs, 2 * bs), own.dtype),
        grid_spec=pltpu.PrefetchScalarGridSpec(
            num_scalar_prefetch=2,
            grid=(),
            in_specs=[pl.BlockSpec(memory_space=VMEM)] * 2,
            out_specs=pl.BlockSpec(memory_space=VMEM),
            scratch_shapes=[
                VMEM((rows, 2 * slots + 1, bs, bs), own.dtype),
                SMEM((rows, sources * rows), jnp.int32),
            ],
        ),
        compiler_params=params(),
        cost_estimate=cost(0, 8 * own.size),
    )(cols, others, own, other)


def look_up(table, k):
    value = jnp.int32(table[0])
    for n, entry in enumerate(table[1:], 1):
        value = jnp.where(k == n, entry, value)
    return value


def arrived_from(order, way, steps):
    spots = [order.index(r) for r in range(len(order))]
    ahead = jnp.where(lax.axis_index("col") == 1, way, -way) * steps
    return look_up(order, lax.rem(look_up(spots, lax.axis_index("row")) - ahead + len(order), len(order)))


def add_products(a_ref, sources, refs, total, first, feet, where, sem):
    groups, bs = total.shape[0], total.shape[3] // 2
    parts, panels, refs = [], [], list(refs)
    for k, (place, start, stop) in enumerate(sources):
        mine, refs, place = refs[:stop], refs[stop:], place()
        slots = (mine[0].shape[0] - FOOT) // bs
        feet[k] = mine[0][slots * bs :, :].astype(jnp.float32).astype(jnp.int32)
        parts += [(mine[p], k, 2 * p) for p in range(start, stop)]
        panels += [a_ref[place, p] for p in range(start, stop)]
    copy = pltpu.make_async_copy(feet, where, sem)
    copy.start()
    copy.wait()
    low = lax.broadcasted_iota(jnp.int32, (bs, 2 * bs), 1) < bs
    left_side = jnp.concatenate(panels, axis=-1)

    def block(part, slot):
        at = pl.multiple_of(jnp.minimum(slot, slots - 1) * bs, bs)
        return jnp.where(slot < slots, part[pl.ds(at, bs), :], jnp.zeros((bs, 2 * bs), part.dtype))

    def body(g, carry):
        rows = []
        for part, k, r in parts:
            for h in range(2):
                tiles = []
                for q in (2 * g, 2 * g + 1):
                    left = block(part, where[k, r + h, 2 * q])
                    right = block(part, where[k, r + h, 2 * q + 1])
                    if h == 0:
                        right = pltpu.roll(right, bs, 1)
                    else:
                        left = pltpu.roll(left, bs, 1)
                    tiles.append(jnp.where(low, left, right))
                rows.append(jnp.concatenate(tiles, axis=-1))
        sums = jnp.dot(left_side, jnp.concatenate(rows, axis=0), preferred_element_type=jnp.float32)
        for t in range(2):
            piece = sums[:, t * 2 * bs : (t + 1) * 2 * bs]
            if first:
                total[g, t] = piece
            else:
                total[g, t] += piece
        return carry

    lax.fori_loop(0, groups, body, 0, unroll=min(groups, 4))


def first_kernel(sources, a_ref, *refs):
    *parts, total, feet, where, sem = refs
    add_products(a_ref, sources, parts, total, True, feet, where, sem)


def middle_kernel(sources, a_ref, before, *refs):
    *parts, total, feet, where, sem = refs
    add_products(a_ref, sources, parts, total, False, feet, where, sem)


def last_kernel(sources, a_ref, total, cols_hbm, *refs):
    *parts, o_hbm, feet, where, sem, cols_ref, o_ref, cols_sem, sems = refs
    fetch = pltpu.make_async_copy(cols_hbm, cols_ref, cols_sem)
    fetch.start()
    add_products(a_ref, sources, parts, total, False, feet, where, sem)
    fetch.wait()
    rows, slots, bs, _ = o_ref.shape
    half = total.shape[0] * 4
    copies = []
    for i in range(rows):
        for k in range(slots):
            l = within(cols_ref[i, k], half)
            tile = total[l >> 2, (l >> 1) & 1, i * bs : (i + 1) * bs, :].astype(o_ref.dtype)
            tile = jnp.where(l & 1 == 0, tile, pltpu.roll(tile, bs, 1))
            o_ref[i, k] = tile[:, :bs]
            if k % STRIDE == STRIDE - 1 or k == slots - 1:
                some = pl.ds(k // STRIDE * STRIDE, k % STRIDE + 1)
                copies.append(pltpu.make_async_copy(o_ref.at[i, some], o_hbm.at[i, some], sems.at[i, k // STRIDE]))
                copies[-1].start()
    for copy in copies:
        copy.wait()


def product(order, arrived, a, total, out, cols=None):
    hbm, vmem = pl.BlockSpec(memory_space=pl.ANY), pl.BlockSpec(memory_space=VMEM)
    kernel = first_kernel if total is None else middle_kernel if cols is None else last_kernel
    sources = [
        (functools.partial(arrived_from, order, way, steps), start, len(refs)) for way, steps, refs, start in arrived
    ]
    parts = [ref for _, _, refs, _ in arrived for ref in refs]
    feet = (len(arrived), FOOT, parts[0].shape[1])
    scratch = [VMEM(feet, jnp.int32), SMEM(feet, jnp.int32), pltpu.SemaphoreType.DMA]
    arrays, specs = [a], [vmem]
    if total is not None:
        arrays, specs = arrays + [total], specs + [vmem]
    if cols is not None:
        arrays, specs = arrays + [cols], specs + [hbm]
        scratch += [
            SMEM(cols.shape, cols.dtype),
            VMEM(out.shape, out.dtype),
            pltpu.SemaphoreType.DMA,
            pltpu.SemaphoreType.DMA((out.shape[0], -(-out.shape[1] // STRIDE))),
        ]
    return pl.pallas_call(
        functools.partial(kernel, sources),
        out_shape=out,
        in_specs=specs + [vmem] * len(parts),
        out_specs=vmem if cols is None else hbm,
        scratch_shapes=scratch,
        input_output_aliases={1: 0} if total is not None and cols is None else {},
        compiler_params=params(),
        cost_estimate=cost(2 * len(arrived) * a.shape[2] * math.prod(out.shape), 0),
    )(*arrays, *parts)


def local(order, a_vals, b_vals, cols):
    sources = len(order)
    rows, slots, bs, _ = a_vals.shape
    half = sources * rows // 2
    hops = {1: sources // 2, -1: (sources - 1) // 2}

    def ring(way):
        return [
            (order[r] * 2 + c, order[(r + (way if c == 1 else -way)) % sources] * 2 + c)
            for r in range(sources)
            for c in range(2)
        ]

    parts = pack(half, cols, b_vals)
    _, *mine = lax.optimization_barrier((parts[0], a_vals, cols))
    swap = [(0, 1), (1, 0)]
    a_other, others = (lax.ppermute(x, "col", swap) for x in mine)
    a = dense_rows(sources, cols, others, a_vals, a_other)
    total_shape = jax.ShapeDtypeStruct((half // 4, 2, rows * bs, 2 * bs), jnp.float32)
    total = None
    held = {way: parts for way in hops}
    rounds = [[(1, 0, parts, 0)]]
    for step in range(1, hops[1] + 1):
        ways = [way for way in hops if step <= hops[way]]
        for way in ways:
            sent = list(held[way])
            if (step, way) == (1, -1):
                sent = [lax.optimization_barrier((part, others))[0] for part in sent]
            if (step, way) == (2, -1):
                sent[0], _ = lax.optimization_barrier((sent[0], a))
            if step > 2 and way == -1:
                total = product(order, rounds.pop(0), a, total, total_shape)
                sent[0], total = lax.optimization_barrier((sent[0], total))
            held[way] = [lax.ppermute(part, ("row", "col"), ring(way)) for part in sent]
        rounds.append([(way, step, held[way], 0) for way in ways])
    *_, late, last = rounds
    total = product(order, sum(rounds[:-2], late[:1]), a, total, total_shape)
    late = late[1:] + last
    total = product(order, [(*what, refs[:1], 0) for *what, refs, _ in late], a, total, total_shape)
    out = jax.ShapeDtypeStruct(a_vals.shape, a_vals.dtype)
    return product(order, [(*what, refs, 1) for *what, refs, _ in late], a, total, out, cols)


def ring_order(mesh):
    count = mesh.shape["row"]
    coords = [getattr(d, "coords", None) for d in mesh.devices[0, :, 0]]
    loop = [*range(0, count, 2), *range(count - 1 - count % 2, 0, -2)]
    if None not in coords:
        steps = [
            sum(abs(x - y) for x, y in zip(coords[loop[k - 1]], coords[loop[k]]))
            for k in range(count)
        ]
        if max(steps) <= 1:
            return loop
    return list(range(count))


def solution(mesh):
    return jax.shard_map(
        functools.partial(local, ring_order(mesh)),
        mesh=mesh,
        in_specs=(
            P(("groups", "row"), "col", None, None),
            P(("groups", "row"), "col", None, None),
            P(("groups", "row"), "col"),
        ),
        out_specs=P(("groups", "row"), "col", None, None),
        check_vma=False,
    )
```
